128 devices in a mesh: skyx: 16 (over x, z), skyy: 8 (over y, core).
Axes of the slice: x: 4, y: 4, z: 4, core: 2. Of those that a mesh axis runs over, the one named last changes fastest.
Arguments:
- patches: float32 [8, 256, 128, 256], P('skyy', 'skyx'), may hold values from -8 to 8
- dest: int32 [8, 256, 1], P('skyy', 'skyx'), may hold values from 0 to 15; in each aligned block of 16 rows (0 to 15, 16 to 31, ..., all dimensions but the last counted through in order) at most 2 rows name the same one
- row_offset: int32 [8, 256], P('skyy', 'skyx'), may hold values from -128 to 512
- col_offset: int32 [8, 256], P('skyy', 'skyx'), may hold values from -128 to 384
- live_rows: int32 [8, 256], P('skyy', 'skyx'), may hold values from 32 to 128
- weight: float32 [8, 256], P('skyy', 'skyx'), may hold values from 0.2 to 2
- coefficient: float32 [8, 256, 8], P('skyy', 'skyx'), may hold values from -3 to 3
- basis: float32 [2, 8, 41], replicated, may hold values from -0.9 to 0.9
Outputs:
- coadd: float32 [4096, 8192], P('skyy', 'skyx')
- depth: float32 [4096, 8192], P('skyy', 'skyx')
The draws below stay inside these ranges and needn't reach their ends.
Inputs may be any that keep to these rules, and one draw needn't show every extreme that they name: `dest`: among the 16 patches of a band k = m * 16 to (m + 1) * 16 - 1, for each m, no tile column is named more than 2 times.
All inputs are finite; a program needn't handle non-finite values.
Results may differ from the reference program's by a relative error of at most 0.0003.
Values sent between devices are 32-bit elements; how exact they have to be, the bound alone decides.
No kernel may reach another device: no remote copies, remote signals or barrier semaphores. Data moves between devices by JAX's collectives and lax.ppermute only.
A program may use at most 192 MiB of HBM per device.

```python
import math
import jax
import jax.numpy as jnp
import numpy as np
from jax import lax

NB = 8
TAPS = 41
PH = 128
PW = 256
TILE = 512
MARGIN = 128
P_DEV = 16
CAP = 2
PBAND = 256
NROWS = 4096
NCOLS = 8192
N_SKYX = 16
N_SKYY = 8


def place_ends(result, stream_key, smallest, largest):
    index_at = [jax.random.randint(jax.random.fold_in(stream_key, axis), (), 0, length) for axis, length in enumerate(result.shape)]
    longest = result.shape.index(max(result.shape))
    next_to = index_at[:longest] + [(index_at[longest] + 1) % result.shape[longest]] + index_at[longest + 1:]
    return result.at[tuple(index_at)].set(smallest).at[tuple(next_to)].set(largest)


def steps_of(own_key, extent, shards, smallest, high):
    factor_of = 1.0
    for position, blocks in shards:
        steps = jax.random.uniform(jax.random.fold_in(jax.random.fold_in(own_key, 6), position), (blocks,), jnp.float32, smallest / len(shards), high / len(shards))
        factor_of = factor_of * jnp.repeat(jnp.exp(steps), extent[position] // blocks).reshape((-1,) + (1,) * (len(extent) - 1 - position))
    return factor_of


def deal_out(key, own, number, rows, count, top, bound, slope):
    order = jax.random.permutation(key, count)
    heavy_load, usual = shares(count, rows * top, bound, slope, True), shares(count, rows * top, bound, slope, False)
    places = jnp.arange(count)

    def named(sizes, turn):
        used = int((sizes > 0).sum())
        fixed = max(1, used // 4)
        moved = fixed + (places - fixed + turn * (used - fixed)) % max(1, count - fixed)
        return jnp.zeros((count,), jnp.int32).at[order[jnp.where(places < fixed, places, moved)]].set(jnp.asarray(sizes, jnp.int32))

    sizes = jnp.where(number % 4 == 0, named(heavy_load, number // 4), named(usual, number - number // 4 - 1))
    mixed = jax.random.permutation(jax.random.fold_in(own, 3), count)
    source_of, taker = mixed[0:count // 2 * 2:2], mixed[1:count // 2 * 2:2]
    room = jnp.minimum(sizes[source_of] - 1, bound - sizes[taker]) // 2
    room = jnp.where((source_of == order[0]) | (taker == order[0]) | (sizes[taker] == 0), 0, jnp.maximum(room, 0))
    moved = jax.random.randint(jax.random.fold_in(own, 4), (count // 2,), 0, 1 << 20) % (room + 1)
    sizes = sizes.at[source_of].add(-moved).at[taker].add(moved)
    labels = jnp.searchsorted(jnp.cumsum(sizes), jnp.arange(rows * top), side="right").astype(jnp.int32)
    table = labels.reshape(top, rows).T
    table = table[jax.random.permutation(jax.random.fold_in(own, 1), rows)]
    turn = jax.random.randint(jax.random.fold_in(own, 2), (rows, 1), 0, top)
    return jnp.take_along_axis(table, (jnp.arange(top)[None, :] + turn) % top, axis=1)


def shares(amount, total, bound, slope, full):
    loads = [(1 << 20) // math.isqrt(standing ** slope) + 1 for standing in range(1, amount + 1)]
    largest = bound if full else min(bound, max(-(-total // amount), total * loads[0] // sum(loads)))
    least = 1 if total - largest >= amount - 1 else 0
    given, surplus = [largest] + [least] * (amount - 1), total - largest - least * (amount - 1)
    while surplus > 0:
        candidates = [i for i in range(1, amount) if given[i] < largest] or [i for i in range(1, amount) if given[i] < bound]
        whole, remaining = sum([loads[i] for i in candidates]), surplus
        for i in candidates:
            addition = min(bound - given[i], max(1, remaining * loads[i] // whole), surplus)
            given[i] = given[i] + addition
            surplus = surplus - addition
    return np.array(given)


def bell_draw(stream_key, shape, scale, most, cuts=(), kind=jnp.bfloat16):
    entries = jax.random.normal(stream_key, shape, jnp.float32) * scale
    if len(cuts) > 0:
        entries = steps_of(stream_key, shape, cuts, -0.22, 0.18) * entries
    return jnp.clip(entries, min=-most, max=most).astype(kind)


def setup_inputs(seed: int = 0) -> dict:
    splits = jax.random.split(jax.random.key(seed), 9)
    patches = bell_draw(splits[0], (N_SKYY, PBAND, PH, PW), 1.0, 8.0, ((0, 8), (1, 16)), jnp.float32)
    dest_keys = jax.random.split(jax.random.fold_in(splits[1], 1), N_SKYY * PBAND // P_DEV)
    dest_turns = jax.random.permutation(jax.random.fold_in(splits[1], 3), N_SKYY * PBAND // P_DEV)
    dest = jax.vmap(lambda own, number: deal_out(jax.random.fold_in(splits[1], 2), own, number, P_DEV, N_SKYX, 1, CAP, 2))(dest_keys, dest_turns).reshape((N_SKYY, PBAND, 1))
    row_offset = place_ends(jax.random.randint(splits[2], (N_SKYY, PBAND), 0 - MARGIN, TILE + MARGIN - PH + 1), jax.random.fold_in(splits[2], 1), 0 - MARGIN, TILE + MARGIN - PH).astype(jnp.int32)
    col_offset = place_ends(jax.random.randint(splits[3], (N_SKYY, PBAND), 0 - MARGIN, TILE + MARGIN - PW + 1), jax.random.fold_in(splits[3], 1), 0 - MARGIN, TILE + MARGIN - PW).astype(jnp.int32)
    live_rows = place_ends(jax.random.randint(splits[4], (N_SKYY, PBAND), PH // 4, PH + 1), jax.random.fold_in(splits[4], 1), PH // 4, PH).astype(jnp.int32)
    weight = jnp.clip(jnp.exp(math.log(2.0) - 2.3025851 * jax.random.uniform(splits[5], (N_SKYY, PBAND), jnp.float32) ** steps_of(splits[5], (N_SKYY, PBAND), ((0, 8), (1, 16)), -0.2, 0.2)), 0.2, 2.0)
    coefficient = bell_draw(splits[6], (N_SKYY, PBAND, NB), 0.5, 3.0, ((0, 8), (1, 16)), jnp.float32)
    basis = bell_draw(splits[7], (2, NB, TAPS), 0.15, 0.9, (), jnp.float32)
    return {"patches": patches, "dest": dest, "row_offset": row_offset, "col_offset": col_offset, "live_rows": live_rows, "weight": weight, "coefficient": coefficient, "basis": basis}


prior_weight = 0.5


def reference(patches, dest, row_offset, col_offset, live_rows, weight, coefficient, basis):
    half_taps = TAPS // 2
    row_index = jnp.arange(PH, dtype=jnp.int32)
    fft_shape = (PH + TAPS - 1, PW + TAPS - 1)

    def one_band(band_args):
        images, coeffs, live_count, scales = band_args
        row_mask = (row_index[None, :] < live_count[:, None]).astype(jnp.float32)[:, :, None]
        masked = images * row_mask
        kernels = jnp.einsum("kb,bs,bt->kst", coeffs, basis[0], basis[1])
        spectrum = jnp.fft.rfft2(masked, fft_shape) * jnp.fft.rfft2(kernels, fft_shape)
        full_conv = jnp.fft.irfft2(spectrum, fft_shape)
        matched = full_conv[:, half_taps:half_taps + PH, half_taps:half_taps + PW]
        return matched * row_mask * scales[:, None, None]

    contribution = lax.map(one_band, (patches, coefficient, live_rows, weight))
    total = N_SKYY * PBAND
    flat_data = contribution.reshape(total, PH, PW)
    band_of = (jnp.arange(total, dtype=jnp.int32) // PBAND).astype(jnp.int32)
    canvas = jnp.zeros((2, NROWS + 2 * MARGIN, NCOLS + 2 * MARGIN), jnp.float32)

    def place(canvas, item):
        piece, band, column, top, left, live_count, scale = item
        plane = scale * (row_index < live_count).astype(jnp.float32)[:, None] * jnp.ones((1, PW), jnp.float32)
        stacked = jnp.stack([piece, plane])
        start_row = (band * TILE + top + MARGIN).astype(jnp.int32)
        start_col = (column * TILE + left + MARGIN).astype(jnp.int32)
        anchor = jnp.zeros((), jnp.int32)
        region = lax.dynamic_slice(canvas, (anchor, start_row, start_col), (2, PH, PW))
        return lax.dynamic_update_slice(canvas, region + stacked, (anchor, start_row, start_col)), None

    items = (flat_data, band_of, dest.reshape(total), row_offset.reshape(total), col_offset.reshape(total),
             live_rows.reshape(total), weight.reshape(total))
    canvas, unused = lax.scan(place, canvas, items)
    core = canvas[:, MARGIN:MARGIN + NROWS, MARGIN:MARGIN + NCOLS]
    depth = core[1]
    coadd = core[0] / (depth + prior_weight)
    return coadd, depth
```

```python
import jax
import jax.numpy as jnp
from jax import lax
from jax.experimental import pallas as pl
from jax.experimental.pallas import tpu as pltpu
from jax.sharding import PartitionSpec as P

TILE = 512
MARGIN = 128
CAP = 2
PH = 128
PW = 256
NB = 8
TAPS = 41
HALF = TAPS // 2
SIDE = TILE + 2 * MARGIN
CANVAS_ROWS = SIDE + 8
CANVAS_COLS = SIDE + 128
META = 8
VMEM_LIMIT = 48 * 1024 * 1024

prior_weight = 0.5
f32 = jnp.float32
bf16 = jnp.bfloat16
i32 = jnp.int32


def whole(shape):
    return pl.BlockSpec(shape, lambda *_: (0,) * len(shape))


smem = pl.BlockSpec(memory_space=pltpu.SMEM)
vmem = pl.BlockSpec(memory_space=pltpu.VMEM)
anywhere = pl.BlockSpec(memory_space=pl.ANY)


def split(x):
    high = x.astype(bf16)
    return high, (x - high.astype(f32)).astype(bf16)


def bands_kernel(basis, down_high, down_low, across_high, across_low):
    for b in range(NB):
        taps = jnp.broadcast_to(basis[1, b : b + 1, :], (PW, PW + 128))
        table = pltpu.roll(taps, 0, 1, stride=1, stride_axis=0)[:, :PW]
        high, low = split(table)
        across_high[b * PW : (b + 1) * PW, :] = high
        across_low[b * PW : (b + 1) * PW, :] = low
        taps = jnp.broadcast_to(basis[0, b : b + 1, :], (PH, PW + 128))
        table = pltpu.roll(taps, 0, 1, stride=1, stride_axis=0)[:, :PH]
        high, low = split(table)
        down_high[b * PH : (b + 1) * PH, :PH] = high
        down_high[b * PH : (b + 1) * PH, PH:] = high
        down_low[b * PH : (b + 1) * PH, :] = low


def make_bands(basis):
    vertical = basis[0][:, ::-1]
    taps = jnp.stack([vertical, basis[1]])
    gap = jnp.zeros((2, NB, PW + 128 - TAPS), f32)
    padded = jnp.concatenate([taps[:, :, HALF:], gap, taps[:, :, :HALF]], axis=2)
    return pl.pallas_call(
        bands_kernel,
        out_shape=(
            jax.ShapeDtypeStruct((NB * PH, 2 * PH), bf16),
            jax.ShapeDtypeStruct((NB * PH, PH), bf16),
            jax.ShapeDtypeStruct((NB * PW, PW), bf16),
            jax.ShapeDtypeStruct((NB * PW, PW), bf16),
        ),
        in_specs=[vmem],
        out_specs=(vmem,) * 4,
        compiler_params=pltpu.CompilerParams(vmem_limit_bytes=VMEM_LIMIT),
        name="bands",
    )(padded)


def pack_kernel(
    dest, row_offset, col_offset, live, weight, coefs, dest_v, row_v, col_v, live_v, weight_v, patches, out, second,
    slots, meta, patch_sems, meta_sem,
):
    count = patches.shape[0]
    tiles = out.shape[0]

    def clear(t, carry):
        slots[0, t] = -1
        slots[1, t] = -1
        return carry

    lax.fori_loop(0, tiles, clear, 0)

    def assign(k, carry):
        t = dest[0, k]
        rank = jnp.where(slots[0, t] >= 0, 1, 0)
        slots[rank, t] = k
        return carry

    lax.fori_loop(0, count, assign, 0)

    def send(t, carry):
        k = slots[0, t]

        @pl.when(k >= 0)
        def _():
            pltpu.make_async_copy(patches.at[k], out.at[t, pl.ds(0, PH)], patch_sems.at[t]).start()

        return carry

    lax.fori_loop(0, tiles, send, 0)

    def list_second(t, n):
        k = slots[1, t]

        @pl.when(k >= 0)
        def _():
            second[0, n] = k
            second[1, n] = t

        return n + jnp.where(k >= 0, 1, 0)

    def fill(j, carry):
        second[0, j] = 0
        second[1, j] = 0
        return carry

    lax.fori_loop(0, tiles, fill, 0)
    n_second = lax.fori_loop(0, tiles, list_second, 0)

    def repeat_last(j, carry):
        last = jnp.maximum(n_second - 1, 0)

        @pl.when(j >= n_second)
        def _():
            second[0, j] = second[0, last]
            second[1, j] = second[1, last]

        return carry

    lax.fori_loop(0, tiles, repeat_last, 0)
    second[2, 0] = n_second

    lane = lax.broadcasted_iota(i32, (1, 128), 1)
    base = jnp.zeros((META, PW), f32)
    meta[...] = jnp.broadcast_to(base[None], meta.shape)
    for row, values in enumerate((dest_v, row_v, col_v, live_v, weight_v)):
        line = values[...].astype(f32)
        for t in range(tiles):
            meta[t, row : row + 1, 0:count] = line

    def describe(t, carry):
        first = slots[0, t]
        k = jnp.maximum(first, 0)
        meta[t, 5:6, 0:NB] = coefs[pl.ds(k, 1), :] * weight[0, k]
        late = slots[1, t]
        j = jnp.maximum(late, 0)
        numbers = (
            jnp.where(first >= 0, 1, 0), row_offset[0, k], col_offset[0, k], live[0, k],
            jnp.where(late >= 0, 1, 0), row_offset[0, j], col_offset[0, j], live[0, j],
        )
        line = jnp.zeros((1, 128), i32)
        for place, number in enumerate(numbers):
            line = jnp.where(lane == place, number, line)
        meta[t, 6:7, 0:128] = line.astype(f32)
        return carry

    lax.fori_loop(0, tiles, describe, 0)
    about = pltpu.make_async_copy(meta, out.at[:, pl.ds(PH, META)], meta_sem)
    about.start()
    about.wait()

    def finish(t, carry):
        k = slots[0, t]

        @pl.when(k >= 0)
        def _():
            pltpu.make_async_copy(patches.at[k], out.at[t, pl.ds(0, PH)], patch_sems.at[t]).wait()

        return carry

    lax.fori_loop(0, tiles, finish, 0)


def pack(patches, dest, row_offset, col_offset, live_rows, weight, coefficient, tiles):
    return pl.pallas_call(
        pack_kernel,
        out_shape=(
            jax.ShapeDtypeStruct((tiles, PH + META, PW), f32),
            jax.ShapeDtypeStruct((3, tiles), i32),
        ),
        in_specs=[smem] * 5 + [vmem] * 6 + [anywhere],
        out_specs=(anywhere, smem),
        scratch_shapes=[
            pltpu.SMEM((CAP, tiles), i32),
            pltpu.VMEM((tiles, META, PW), f32),
            pltpu.SemaphoreType.DMA((tiles,)),
            pltpu.SemaphoreType.DMA,
        ],
        compiler_params=pltpu.CompilerParams(vmem_limit_bytes=VMEM_LIMIT),
        name="pack",
    )(
        dest, row_offset, col_offset, live_rows, weight, coefficient,
        dest, row_offset, col_offset, live_rows, weight, patches,
    )


def match(image, coefs, down_high, down_low, across_high, across_low, terms):
    high, low = split(image)
    both = jnp.concatenate([high, low], axis=0)
    downward = jnp.dot(down_high[...], both, preferred_element_type=f32)
    downward += jnp.dot(down_low[...], high, preferred_element_type=f32)
    for b in range(NB):
        high, low = split(downward[b * PH : (b + 1) * PH] * coefs[b])
        terms[:PH, b * PW : (b + 1) * PW] = high
        terms[PH:, b * PW : (b + 1) * PW] = low
    wide = jnp.dot(terms[...], across_high[...], preferred_element_type=f32)
    fine = jnp.dot(terms[:PH], across_low[...], preferred_element_type=f32)
    return wide[:PH] + wide[PH:] + fine


def live_mask(live):
    return lax.broadcasted_iota(i32, (PH, PW), 0) < live


def second_kernel(second, coefs, live, weight, patch, down_high, down_low, across_high, across_low, out, terms):
    j = pl.program_id(0)

    @pl.when(j < second[2, 0])
    def _():
        k = second[0, j]
        mask = live_mask(live[0, k])
        scaled = [coefs[k, b] * weight[0, k] for b in range(NB)]
        image = jnp.where(mask, patch[0], 0.0)
        matched = match(image, scaled, down_high, down_low, across_high, across_low, terms)
        out[0] = jnp.where(mask, matched, 0.0)


BAND_SHAPES = ((NB * PH, 2 * PH), (NB * PH, PH), (NB * PW, PW), (NB * PW, PW))


def match_second(second, coefficient, live_rows, weight, patches, bands, tiles):
    steps = patches.shape[0] // CAP
    return pl.pallas_call(
        second_kernel,
        out_shape=jax.ShapeDtypeStruct((tiles, PH, PW), f32),
        grid_spec=pltpu.PrefetchScalarGridSpec(
            num_scalar_prefetch=1,
            grid=(steps,),
            in_specs=[smem] * 3
            + [pl.BlockSpec((1, PH, PW), lambda j, second: (second[0, j], 0, 0))]
            + [whole(s) for s in BAND_SHAPES],
            out_specs=pl.BlockSpec((1, PH, PW), lambda j, second: (second[1, j], 0, 0)),
            scratch_shapes=[pltpu.VMEM((2 * PH, NB * PW), bf16)],
        ),
        compiler_params=pltpu.CompilerParams(vmem_limit_bytes=VMEM_LIMIT),
        cost_estimate=pl.CostEstimate(flops=5_000_000_000, bytes_accessed=6_000_000, transcendentals=0),
        name="match_second",
    )(second, coefficient, live_rows, weight, patches, *bands)


def place(canvas, piece, top, left):
    down = top % 8
    right = left % 128
    row = pl.multiple_of(top - down, 8)
    col = pl.multiple_of(left - right, 128)
    piece = jnp.concatenate([piece, jnp.zeros((8, PW), f32)], axis=0)
    piece = pltpu.roll(piece, down, 0)
    lane = lax.broadcasted_iota(i32, (PH + 8, 128), 1)
    near = pltpu.roll(piece[:, :128], right, 1)
    far = pltpu.roll(piece[:, 128:], right, 1)
    inside = lane >= right
    shifted = jnp.concatenate(
        [jnp.where(inside, near, 0.0), jnp.where(inside, far, near), jnp.where(inside, 0.0, far)], axis=1
    )
    canvas[pl.ds(row, PH + 8), pl.ds(col, PW + 128)] += shifted


def first_kernel(numbers, coefs, slot, down_high, down_low, across_high, across_low, canvas, terms):
    s = pl.program_id(0)

    @pl.when(s == 0)
    def _():
        canvas[...] = jnp.zeros_like(canvas)

    @pl.when(numbers[s, 0] > 0)
    def _():
        mask = live_mask(numbers[s, 3])
        image = jnp.where(mask, slot[0, :PH, :], 0.0)
        scaled = [coefs[s, b] for b in range(NB)]
        matched = match(image, scaled, down_high, down_low, across_high, across_low, terms)
        place(canvas, jnp.where(mask, matched, 0.0), numbers[s, 1] + MARGIN, numbers[s, 2] + MARGIN)


def match_first(numbers, coefs, slots, bands):
    tiles = slots.shape[0]
    return pl.pallas_call(
        first_kernel,
        out_shape=jax.ShapeDtypeStruct((CANVAS_ROWS, CANVAS_COLS), f32),
        grid=(tiles,),
        in_specs=[smem] * 2
        + [pl.BlockSpec((1, PH + META, PW), lambda s: (s, 0, 0))]
        + [whole(s) for s in BAND_SHAPES],
        out_specs=whole((CANVAS_ROWS, CANVAS_COLS)),
        scratch_shapes=[pltpu.VMEM((2 * PH, NB * PW), bf16)],
        compiler_params=pltpu.CompilerParams(vmem_limit_bytes=VMEM_LIMIT),
        cost_estimate=pl.CostEstimate(flops=10_000_000_000, bytes_accessed=8_000_000, transcendentals=0),
        name="match_first",
    )(numbers, coefs, slots, *bands)


def second_place_kernel(numbers, start, slot, north, south, middle, canvas):
    s = pl.program_id(0)

    @pl.when(s == 0)
    def _():
        canvas[...] = start[...]

    @pl.when(numbers[s, 4] > 0)
    def _():
        place(canvas, slot[0], numbers[s, 5] + MARGIN, numbers[s, 6] + MARGIN)

    @pl.when(s == pl.num_programs(0) - 1)
    def _():
        north[...] = canvas[:MARGIN, :SIDE]
        south[...] = canvas[MARGIN + TILE : SIDE, :SIDE]
        middle[...] = canvas[MARGIN : MARGIN + TILE, :SIDE]


def place_second(numbers, canvas, slots):
    tiles = slots.shape[0]
    strip = (MARGIN, SIDE)
    return pl.pallas_call(
        second_place_kernel,
        out_shape=(
            jax.ShapeDtypeStruct(strip, f32),
            jax.ShapeDtypeStruct(strip, f32),
            jax.ShapeDtypeStruct((TILE, SIDE), f32),
        ),
        grid=(tiles,),
        in_specs=[smem, whole((CANVAS_ROWS, CANVAS_COLS)), pl.BlockSpec((1, PH, PW), lambda s: (s, 0, 0))],
        out_specs=(whole(strip), whole(strip), whole((TILE, SIDE))),
        scratch_shapes=[pltpu.VMEM((CANVAS_ROWS, CANVAS_COLS), f32)],
        compiler_params=pltpu.CompilerParams(vmem_limit_bytes=VMEM_LIMIT),
        name="place_second",
    )(numbers, canvas, slots)


def depth_kernel(own, above, below, depth):
    total = jnp.zeros((TILE, TILE), f32)
    for about, step in ((own, 0), (above, -TILE), (below, TILE)):
        count = about.shape[1]
        place_at = lax.broadcasted_iota(i32, (TILE, count), 0).astype(f32)
        from_top = place_at - (about[0:1, :] + step)
        rows = jnp.where((from_top >= 0) & (from_top < about[2:3, :]), about[3:4, :], 0.0)
        from_left = place_at - about[1:2, :]
        cols = jnp.where((from_left >= 0) & (from_left < PW), 1.0, 0.0).astype(bf16)
        for part in split(rows):
            total += lax.dot_general(part, cols, (((1,), (1,)), ((), ())), preferred_element_type=f32)
    depth[...] = total


def make_depth(own, above, below):
    return pl.pallas_call(
        depth_kernel,
        out_shape=jax.ShapeDtypeStruct((TILE, TILE), f32),
        in_specs=[vmem] * 3,
        out_specs=vmem,
        compiler_params=pltpu.CompilerParams(vmem_limit_bytes=VMEM_LIMIT),
        cost_estimate=pl.CostEstimate(flops=1_000_000_000, bytes_accessed=1_000_000, transcendentals=0),
        name="make_depth",
    )(own, above, below)


def shifted(block, axis, distance):
    devices = range(lax.axis_size(axis))
    return lax.ppermute(block, axis, [(i - distance, i) for i in devices if i - distance in devices])


def edges_kernel(middle, from_above, from_below, west, east):
    low = TILE - MARGIN
    for out, cols in ((west, slice(0, MARGIN)), (east, slice(MARGIN + TILE, SIDE))):
        out[:MARGIN] = middle[:MARGIN, cols] + from_above[:, cols]
        out[MARGIN:low] = middle[MARGIN:low, cols]
        out[low:] = middle[low:, cols] + from_below[:, cols]


def make_edges(middle, from_above, from_below):
    edge = jax.ShapeDtypeStruct((TILE, MARGIN), f32)
    return pl.pallas_call(
        edges_kernel,
        out_shape=(edge, edge),
        in_specs=[vmem] * 3,
        out_specs=(vmem, vmem),
        compiler_params=pltpu.CompilerParams(vmem_limit_bytes=VMEM_LIMIT),
        name="make_edges",
    )(middle, from_above, from_below)


def final_kernel(middle, from_above, from_below, from_west, from_east, depth, coadd):
    core = slice(MARGIN, MARGIN + TILE)
    low = TILE - MARGIN
    coadd[...] = middle[:, core]
    coadd[:MARGIN] += from_above[:, core]
    coadd[low:] += from_below[:, core]
    coadd[:, :MARGIN] += from_west[...]
    coadd[:, low:] += from_east[...]
    coadd[...] = coadd[...] / (depth[...] + prior_weight)


def make_coadd(*parts):
    return pl.pallas_call(
        final_kernel,
        out_shape=jax.ShapeDtypeStruct((TILE, TILE), f32),
        in_specs=[vmem] * 6,
        out_specs=vmem,
        compiler_params=pltpu.CompilerParams(vmem_limit_bytes=VMEM_LIMIT),
        name="make_coadd",
    )(*parts)


def per_device(patches, dest, row_offset, col_offset, live_rows, weight, coefficient, basis):
    tiles = lax.axis_size("skyx")
    images = patches[0]
    outgoing, second = pack(
        images, dest[:, :, 0], row_offset, col_offset, live_rows, weight, coefficient[0], tiles
    )
    arrived = lax.all_to_all(outgoing, "skyx", split_axis=0, concat_axis=0, tiled=True)
    bands = make_bands(basis)
    late = match_second(second, coefficient[0], live_rows, weight, images, bands, tiles)
    late = lax.all_to_all(late, "skyx", split_axis=0, concat_axis=0, tiled=True)

    about = arrived[:, PH:, :128]
    numbers = about[:, 6, :16].astype(i32)
    coefs = about[:, 5, :NB]
    canvas = match_first(numbers, coefs, arrived, bands)

    band = jnp.transpose(about[:, :5, : images.shape[0]], (1, 0, 2)).reshape(5, -1)
    left = band[2] + (band[0] - lax.axis_index("skyx").astype(f32)) * TILE
    own = jnp.pad(jnp.stack([band[1], left, band[3], band[4]]), ((0, 4), (0, 0)))
    depth = make_depth(own, shifted(own, "skyy", 1), shifted(own, "skyy", -1))

    north, south, middle = place_second(numbers, canvas, late)
    from_above = shifted(south, "skyy", 1)
    from_below = shifted(north, "skyy", -1)
    west, east = make_edges(middle, from_above, from_below)
    from_west = shifted(east, "skyx", 1)
    from_east = shifted(west, "skyx", -1)
    coadd = make_coadd(middle, from_above, from_below, from_west, from_east, depth)
    return (coadd, depth)


def solution(mesh):
    in_specs = (
        P("skyy", "skyx", None, None),
        P("skyy", "skyx", None),
        P("skyy", "skyx"),
        P("skyy", "skyx"),
        P("skyy", "skyx"),
        P("skyy", "skyx"),
        P("skyy", "skyx", None),
        P(),
    )
    out_specs = (P("skyy", "skyx"), P("skyy", "skyx"))
    return jax.shard_map(
        per_device, mesh=mesh, in_specs=in_specs, out_specs=out_specs, check_vma=False
    )
```

```python
import jax
import jax.numpy as jnp
from jax import lax
from jax.experimental import pallas as pl
from jax.experimental.pallas import tpu as pltpu
from jax.sharding import PartitionSpec as P

TILE = 512
MARGIN = 128
CAP = 2
PH = 128
PW = 256
NB = 8
TAPS = 41
HALF = TAPS // 2
SIDE = TILE + 2 * MARGIN
CANVAS_ROWS = SIDE + 8
CANVAS_COLS = SIDE + 128
META = 8
GROUP = 4
MIB = 1024 * 1024

prior_weight = 0.5
f32 = jnp.float32
bf16 = jnp.bfloat16
i32 = jnp.int32


def whole(shape):
    return pl.BlockSpec(shape, lambda *_: (0,) * len(shape))


smem = pl.BlockSpec(memory_space=pltpu.SMEM)
vmem = pl.BlockSpec(memory_space=pltpu.VMEM)
anywhere = pl.BlockSpec(memory_space=pl.ANY)


def split(x):
    high = x.astype(bf16)
    return high, (x - high.astype(f32)).astype(bf16)


def fill_bands(basis, down_high, down_low, across_high, across_low):
    for b in range(NB):
        taps = jnp.broadcast_to(basis[1, b : b + 1, :], (PW, PW + 128))
        table = pltpu.roll(taps, 0, 1, stride=1, stride_axis=0)[:, :PW]
        high, low = split(table)
        across_high[b * PW : (b + 1) * PW, :] = high
        across_low[b * PW : (b + 1) * PW, :] = low
        taps = jnp.broadcast_to(basis[0, b : b + 1, :], (PH, PW + 128))
        table = pltpu.roll(taps, 0, 1, stride=1, stride_axis=0)[:, :PH]
        high, low = split(table)
        down_high[b * PH : (b + 1) * PH, :PH] = high
        down_high[b * PH : (b + 1) * PH, PH:] = high
        down_low[b * PH : (b + 1) * PH, :] = low


BANDS = [
    pltpu.VMEM((NB * PH, 2 * PH), bf16),
    pltpu.VMEM((NB * PH, PH), bf16),
    pltpu.VMEM((NB * PW, PW), bf16),
    pltpu.VMEM((NB * PW, PW), bf16),
]


def spread_taps(basis):
    taps = jnp.stack([basis[0][:, ::-1], basis[1]])
    gap = jnp.zeros((2, NB, PW + 128 - TAPS), f32)
    return jnp.concatenate([taps[:, :, HALF:], gap, taps[:, :, :HALF]], axis=2)


def pack_kernel(*refs):
    given, patches, out, second = refs[:6], refs[6], refs[7], refs[8]
    scalars, vectors = refs[9:15], refs[15:20]
    slots, held, meta, small_sems, in_sems, out_sems, meta_sem = refs[20:]
    dest, row_offset, col_offset, live, weight, coefs = scalars
    count = patches.shape[0]
    tiles = out.shape[0]

    def bring(k):
        return pltpu.make_async_copy(patches.at[k], held.at[k], in_sems.at[k])

    def give(k, t):
        return pltpu.make_async_copy(held.at[k], out.at[t, pl.ds(0, PH)], out_sems.at[k])

    small = [
        pltpu.make_async_copy(source, target, small_sems.at[n])
        for n, (source, target) in enumerate(zip(given + given[:5], scalars + vectors))
    ]
    for copy in small:
        copy.start()
    for k in range(count):
        bring(k).start()
    for copy in small:
        copy.wait()

    def clear(t, carry):
        slots[0, t] = -1
        slots[1, t] = -1
        return carry

    lax.fori_loop(0, tiles, clear, 0)

    def assign(k, carry):
        t = dest[0, k]
        rank = jnp.where(slots[0, t] >= 0, 1, 0)
        slots[rank, t] = k
        return carry

    lax.fori_loop(0, count, assign, 0)

    meta[...] = jnp.zeros_like(meta)
    for row, values in enumerate(vectors):
        line = values[...].astype(f32)
        for t in range(tiles):
            meta[t, row : row + 1, 0:count] = line

    def forward(k, carry):
        bring(k).wait()
        t = dest[0, k]

        @pl.when(slots[0, t] == k)
        def _():
            give(k, t).start()

        return carry

    lax.fori_loop(0, count, forward, 0)

    def list_second(t, n):
        k = slots[1, t]

        @pl.when(k >= 0)
        def _():
            second[0, n] = k
            second[1, n] = t

        return n + jnp.where(k >= 0, 1, 0)

    def fill(j, carry):
        second[0, j] = 0
        second[1, j] = 0
        return carry

    lax.fori_loop(0, tiles, fill, 0)
    n_second = lax.fori_loop(0, tiles, list_second, 0)

    def repeat_last(j, carry):
        last = jnp.maximum(n_second - 1, 0)

        @pl.when(j >= n_second)
        def _():
            second[0, j] = second[0, last]
            second[1, j] = second[1, last]

        return carry

    lax.fori_loop(0, tiles, repeat_last, 0)
    second[2, 0] = n_second

    lane = lax.broadcasted_iota(i32, (1, 128), 1)

    def describe(t, carry):
        first = slots[0, t]
        k = jnp.maximum(first, 0)
        late = slots[1, t]
        j = jnp.maximum(late, 0)
        numbers = (
            jnp.where(first >= 0, 1, 0), row_offset[0, k], col_offset[0, k], live[0, k],
            jnp.where(late >= 0, 1, 0), row_offset[0, j], col_offset[0, j], live[0, j],
        )
        line = jnp.zeros((1, 128), i32)
        for place, number in enumerate(numbers):
            line = jnp.where(lane == place, number, line)
        meta[t, 6:7, 0:128] = line.astype(f32)
        line = jnp.zeros((1, 128), f32)
        for b in range(NB):
            line = jnp.where(lane == b, coefs[b, k] * weight[0, k], line)
        meta[t, 5:6, 0:128] = line
        return carry

    lax.fori_loop(0, tiles, describe, 0, unroll=4)

    about = pltpu.make_async_copy(meta, out.at[:, pl.ds(PH, META)], meta_sem)
    about.start()

    def finish(k, carry):
        t = dest[0, k]

        @pl.when(slots[0, t] == k)
        def _():
            give(k, t).wait()

        return carry

    lax.fori_loop(0, count, finish, 0)
    about.wait()


def pack(patches, dest, row_offset, col_offset, live_rows, weight, coefficient, tiles):
    given = (dest, row_offset, col_offset, live_rows, weight, coefficient)
    return pl.pallas_call(
        pack_kernel,
        out_shape=(
            jax.ShapeDtypeStruct((tiles, PH + META, PW), f32),
            jax.ShapeDtypeStruct((3, tiles), i32),
        ),
        in_specs=[anywhere] * 7,
        out_specs=(anywhere, smem),
        scratch_shapes=[pltpu.SMEM(x.shape, x.dtype) for x in given]
        + [pltpu.VMEM(x.shape, x.dtype) for x in given[:5]]
        + [
            pltpu.SMEM((CAP, tiles), i32),
            pltpu.VMEM(patches.shape, f32),
            pltpu.VMEM((tiles, META, PW), f32),
            pltpu.SemaphoreType.DMA((11,)),
            pltpu.SemaphoreType.DMA(patches.shape[:1]),
            pltpu.SemaphoreType.DMA(patches.shape[:1]),
            pltpu.SemaphoreType.DMA,
        ],
        compiler_params=pltpu.CompilerParams(vmem_limit_bytes=62 * MIB),
        name="pack",
    )(*given, patches)


def match(images, coefs, terms, down_high, down_low, across_high, across_low):
    middle = PH * len(images)
    for g, (image, scales) in enumerate(zip(images, coefs)):
        high, low = split(image)
        both = jnp.concatenate([high, low], axis=0)
        rows = slice(g * PH, (g + 1) * PH)
        low_rows = slice(middle + g * PH, middle + (g + 1) * PH)
        for b in range(NB):
            taps = slice(b * PH, (b + 1) * PH)
            cols = slice(b * PW, (b + 1) * PW)
            downward = jnp.dot(down_high[taps], both, preferred_element_type=f32)
            downward += jnp.dot(down_low[taps], high, preferred_element_type=f32)
            terms[rows, cols], terms[low_rows, cols] = split(downward * scales[b])
    wide = jnp.dot(terms[...], across_high[...], preferred_element_type=f32)
    fine = jnp.dot(terms[:middle], across_low[...], preferred_element_type=f32)
    total = wide[:middle] + wide[middle:] + fine
    return [total[g * PH : (g + 1) * PH] for g in range(len(images))]


def live_mask(live):
    return lax.broadcasted_iota(i32, (PH, PW), 0) < live


def second_kernel(second, coefs, live, weight, row_offset, col_offset, patch, taps, out, terms, *bands):
    j = pl.program_id(0)

    @pl.when(j == 0)
    def _():
        fill_bands(taps, *bands)

    @pl.when(j < second[2, 0])
    def _():
        k = second[0, j]
        mask = live_mask(live[0, k])
        scaled = [coefs[b, k] * weight[0, k] for b in range(NB)]
        image = jnp.where(mask, patch[0], 0.0)
        (matched,) = match([image], [scaled], terms, *bands)
        out[0] = turn(jnp.where(mask, matched, 0.0), row_offset[0, k] + MARGIN, col_offset[0, k] + MARGIN)


def match_second(second, coefficient, live_rows, weight, row_offset, col_offset, patches, taps, tiles):
    steps = patches.shape[0] // CAP
    return pl.pallas_call(
        second_kernel,
        out_shape=jax.ShapeDtypeStruct((tiles, PH, PW), f32),
        grid_spec=pltpu.PrefetchScalarGridSpec(
            num_scalar_prefetch=1,
            grid=(steps,),
            in_specs=[smem] * 5
            + [pl.BlockSpec((1, PH, PW), lambda j, second: (second[0, j], 0, 0))]
            + [whole((2, NB, PW + 128))],
            out_specs=pl.BlockSpec((1, PH, PW), lambda j, second: (second[1, j], 0, 0)),
            scratch_shapes=[pltpu.VMEM((2 * PH, NB * PW), bf16)] + BANDS,
        ),
        compiler_params=pltpu.CompilerParams(vmem_limit_bytes=24 * MIB),
        cost_estimate=pl.CostEstimate(flops=5_000_000_000, bytes_accessed=6_000_000, transcendentals=0),
        name="match_second",
    )(second, coefficient, live_rows, weight, row_offset, col_offset, patches, taps)


def turn(piece, top, left):
    down = top % 8
    right = left % 128
    tiles = pltpu.roll(piece.reshape(PH // 8, 8, PW), down, 1)
    before = jnp.concatenate([tiles[-1:], tiles[:-1]], axis=0)
    wrapped = lax.broadcasted_iota(i32, tiles.shape, 1) < down
    piece = jnp.where(wrapped, before, tiles).reshape(PH, PW)
    near = pltpu.roll(piece[:, :128], right, 1)
    far = pltpu.roll(piece[:, 128:], right, 1)
    wrapped = lax.broadcasted_iota(i32, near.shape, 1) < right
    return jnp.concatenate([jnp.where(wrapped, far, near), jnp.where(wrapped, near, far)], axis=1)


def add_turned(canvas, piece, top, left):
    down = top % 8
    right = left % 128
    row = pl.multiple_of(top - down, 8)
    col = pl.multiple_of(left - right, 128)
    near = piece[:, :128]
    wrapped = lax.broadcasted_iota(i32, near.shape, 1) < right
    columns = (jnp.where(wrapped, 0.0, near), piece[:, 128:], jnp.where(wrapped, near, 0.0))
    over = lax.broadcasted_iota(i32, (8, 128), 0) < down
    for place, part in enumerate(columns):
        at = pl.ds(pl.multiple_of(col + 128 * place, 128), 128)
        canvas[pl.ds(row, 8), at] += jnp.where(over, 0.0, part[:8])
        canvas[pl.ds(pl.multiple_of(row + 8, 8), PH - 8), at] += part[8:]
        canvas[pl.ds(pl.multiple_of(row + PH, 8), 8), at] += jnp.where(over, part[:8], 0.0)


def first_kernel(slots, group, taps, out, numbers, canvas, about, sem, out_sem, terms, *bands):
    step = pl.program_id(0)
    tiles = slots.shape[0]
    told = pltpu.make_async_copy(slots.at[:, pl.ds(PH, META), pl.ds(0, 128)], about, sem)

    @pl.when(step == 0)
    def _():
        told.start()
        fill_bands(taps, *bands)
        canvas[...] = jnp.zeros_like(canvas)

    images, coefs, masks = [], [], []
    for g in range(GROUP):
        line = group[g, PH + 6 : PH + 7, 0:8]
        rows = jnp.broadcast_to(line[:, 3:4] * line[:, 0:1], (PH, PW)).astype(i32)
        mask = live_mask(rows)
        masks.append(mask)
        images.append(jnp.where(mask, group[g, :PH, :], 0.0))
        line = group[g, PH + 5 : PH + 6, 0:NB]
        coefs.append([line[:, b : b + 1] for b in range(NB)])
    matched = match(images, coefs, terms, *bands)

    @pl.when(step == 0)
    def _():
        told.wait()

        def tell(t, carry):
            for place in range(8):
                numbers[t, place] = about[t, 6, place].astype(i32)
            return carry

        lax.fori_loop(0, tiles, tell, 0)

    for g, (mask, image) in enumerate(zip(masks, matched)):
        t = step * GROUP + g
        corner = numbers[t, 1] + MARGIN, numbers[t, 2] + MARGIN
        add_turned(canvas, turn(jnp.where(mask, image, 0.0), *corner), *corner)

    @pl.when(step == pl.num_programs(0) - 1)
    def _():
        give = pltpu.make_async_copy(canvas.at[pl.ds(0, SIDE), pl.ds(0, SIDE)], out, out_sem)
        give.start()
        give.wait()


def match_first(slots, taps):
    tiles = slots.shape[0]
    return pl.pallas_call(
        first_kernel,
        out_shape=(
            jax.ShapeDtypeStruct((SIDE, SIDE), f32),
            jax.ShapeDtypeStruct((tiles, 8), i32),
        ),
        grid=(tiles // GROUP,),
        in_specs=[
            anywhere,
            pl.BlockSpec((GROUP, PH + META, PW), lambda s: (s, 0, 0)),
            whole((2, NB, PW + 128)),
        ],
        out_specs=(anywhere, smem),
        scratch_shapes=[
            pltpu.VMEM((CANVAS_ROWS, CANVAS_COLS), f32),
            pltpu.SMEM((tiles, META, 128), f32),
            pltpu.SemaphoreType.DMA,
            pltpu.SemaphoreType.DMA,
            pltpu.VMEM((2 * GROUP * PH, NB * PW), bf16),
        ]
        + BANDS,
        compiler_params=pltpu.CompilerParams(vmem_limit_bytes=62 * MIB),
        cost_estimate=pl.CostEstimate(flops=10_000_000_000, bytes_accessed=8_000_000, transcendentals=0),
        name="match_first",
    )(slots, slots, taps)


def second_place_kernel(numbers, start, slots, north, south, middle, west, east, canvas, held, base, sems, base_sem):
    tiles = slots.shape[0]

    def bring(t):
        return pltpu.make_async_copy(slots.at[t], held.at[t], sems.at[t])

    def fetch(t, carry):
        @pl.when(numbers[t, 4] > 0)
        def _():
            bring(t).start()

        return carry

    lax.fori_loop(0, tiles, fetch, 0)
    copy = pltpu.make_async_copy(start, base, base_sem)
    copy.start()
    canvas[...] = jnp.zeros_like(canvas)

    def add(t, carry):
        @pl.when(numbers[t, 4] > 0)
        def _():
            bring(t).wait()
            add_turned(canvas, held[t], numbers[t, 5] + MARGIN, numbers[t, 6] + MARGIN)

        return carry

    lax.fori_loop(0, tiles, add, 0)
    copy.wait()
    middle_rows = slice(MARGIN, MARGIN + TILE)
    inner = slice(2 * MARGIN, TILE)
    parts = (
        (north, slice(0, MARGIN), slice(0, SIDE)),
        (south, slice(MARGIN + TILE, SIDE), slice(0, SIDE)),
        (middle, middle_rows, slice(0, SIDE)),
        (west, inner, slice(0, MARGIN)),
        (east, inner, slice(MARGIN + TILE, SIDE)),
    )
    for out, rows, cols in parts:
        out[...] = base[rows, cols] + canvas[rows, cols]


def place_second(numbers, canvas, slots):
    strip = jax.ShapeDtypeStruct((MARGIN, SIDE), f32)
    side = jax.ShapeDtypeStruct((TILE - 2 * MARGIN, MARGIN), f32)
    return pl.pallas_call(
        second_place_kernel,
        out_shape=(strip, strip, jax.ShapeDtypeStruct((TILE, SIDE), f32), side, side),
        in_specs=[smem, anywhere, anywhere],
        out_specs=(vmem,) * 5,
        scratch_shapes=[
            pltpu.VMEM((CANVAS_ROWS, CANVAS_COLS), f32),
            pltpu.VMEM(slots.shape, f32),
            pltpu.VMEM(canvas.shape, f32),
            pltpu.SemaphoreType.DMA(slots.shape[:1]),
            pltpu.SemaphoreType.DMA,
        ],
        compiler_params=pltpu.CompilerParams(vmem_limit_bytes=20 * MIB),
        name="place_second",
    )(numbers, canvas, slots)


def depth_kernel(own, above, below, depth):
    total = jnp.zeros((TILE, TILE), f32)
    for about, step in ((own, 0), (above, -TILE), (below, TILE)):
        count = about.shape[1]
        place_at = lax.broadcasted_iota(i32, (TILE, count), 0).astype(f32)
        from_top = place_at - (about[0:1, :] + step)
        rows = jnp.where((from_top >= 0) & (from_top < about[2:3, :]), about[3:4, :], 0.0)
        from_left = place_at - about[1:2, :]
        cols = jnp.where((from_left >= 0) & (from_left < PW), 1.0, 0.0).astype(bf16)
        for part in split(rows):
            total += lax.dot_general(part, cols, (((1,), (1,)), ((), ())), preferred_element_type=f32)
    depth[...] = total


def make_depth(own, above, below):
    return pl.pallas_call(
        depth_kernel,
        out_shape=jax.ShapeDtypeStruct((TILE, TILE), f32),
        in_specs=[vmem] * 3,
        out_specs=vmem,
        compiler_params=pltpu.CompilerParams(vmem_limit_bytes=16 * MIB),
        cost_estimate=pl.CostEstimate(flops=1_000_000_000, bytes_accessed=1_000_000, transcendentals=0),
        name="make_depth",
    )(own, above, below)


def shifted(block, axis, distance):
    devices = range(lax.axis_size(axis))
    return lax.ppermute(block, axis, [(i - distance, i) for i in devices if i - distance in devices])


def edges_kernel(middle, from_above, from_below, west, east):
    low = TILE - MARGIN
    for out, cols in ((west, slice(0, MARGIN)), (east, slice(MARGIN + TILE, SIDE))):
        out[:MARGIN] = middle[:MARGIN, cols] + from_above[:, cols]
        out[MARGIN:] = middle[low:, cols] + from_below[:, cols]


def make_edges(middle, from_above, from_below):
    edge = jax.ShapeDtypeStruct((2 * MARGIN, MARGIN), f32)
    return pl.pallas_call(
        edges_kernel,
        out_shape=(edge, edge),
        in_specs=[vmem] * 3,
        out_specs=(vmem, vmem),
        compiler_params=pltpu.CompilerParams(vmem_limit_bytes=12 * MIB),
        name="make_edges",
    )(middle, from_above, from_below)


def final_kernel(middle, from_above, from_below, inner_west, inner_east, outer_west, outer_east, depth, coadd):
    core = slice(MARGIN, MARGIN + TILE)
    low = TILE - MARGIN
    coadd[...] = middle[:, core]
    coadd[:MARGIN] += from_above[:, core]
    coadd[low:] += from_below[:, core]
    for cols, inner, outer in ((slice(0, MARGIN), inner_west, outer_west), (slice(low, TILE), inner_east, outer_east)):
        coadd[:MARGIN, cols] += outer[:MARGIN]
        coadd[MARGIN:low, cols] += inner[...]
        coadd[low:, cols] += outer[MARGIN:]
    coadd[...] = coadd[...] / (depth[...] + prior_weight)


def make_coadd(*parts):
    return pl.pallas_call(
        final_kernel,
        out_shape=jax.ShapeDtypeStruct((TILE, TILE), f32),
        in_specs=[vmem] * 8,
        out_specs=vmem,
        compiler_params=pltpu.CompilerParams(vmem_limit_bytes=16 * MIB),
        name="make_coadd",
    )(*parts)


def per_device(patches, dest, row_offset, col_offset, live_rows, weight, coefficient, basis):
    tiles = lax.axis_size("skyx")
    images = patches[0]
    outgoing, second = pack(
        images, dest[:, :, 0], row_offset, col_offset, live_rows, weight, coefficient[0].T, tiles
    )
    arrived = lax.all_to_all(outgoing, "skyx", split_axis=0, concat_axis=0, tiled=True)
    taps = spread_taps(basis)
    late = match_second(second, coefficient[0].T, live_rows, weight, row_offset, col_offset, images, taps, tiles)
    late = lax.all_to_all(late, "skyx", split_axis=0, concat_axis=0, tiled=True)

    canvas, numbers = match_first(arrived, taps)

    about = arrived[:, PH : PH + 5, : images.shape[0]]
    band = jnp.transpose(about, (1, 0, 2)).reshape(5, -1)
    left = band[2] + (band[0] - lax.axis_index("skyx").astype(f32)) * TILE
    own = jnp.pad(jnp.stack([band[1], left, band[3], band[4]]), ((0, 4), (0, 0)))
    depth = make_depth(own, shifted(own, "skyy", 1), shifted(own, "skyy", -1))

    numbers, depth = lax.optimization_barrier((numbers, depth))
    north, south, middle, west, east = place_second(numbers, canvas, late)
    from_above = shifted(south, "skyy", 1)
    from_below = shifted(north, "skyy", -1)
    inner_west = shifted(east, "skyx", 1)
    inner_east = shifted(west, "skyx", -1)
    west, east = make_edges(middle, from_above, from_below)
    outer_west = shifted(east, "skyx", 1)
    outer_east = shifted(west, "skyx", -1)
    coadd = make_coadd(
        middle, from_above, from_below, inner_west, inner_east, outer_west, outer_east, depth
    )
    return (coadd, depth)


def solution(mesh):
    in_specs = (
        P("skyy", "skyx", None, None),
        P("skyy", "skyx", None),
        P("skyy", "skyx"),
        P("skyy", "skyx"),
        P("skyy", "skyx"),
        P("skyy", "skyx"),
        P("skyy", "skyx", None),
        P(),
    )
    out_specs = (P("skyy", "skyx"), P("skyy", "skyx"))
    return jax.shard_map(
        per_device, mesh=mesh, in_specs=in_specs, out_specs=out_specs, check_vma=False
    )
```

```python
import jax
import jax.numpy as jnp
from jax import lax
from jax.experimental import pallas as pl
from jax.experimental.pallas import tpu as pltpu
from jax.sharding import PartitionSpec as P

TILE = 512
MARGIN = 128
CAP = 2
PH = 128
PW = 256
NB = 8
TAPS = 41
HALF = TAPS // 2
SIDE = TILE + 2 * MARGIN
CANVAS_ROWS = SIDE + 8
CANVAS_COLS = SIDE + 128
META = 8
GROUP = 4
KEPT_ROWS = 20 * SIDE
MIB = 1024 * 1024

prior_weight = 0.5
f32 = jnp.float32
bf16 = jnp.bfloat16
i32 = jnp.int32


def whole(shape):
    return pl.BlockSpec(shape, lambda *_: (0,) * len(shape))


smem = pl.BlockSpec(memory_space=pltpu.SMEM)
vmem = pl.BlockSpec(memory_space=pltpu.VMEM)
anywhere = pl.BlockSpec(memory_space=pl.ANY)
hbm = pl.BlockSpec(memory_space=pltpu.HBM)


def split(x):
    high = x.astype(bf16)
    return high, (x - high.astype(f32)).astype(bf16)


def fill_bands(basis, down_high, down_low, across_high, across_low):
    for b in range(NB):
        taps = jnp.broadcast_to(basis[1, b : b + 1, :], (PW, PW + 128))
        table = pltpu.roll(taps, 0, 1, stride=1, stride_axis=0)[:, :PW]
        high, low = split(table)
        across_high[b * PW : (b + 1) * PW, :] = high
        across_low[b * PW : (b + 1) * PW, :] = low
        taps = jnp.broadcast_to(basis[0, b : b + 1, :], (PH, PW + 128))
        table = pltpu.roll(taps, 0, 1, stride=1, stride_axis=0)[:, :PH]
        high, low = split(table)
        down_high[b * PH : (b + 1) * PH, :PH] = high
        down_high[b * PH : (b + 1) * PH, PH:] = high
        down_low[b * PH : (b + 1) * PH, :] = low


BANDS = [
    pltpu.VMEM((NB * PH, 2 * PH), bf16),
    pltpu.VMEM((NB * PH, PH), bf16),
    pltpu.VMEM((NB * PW, PW), bf16),
    pltpu.VMEM((NB * PW, PW), bf16),
]


def spread_taps(basis):
    taps = jnp.stack([basis[0][:, ::-1], basis[1]])
    gap = jnp.zeros((2, NB, PW + 128 - TAPS), f32)
    return jnp.concatenate([taps[:, :, HALF:], gap, taps[:, :, :HALF]], axis=2)


def pack_kernel(*refs):
    given, patches, out, second = refs[:6], refs[6], refs[7], refs[8]
    scalars, vectors = refs[9:15], refs[15:20]
    slots, held, meta, small_sems, in_sems, out_sems, meta_sem = refs[20:]
    dest, row_offset, col_offset, live, weight, coefs = scalars
    count = patches.shape[0]
    tiles = out.shape[0]

    def bring(k):
        return pltpu.make_async_copy(patches.at[k], held.at[k], in_sems.at[k])

    def give(k, t):
        return pltpu.make_async_copy(held.at[k], out.at[t, pl.ds(0, PH)], out_sems.at[k])

    small = [
        pltpu.make_async_copy(source, target, small_sems.at[n])
        for n, (source, target) in enumerate(zip(given + given[:5], scalars + vectors))
    ]
    for copy in small:
        copy.start()
    for k in range(count):
        bring(k).start()
    for copy in small:
        copy.wait()

    def clear(t, carry):
        slots[0, t] = -1
        slots[1, t] = -1
        return carry

    lax.fori_loop(0, tiles, clear, 0)

    def assign(k, carry):
        t = dest[0, k]
        rank = jnp.where(slots[0, t] >= 0, 1, 0)
        slots[rank, t] = k
        return carry

    lax.fori_loop(0, count, assign, 0)

    meta[...] = jnp.zeros_like(meta)
    for row, values in enumerate(vectors):
        line = values[...].astype(f32)
        for t in range(tiles):
            meta[t, row : row + 1, 0:count] = line

    def forward(k, carry):
        bring(k).wait()
        t = dest[0, k]

        @pl.when(slots[0, t] == k)
        def _():
            give(k, t).start()

        return carry

    lax.fori_loop(0, count, forward, 0)

    def list_second(t, n):
        k = slots[1, t]

        @pl.when(k >= 0)
        def _():
            second[0, n] = k
            second[1, n] = t

        return n + jnp.where(k >= 0, 1, 0)

    def fill(j, carry):
        second[0, j] = 0
        second[1, j] = 0
        return carry

    lax.fori_loop(0, tiles, fill, 0)
    n_second = lax.fori_loop(0, tiles, list_second, 0)

    def repeat_last(j, carry):
        last = jnp.maximum(n_second - 1, 0)

        @pl.when(j >= n_second)
        def _():
            second[0, j] = second[0, last]
            second[1, j] = second[1, last]

        return carry

    lax.fori_loop(0, tiles, repeat_last, 0)
    second[2, 0] = n_second

    lane = lax.broadcasted_iota(i32, (1, 128), 1)

    def describe(t, carry):
        first = slots[0, t]
        k = jnp.maximum(first, 0)
        late = slots[1, t]
        j = jnp.maximum(late, 0)
        numbers = (
            jnp.where(first >= 0, 1, 0), row_offset[0, k], col_offset[0, k], live[0, k],
            jnp.where(late >= 0, 1, 0), row_offset[0, j], col_offset[0, j], live[0, j],
        )
        line = jnp.zeros((1, 128), i32)
        for place, number in enumerate(numbers):
            line = jnp.where(lane == place, number, line)
        meta[t, 6:7, 0:128] = line.astype(f32)
        line = jnp.zeros((1, 128), f32)
        for b in range(NB):
            line = jnp.where(lane == b, coefs[b, k] * weight[0, k], line)
        meta[t, 5:6, 0:128] = line
        return carry

    lax.fori_loop(0, tiles, describe, 0, unroll=4)

    about = pltpu.make_async_copy(meta, out.at[:, pl.ds(PH, META)], meta_sem)
    about.start()

    def finish(k, carry):
        t = dest[0, k]

        @pl.when(slots[0, t] == k)
        def _():
            give(k, t).wait()

        return carry

    lax.fori_loop(0, count, finish, 0)
    about.wait()


def pack(patches, dest, row_offset, col_offset, live_rows, weight, coefficient, tiles):
    given = (dest, row_offset, col_offset, live_rows, weight, coefficient)
    return pl.pallas_call(
        pack_kernel,
        out_shape=(
            jax.ShapeDtypeStruct((tiles, PH + META, PW), f32),
            jax.ShapeDtypeStruct((3, tiles), i32),
        ),
        in_specs=[anywhere] * 7,
        out_specs=(anywhere, smem),
        scratch_shapes=[pltpu.SMEM(x.shape, x.dtype) for x in given]
        + [pltpu.VMEM(x.shape, x.dtype) for x in given[:5]]
        + [
            pltpu.SMEM((CAP, tiles), i32),
            pltpu.VMEM(patches.shape, f32),
            pltpu.VMEM((tiles, META, PW), f32),
            pltpu.SemaphoreType.DMA((11,)),
            pltpu.SemaphoreType.DMA(patches.shape[:1]),
            pltpu.SemaphoreType.DMA(patches.shape[:1]),
            pltpu.SemaphoreType.DMA,
        ],
        compiler_params=pltpu.CompilerParams(vmem_limit_bytes=62 * MIB),
        name="pack",
    )(*given, patches)


def match(images, coefs, terms, down_high, down_low, across_high, across_low):
    middle = PH * len(images)
    for g, (image, scales) in enumerate(zip(images, coefs)):
        high, low = split(image)
        both = jnp.concatenate([high, low], axis=0)
        rows = slice(g * PH, (g + 1) * PH)
        low_rows = slice(middle + g * PH, middle + (g + 1) * PH)
        for b in range(NB):
            taps = slice(b * PH, (b + 1) * PH)
            cols = slice(b * PW, (b + 1) * PW)
            downward = jnp.dot(down_high[taps], both, preferred_element_type=f32)
            downward += jnp.dot(down_low[taps], high, preferred_element_type=f32)
            terms[rows, cols], terms[low_rows, cols] = split(downward * scales[b])
    wide = jnp.dot(terms[...], across_high[...], preferred_element_type=f32)
    fine = jnp.dot(terms[:middle], across_low[...], preferred_element_type=f32)
    total = wide[:middle] + wide[middle:] + fine
    return [total[g * PH : (g + 1) * PH] for g in range(len(images))]


def live_mask(live):
    return lax.broadcasted_iota(i32, (PH, PW), 0) < live


def second_kernel(second, coefs, live, weight, row_offset, col_offset, patch, taps, out, terms, *bands):
    j = pl.program_id(0)

    @pl.when(j == 0)
    def _():
        fill_bands(taps, *bands)

    @pl.when(j < second[2, 0])
    def _():
        k = second[0, j]
        mask = live_mask(live[0, k])
        scaled = [coefs[b, k] * weight[0, k] for b in range(NB)]
        image = jnp.where(mask, patch[0], 0.0)
        (matched,) = match([image], [scaled], terms, *bands)
        out[0] = turn(jnp.where(mask, matched, 0.0), row_offset[0, k] + MARGIN, col_offset[0, k] + MARGIN)


def match_second(second, coefficient, live_rows, weight, row_offset, col_offset, patches, taps, tiles):
    steps = patches.shape[0] // CAP
    return pl.pallas_call(
        second_kernel,
        out_shape=jax.ShapeDtypeStruct((tiles, PH, PW), f32),
        grid_spec=pltpu.PrefetchScalarGridSpec(
            num_scalar_prefetch=1,
            grid=(steps,),
            in_specs=[smem] * 5
            + [pl.BlockSpec((1, PH, PW), lambda j, second: (second[0, j], 0, 0))]
            + [whole((2, NB, PW + 128))],
            out_specs=pl.BlockSpec((1, PH, PW), lambda j, second: (second[1, j], 0, 0)),
            scratch_shapes=[pltpu.VMEM((2 * PH, NB * PW), bf16)] + BANDS,
        ),
        compiler_params=pltpu.CompilerParams(vmem_limit_bytes=24 * MIB),
        cost_estimate=pl.CostEstimate(flops=5_000_000_000, bytes_accessed=6_000_000, transcendentals=0),
        name="match_second",
    )(second, coefficient, live_rows, weight, row_offset, col_offset, patches, taps)


def turn(piece, top, left):
    down = top % 8
    right = left % 128
    tiles = pltpu.roll(piece.reshape(PH // 8, 8, PW), down, 1)
    before = jnp.concatenate([tiles[-1:], tiles[:-1]], axis=0)
    wrapped = lax.broadcasted_iota(i32, tiles.shape, 1) < down
    piece = jnp.where(wrapped, before, tiles).reshape(PH, PW)
    near = pltpu.roll(piece[:, :128], right, 1)
    far = pltpu.roll(piece[:, 128:], right, 1)
    wrapped = lax.broadcasted_iota(i32, near.shape, 1) < right
    return jnp.concatenate([jnp.where(wrapped, far, near), jnp.where(wrapped, near, far)], axis=1)


def add_turned(canvas, piece, top, left):
    down = top % 8
    right = left % 128
    row = pl.multiple_of(top - down, 8)
    col = pl.multiple_of(left - right, 128)
    near = piece[:, :128]
    wrapped = lax.broadcasted_iota(i32, near.shape, 1) < right
    columns = (jnp.where(wrapped, 0.0, near), piece[:, 128:], jnp.where(wrapped, near, 0.0))
    over = lax.broadcasted_iota(i32, (8, 128), 0) < down
    for place, part in enumerate(columns):
        at = pl.ds(pl.multiple_of(col + 128 * place, 128), 128)
        canvas[pl.ds(row, 8), at] += jnp.where(over, 0.0, part[:8])
        canvas[pl.ds(pl.multiple_of(row + 8, 8), PH - 8), at] += part[8:]
        canvas[pl.ds(pl.multiple_of(row + PH, 8), 8), at] += jnp.where(over, part[:8], 0.0)


def first_kernel(slots, group, taps, out, canvas, about, numbers, lines, sem, out_sem, terms, *bands):
    step = pl.program_id(0)
    tiles = slots.shape[0]
    told = pltpu.make_async_copy(slots.at[:, pl.ds(PH, META), pl.ds(0, 128)], about, sem)

    @pl.when(step == 0)
    def _():
        told.start()
        fill_bands(taps, *bands)
        canvas[...] = jnp.zeros_like(canvas)

    images, coefs, masks = [], [], []
    for g in range(GROUP):
        lines[pl.ds(step * GROUP + g, 1), :] = group[g, PH + 6 : PH + 7, 0:128]
        line = group[g, PH + 6 : PH + 7, 0:8]
        rows = jnp.broadcast_to(line[:, 3:4] * line[:, 0:1], (PH, PW)).astype(i32)
        mask = live_mask(rows)
        masks.append(mask)
        images.append(jnp.where(mask, group[g, :PH, :], 0.0))
        line = group[g, PH + 5 : PH + 6, 0:NB]
        coefs.append([line[:, b : b + 1] for b in range(NB)])
    matched = match(images, coefs, terms, *bands)

    @pl.when(step == 0)
    def _():
        told.wait()

        def tell(t, carry):
            for place in range(8):
                numbers[t, place] = about[t, 6, place].astype(i32)
            return carry

        lax.fori_loop(0, tiles, tell, 0)

    for g, (mask, image) in enumerate(zip(masks, matched)):
        t = step * GROUP + g
        corner = numbers[t, 1] + MARGIN, numbers[t, 2] + MARGIN
        add_turned(canvas, turn(jnp.where(mask, image, 0.0), *corner), *corner)

    @pl.when(step == pl.num_programs(0) - 1)
    def _():
        parts = (canvas.at[pl.ds(0, SIDE), pl.ds(0, SIDE)], lines)
        places = (out.at[pl.ds(0, SIDE)], out.at[pl.ds(SIDE, tiles), pl.ds(0, 128)])
        copies = [pltpu.make_async_copy(part, at, out_sem.at[n]) for n, (part, at) in enumerate(zip(parts, places))]
        for copy in copies:
            copy.start()
        for copy in copies:
            copy.wait()


def match_first(slots, taps):
    tiles = slots.shape[0]
    return pl.pallas_call(
        first_kernel,
        out_shape=jax.ShapeDtypeStruct((KEPT_ROWS, SIDE), f32),
        grid=(tiles // GROUP,),
        in_specs=[
            anywhere,
            pl.BlockSpec((GROUP, PH + META, PW), lambda s: (s, 0, 0)),
            whole((2, NB, PW + 128)),
        ],
        out_specs=anywhere,
        scratch_shapes=[
            pltpu.VMEM((CANVAS_ROWS, CANVAS_COLS), f32),
            pltpu.SMEM((tiles, META, 128), f32),
            pltpu.SMEM((tiles, 8), i32),
            pltpu.VMEM((tiles, 128), f32),
            pltpu.SemaphoreType.DMA,
            pltpu.SemaphoreType.DMA((2,)),
            pltpu.VMEM((2 * GROUP * PH, NB * PW), bf16),
        ]
        + BANDS,
        compiler_params=pltpu.CompilerParams(vmem_limit_bytes=62 * MIB),
        cost_estimate=pl.CostEstimate(flops=10_000_000_000, bytes_accessed=8_000_000, transcendentals=0),
        name="match_first",
    )(slots, slots, taps)


def second_place_kernel(
    kept, band, slots, rows_next, rows_last, middle, cols_next, cols_last,
    told, numbers, canvas, held, base, sems, base_sem, told_sem,
):
    tiles = slots.shape[0]

    def bring(t):
        return pltpu.make_async_copy(slots.at[t], held.at[t], sems.at[t])

    tell = pltpu.make_async_copy(kept.at[pl.ds(SIDE, tiles), pl.ds(0, 128)], told, told_sem)
    tell.start()
    copy = pltpu.make_async_copy(kept.at[pl.ds(0, SIDE)], base, base_sem)
    copy.start()
    canvas[...] = jnp.zeros_like(canvas)
    tell.wait()

    def fetch(t, carry):
        for place in range(4, 7):
            numbers[t, place] = told[t, place].astype(i32)

        @pl.when(numbers[t, 4] > 0)
        def _():
            bring(t).start()

        return carry

    lax.fori_loop(0, tiles, fetch, 0)

    def add(t, carry):
        @pl.when(numbers[t, 4] > 0)
        def _():
            bring(t).wait()
            add_turned(canvas, held[t], numbers[t, 5] + MARGIN, numbers[t, 6] + MARGIN)

        return carry

    lax.fori_loop(0, tiles, add, 0)
    copy.wait()
    low, high = slice(0, MARGIN), slice(MARGIN + TILE, SIDE)
    core, inner = slice(MARGIN, MARGIN + TILE), slice(2 * MARGIN, TILE)
    middle[...] = base[core] + canvas[core, :SIDE]
    for out in (rows_next, rows_last):
        out[MARGIN:] = jnp.zeros((META, SIDE), f32)
        out[MARGIN:, : band.shape[1]] = band[...]
    for axis, outs in (("skyy", (rows_next, rows_last)), ("skyx", (cols_next, cols_last))):
        for parity in range(2):

            @pl.when(lax.axis_index(axis) % 2 == parity)
            def _():
                for out, strip in zip(outs, (high, low) if parity == 0 else (low, high)):
                    rows, cols = (strip, slice(0, SIDE)) if axis == "skyy" else (inner, strip)
                    out[: rows.stop - rows.start] = base[rows, cols] + canvas[rows, cols]


def place_second(kept, band, slots):
    tiles = slots.shape[0]
    strip = jax.ShapeDtypeStruct((MARGIN + META, SIDE), f32)
    side = jax.ShapeDtypeStruct((TILE - 2 * MARGIN, MARGIN), f32)
    return pl.pallas_call(
        second_place_kernel,
        out_shape=(strip, strip, jax.ShapeDtypeStruct((TILE, SIDE), f32), side, side),
        in_specs=[anywhere, vmem, anywhere],
        out_specs=(vmem,) * 5,
        scratch_shapes=[
            pltpu.SMEM((tiles, 128), f32),
            pltpu.SMEM((tiles, 8), i32),
            pltpu.VMEM((CANVAS_ROWS, CANVAS_COLS), f32),
            pltpu.VMEM(slots.shape, f32),
            pltpu.VMEM((SIDE, SIDE), f32),
            pltpu.SemaphoreType.DMA(slots.shape[:1]),
            pltpu.SemaphoreType.DMA,
            pltpu.SemaphoreType.DMA,
        ],
        compiler_params=pltpu.CompilerParams(vmem_limit_bytes=20 * MIB),
        name="place_second",
    )(kept, band, slots)


def depth_kernel(own, rows_next, rows_last, depth, divisor):
    total = jnp.zeros((TILE, TILE), f32)
    count = own.shape[1]
    toward = jnp.where(lax.axis_index("skyy") % 2 == 0, TILE, -TILE).astype(f32)
    for about, step in ((own, 0.0), (rows_next, toward), (rows_last, -toward)):
        about = about[-META:, :count]
        place_at = lax.broadcasted_iota(i32, (TILE, count), 0).astype(f32)
        from_top = place_at - (about[0:1, :] + step)
        rows = jnp.where((from_top >= 0) & (from_top < about[2:3, :]), about[3:4, :], 0.0)
        from_left = place_at - about[1:2, :]
        cols = jnp.where((from_left >= 0) & (from_left < PW), 1.0, 0.0).astype(bf16)
        for part in split(rows):
            total += lax.dot_general(part, cols, (((1,), (1,)), ((), ())), preferred_element_type=f32)
    depth[...] = total
    divisor[...] = total + prior_weight


def make_depth(own, rows_next, rows_last):
    return pl.pallas_call(
        depth_kernel,
        out_shape=(jax.ShapeDtypeStruct((TILE, TILE), f32),) * 2,
        in_specs=[vmem] * 3,
        out_specs=(vmem, vmem),
        compiler_params=pltpu.CompilerParams(vmem_limit_bytes=16 * MIB),
        cost_estimate=pl.CostEstimate(flops=1_000_000_000, bytes_accessed=1_000_000, transcendentals=0),
        name="make_depth",
    )(own, rows_next, rows_last)


def exchange(block, axis, first):
    pairs = [(i, i + 1) for i in range(first, lax.axis_size(axis) - 1, 2)]
    return lax.ppermute(block, axis, pairs + [(j, i) for i, j in pairs])


def by_side(axis, following, preceding):
    even = lax.axis_index(axis) % 2 == 0
    return jnp.where(even, preceding, following), jnp.where(even, following, preceding)


def edges_kernel(middle, rows_next, rows_last, cols_next, cols_last):
    low = TILE - MARGIN
    strips = slice(0, MARGIN), slice(MARGIN + TILE, SIDE)
    for parity in range(2):

        @pl.when(lax.axis_index("skyx") % 2 == parity)
        def _():
            for out, cols in zip((cols_next, cols_last), strips[::-1] if parity == 0 else strips):
                above, below = by_side("skyy", rows_next[:MARGIN, cols], rows_last[:MARGIN, cols])
                out[:MARGIN] = middle[:MARGIN, cols] + above
                out[MARGIN:] = middle[low:, cols] + below


def make_edges(middle, rows_next, rows_last):
    edge = jax.ShapeDtypeStruct((2 * MARGIN, MARGIN), f32)
    return pl.pallas_call(
        edges_kernel,
        out_shape=(edge, edge),
        in_specs=[vmem] * 3,
        out_specs=(vmem, vmem),
        compiler_params=pltpu.CompilerParams(vmem_limit_bytes=12 * MIB),
        name="make_edges",
    )(middle, rows_next, rows_last)


def final_kernel(middle, rows_next, rows_last, inner_next, inner_last, outer_next, outer_last, divisor, coadd):
    core = slice(MARGIN, MARGIN + TILE)
    low = TILE - MARGIN
    above, below = by_side("skyy", rows_next[:MARGIN, core], rows_last[:MARGIN, core])
    coadd[...] = middle[:, core]
    coadd[:MARGIN] += above
    coadd[low:] += below
    inner = by_side("skyx", inner_next[...], inner_last[...])
    outer = by_side("skyx", outer_next[...], outer_last[...])
    for cols, close, far in zip((slice(0, MARGIN), slice(low, TILE)), inner, outer):
        coadd[:MARGIN, cols] += far[:MARGIN]
        coadd[MARGIN:low, cols] += close
        coadd[low:, cols] += far[MARGIN:]
    coadd[...] = coadd[...] / divisor[...]


def make_coadd(*parts):
    return pl.pallas_call(
        final_kernel,
        out_shape=jax.ShapeDtypeStruct((TILE, TILE), f32),
        in_specs=[vmem] * 8,
        out_specs=vmem,
        compiler_params=pltpu.CompilerParams(vmem_limit_bytes=16 * MIB),
        name="make_coadd",
    )(*parts)


def per_device(patches, dest, row_offset, col_offset, live_rows, weight, coefficient, basis):
    tiles = lax.axis_size("skyx")
    images = patches[0]
    outgoing, second = pack(
        images, dest[:, :, 0], row_offset, col_offset, live_rows, weight, coefficient[0].T, tiles
    )
    arrived = lax.all_to_all(outgoing, "skyx", split_axis=0, concat_axis=0, tiled=True)
    taps = spread_taps(basis)
    late = match_second(second, coefficient[0].T, live_rows, weight, row_offset, col_offset, images, taps, tiles)
    late = lax.all_to_all(late, "skyx", split_axis=0, concat_axis=0, tiled=True)

    kept = match_first(arrived, taps)

    about = arrived[:, PH : PH + 5, : images.shape[0]]
    band = jnp.transpose(about, (1, 0, 2)).reshape(5, -1)
    left = band[2] + (band[0] - lax.axis_index("skyx").astype(f32)) * TILE
    own = jnp.pad(jnp.stack([band[1], left, band[3], band[4]]), ((0, META - 4), (0, 0)))

    rows_next, rows_last, middle, cols_next, cols_last = place_second(kept, own, late)
    rows_last = exchange(rows_last, "skyy", 1)
    rows_next = exchange(rows_next, "skyy", 0)
    inner_last = exchange(cols_last, "skyx", 1)
    inner_next = exchange(cols_next, "skyx", 0)
    cols_next, cols_last = make_edges(middle, rows_next, rows_last)
    outer_last = exchange(cols_last, "skyx", 1)
    outer_next = exchange(cols_next, "skyx", 0)
    depth, divisor = make_depth(own, rows_next, rows_last)
    coadd = make_coadd(
        middle, rows_next, rows_last, inner_next, inner_last, outer_next, outer_last, divisor
    )
    return (coadd, depth)


def solution(mesh):
    in_specs = (
        P("skyy", "skyx", None, None),
        P("skyy", "skyx", None),
        P("skyy", "skyx"),
        P("skyy", "skyx"),
        P("skyy", "skyx"),
        P("skyy", "skyx"),
        P("skyy", "skyx", None),
        P(),
    )
    out_specs = (P("skyy", "skyx"), P("skyy", "skyx"))
    return jax.shard_map(
        per_device, mesh=mesh, in_specs=in_specs, out_specs=out_specs, check_vma=False
    )
```

```python
import jax
import jax.numpy as jnp
from jax import lax
from jax.experimental import pallas as pl
from jax.experimental.pallas import tpu as pltpu
from jax.sharding import PartitionSpec as P

TILE = 512
MARGIN = 128
CAP = 2
PH = 128
PW = 256
NB = 8
TAPS = 41
HALF = TAPS // 2
SIDE = TILE + 2 * MARGIN
CANVAS_ROWS = SIDE + 8
CANVAS_COLS = SIDE + 128
META = 8
HALF_COLS = PW // 2
SLOT = 2 * PH
GROUP = 4
KEPT_ROWS = 20 * SIDE
MIB = 1024 * 1024

prior_weight = 0.5
f32 = jnp.float32
bf16 = jnp.bfloat16
i32 = jnp.int32


def whole(shape):
    return pl.BlockSpec(shape, lambda *_: (0,) * len(shape))


smem = pl.BlockSpec(memory_space=pltpu.SMEM)
vmem = pl.BlockSpec(memory_space=pltpu.VMEM)
anywhere = pl.BlockSpec(memory_space=pl.ANY)
hbm = pl.BlockSpec(memory_space=pltpu.HBM)


def split(x):
    high = x.astype(bf16)
    return high, (x - high.astype(f32)).astype(bf16)


def fill_bands(basis, down_high, down_low, across_high, across_low):
    for b in range(NB):
        taps = jnp.broadcast_to(basis[1, b : b + 1, :], (PW, PW + 128))
        table = pltpu.roll(taps, 0, 1, stride=1, stride_axis=0)[:, :PW]
        high, low = split(table)
        across_high[b * PW : (b + 1) * PW, :] = high
        across_low[b * PW : (b + 1) * PW, :] = low
        taps = jnp.broadcast_to(basis[0, b : b + 1, :], (PH, PW + 128))
        table = pltpu.roll(taps, 0, 1, stride=1, stride_axis=0)[:, :PH]
        high, low = split(table)
        down_high[b * PH : (b + 1) * PH, :PH] = high
        down_high[b * PH : (b + 1) * PH, PH:] = high
        down_low[b * PH : (b + 1) * PH, :] = low


BANDS = [
    pltpu.VMEM((NB * PH, 2 * PH), bf16),
    pltpu.VMEM((NB * PH, PH), bf16),
    pltpu.VMEM((NB * PW, PW), bf16),
    pltpu.VMEM((NB * PW, PW), bf16),
]


def spread_taps(basis):
    taps = jnp.stack([basis[0][:, ::-1], basis[1]])
    gap = jnp.zeros((2, NB, PW + 128 - TAPS), f32)
    return jnp.concatenate([taps[:, :, HALF:], gap, taps[:, :, :HALF]], axis=2)


def assign_slots(dest, slots):
    tiles = slots.shape[1]
    for t in range(tiles):
        slots[0, t] = -1
        slots[1, t] = -1
    for k in range(dest.shape[1]):
        t = dest[0, k]
        rank = jnp.where(slots[0, t] >= 0, 1, 0)
        slots[rank, t] = k


def pack_kernel(*refs):
    given, patches, out = refs[:6], refs[6], refs[7]
    scalars, vectors = refs[8:14], refs[14:19]
    slots, held, meta, small_sems, in_sem, out_sems, meta_sem = refs[19:]
    dest, row_offset, col_offset, live, weight, coefs = scalars
    count = patches.shape[0]
    tiles = out.shape[0]

    def give(k, t, half):
        source = held.at[k, :, pl.ds(half * HALF_COLS, HALF_COLS)]
        return pltpu.make_async_copy(source, out.at[t, pl.ds(half * PH, PH)], out_sems.at[k, half])

    small = [
        pltpu.make_async_copy(source, target, small_sems.at[n])
        for n, (source, target) in enumerate(zip(given + given[:5], scalars + vectors))
    ]
    for copy in small:
        copy.start()
    bring = pltpu.make_async_copy(patches, held, in_sem)
    bring.start()
    meta[...] = jnp.zeros_like(meta)
    for copy in small:
        copy.wait()

    assign_slots(dest, slots)
    for row, values in enumerate(vectors):
        line = values[...].astype(f32)
        for t in range(tiles):
            meta[t, row : row + 1, 0:count] = line

    lane = lax.broadcasted_iota(i32, (1, 128), 1)

    def describe(t, carry):
        first = slots[0, t]
        k = jnp.maximum(first, 0)
        late = slots[1, t]
        j = jnp.maximum(late, 0)
        numbers = (
            jnp.where(first >= 0, 1, 0), row_offset[0, k], col_offset[0, k], live[0, k],
            jnp.where(late >= 0, 1, 0), row_offset[0, j], col_offset[0, j], live[0, j],
        )
        line = jnp.zeros((1, 128), i32)
        for place, number in enumerate(numbers):
            line = jnp.where(lane == place, number, line)
        meta[t, 6:7, 0:128] = line.astype(f32)
        line = jnp.zeros((1, 128), f32)
        for b in range(NB):
            line = jnp.where(lane == b, coefs[b, k] * weight[0, k], line)
        meta[t, 5:6, 0:128] = line
        return carry

    lax.fori_loop(0, tiles, describe, 0, unroll=4)
    about = pltpu.make_async_copy(meta, out.at[:, pl.ds(SLOT, META)], meta_sem)
    about.start()

    bring.wait()
    for k in range(count):
        t = dest[0, k]

        @pl.when(slots[0, t] == k)
        def _():
            give(k, t, 0).start()
            give(k, t, 1).start()

    for k in range(count):
        t = dest[0, k]

        @pl.when(slots[0, t] == k)
        def _():
            give(k, t, 0).wait()
            give(k, t, 1).wait()

    about.wait()


def pack(patches, dest, row_offset, col_offset, live_rows, weight, coefficient, tiles):
    given = (dest, row_offset, col_offset, live_rows, weight, coefficient)
    return pl.pallas_call(
        pack_kernel,
        out_shape=jax.ShapeDtypeStruct((tiles, SLOT + META, HALF_COLS), f32),
        in_specs=[anywhere] * 7,
        out_specs=anywhere,
        scratch_shapes=[pltpu.SMEM(x.shape, x.dtype) for x in given]
        + [pltpu.VMEM(x.shape, x.dtype) for x in given[:5]]
        + [
            pltpu.SMEM((CAP, tiles), i32),
            pltpu.VMEM(patches.shape, f32),
            pltpu.VMEM((tiles, META, HALF_COLS), f32),
            pltpu.SemaphoreType.DMA((11,)),
            pltpu.SemaphoreType.DMA,
            pltpu.SemaphoreType.DMA((patches.shape[0], 2)),
            pltpu.SemaphoreType.DMA,
        ],
        compiler_params=pltpu.CompilerParams(vmem_limit_bytes=62 * MIB),
        name="pack",
    )(*given, patches)


def list_kernel(dest, second, slots):
    tiles = slots.shape[1]
    assign_slots(dest, slots)
    for j in range(tiles):
        second[0, j] = 0
        second[1, j] = 0

    def note(t, n):
        k = slots[1, t]

        @pl.when(k >= 0)
        def _():
            second[0, n] = k
            second[1, n] = t

        return n + jnp.where(k >= 0, 1, 0)

    number = lax.fori_loop(0, tiles, note, 0)
    last = jnp.maximum(number - 1, 0)

    def repeat_last(j, carry):
        second[0, j] = second[0, last]
        second[1, j] = second[1, last]
        return carry

    lax.fori_loop(number, tiles, repeat_last, 0)
    for j in range(tiles):
        second[2, j] = number


def list_second(dest, tiles):
    return pl.pallas_call(
        list_kernel,
        out_shape=jax.ShapeDtypeStruct((3, tiles), i32),
        in_specs=[smem],
        out_specs=smem,
        scratch_shapes=[pltpu.SMEM((CAP, tiles), i32)],
        name="list_second",
    )(dest)


def match(images, coefs, terms, down_high, down_low, across_high, across_low):
    middle = PH * len(images)
    for g, (image, scales) in enumerate(zip(images, coefs)):
        high, low = split(image)
        both = jnp.concatenate([high, low], axis=0)
        rows = slice(g * PH, (g + 1) * PH)
        low_rows = slice(middle + g * PH, middle + (g + 1) * PH)
        for b in range(NB):
            taps = slice(b * PH, (b + 1) * PH)
            cols = slice(b * PW, (b + 1) * PW)
            downward = jnp.dot(down_high[taps], both, preferred_element_type=f32)
            downward += jnp.dot(down_low[taps], high, preferred_element_type=f32)
            terms[rows, cols], terms[low_rows, cols] = split(downward * scales[b])
    wide = jnp.dot(terms[...], across_high[...], preferred_element_type=f32)
    fine = jnp.dot(terms[:middle], across_low[...], preferred_element_type=f32)
    total = wide[:middle] + wide[middle:] + fine
    return [total[g * PH : (g + 1) * PH] for g in range(len(images))]


def live_mask(live):
    return lax.broadcasted_iota(i32, (PH, PW), 0) < live


def second_kernel(second, coefs, live, weight, row_offset, col_offset, patch, taps, out, terms, *bands):
    j = pl.program_id(0)

    @pl.when(j == 0)
    def _():
        fill_bands(taps, *bands)

    @pl.when(j < second[2, 0])
    def _():
        k = second[0, j]
        mask = live_mask(live[0, k])
        scaled = [coefs[b, k] * weight[0, k] for b in range(NB)]
        image = jnp.where(mask, patch[0], 0.0)
        (matched,) = match([image], [scaled], terms, *bands)
        out[0] = turn(jnp.where(mask, matched, 0.0), row_offset[0, k] + MARGIN, col_offset[0, k] + MARGIN)


def match_second(second, coefficient, live_rows, weight, row_offset, col_offset, patches, taps, tiles):
    steps = patches.shape[0] // CAP
    return pl.pallas_call(
        second_kernel,
        out_shape=jax.ShapeDtypeStruct((tiles, PH, PW), f32),
        grid_spec=pltpu.PrefetchScalarGridSpec(
            num_scalar_prefetch=1,
            grid=(steps,),
            in_specs=[smem] * 5
            + [pl.BlockSpec((1, PH, PW), lambda j, second: (second[0, j], 0, 0))]
            + [whole((2, NB, PW + 128))],
            out_specs=pl.BlockSpec((1, PH, PW), lambda j, second: (second[1, j], 0, 0)),
            scratch_shapes=[pltpu.VMEM((2 * PH, NB * PW), bf16)] + BANDS,
        ),
        compiler_params=pltpu.CompilerParams(vmem_limit_bytes=24 * MIB),
        cost_estimate=pl.CostEstimate(flops=5_000_000_000, bytes_accessed=6_000_000, transcendentals=0),
        name="match_second",
    )(second, coefficient, live_rows, weight, row_offset, col_offset, patches, taps)


def turn(piece, top, left):
    down = top % 8
    right = left % 128
    tiles = pltpu.roll(piece.reshape(PH // 8, 8, PW), down, 1)
    before = jnp.concatenate([tiles[-1:], tiles[:-1]], axis=0)
    wrapped = lax.broadcasted_iota(i32, tiles.shape, 1) < down
    piece = jnp.where(wrapped, before, tiles).reshape(PH, PW)
    near = pltpu.roll(piece[:, :128], right, 1)
    far = pltpu.roll(piece[:, 128:], right, 1)
    wrapped = lax.broadcasted_iota(i32, near.shape, 1) < right
    return jnp.concatenate([jnp.where(wrapped, far, near), jnp.where(wrapped, near, far)], axis=1)


def add_turned(canvas, piece, top, left):
    down = top % 8
    right = left % 128
    row = pl.multiple_of(top - down, 8)
    col = pl.multiple_of(left - right, 128)
    near = piece[:, :128]
    wrapped = lax.broadcasted_iota(i32, near.shape, 1) < right
    columns = (jnp.where(wrapped, 0.0, near), piece[:, 128:], jnp.where(wrapped, near, 0.0))
    over = lax.broadcasted_iota(i32, (8, 128), 0) < down
    for place, part in enumerate(columns):
        at = pl.ds(pl.multiple_of(col + 128 * place, 128), 128)
        canvas[pl.ds(row, 8), at] += jnp.where(over, 0.0, part[:8])
        canvas[pl.ds(pl.multiple_of(row + 8, 8), PH - 8), at] += part[8:]
        canvas[pl.ds(pl.multiple_of(row + PH, 8), 8), at] += jnp.where(over, part[:8], 0.0)


def first_kernel(slots, group, taps, out, canvas, about, numbers, lines, sem, out_sem, terms, *bands):
    step = pl.program_id(0)
    tiles = slots.shape[0]
    told = pltpu.make_async_copy(slots.at[:, pl.ds(SLOT, META)], about, sem)

    @pl.when(step == 0)
    def _():
        told.start()
        fill_bands(taps, *bands)
        canvas[...] = jnp.zeros_like(canvas)

    images, coefs, masks = [], [], []
    for g in range(GROUP):
        lines[pl.ds(step * GROUP + g, 1), :] = group[g, SLOT + 6 : SLOT + 7, :]
        line = group[g, SLOT + 6 : SLOT + 7, 0:8]
        rows = jnp.broadcast_to(line[:, 3:4] * line[:, 0:1], (PH, PW)).astype(i32)
        mask = live_mask(rows)
        masks.append(mask)
        image = jnp.concatenate([group[g, :PH, :], group[g, PH:SLOT, :]], axis=1)
        images.append(jnp.where(mask, image, 0.0))
        line = group[g, SLOT + 5 : SLOT + 6, 0:NB]
        coefs.append([line[:, b : b + 1] for b in range(NB)])
    matched = match(images, coefs, terms, *bands)

    @pl.when(step == 0)
    def _():
        told.wait()

        def tell(t, carry):
            for place in range(8):
                numbers[t, place] = about[t, 6, place].astype(i32)
            return carry

        lax.fori_loop(0, tiles, tell, 0)

    for g, (mask, image) in enumerate(zip(masks, matched)):
        t = step * GROUP + g
        corner = numbers[t, 1] + MARGIN, numbers[t, 2] + MARGIN
        add_turned(canvas, turn(jnp.where(mask, image, 0.0), *corner), *corner)

    @pl.when(step == pl.num_programs(0) - 1)
    def _():
        parts = (canvas.at[pl.ds(0, SIDE), pl.ds(0, SIDE)], lines)
        places = (out.at[pl.ds(0, SIDE)], out.at[pl.ds(SIDE, tiles), pl.ds(0, 128)])
        copies = [pltpu.make_async_copy(part, at, out_sem.at[n]) for n, (part, at) in enumerate(zip(parts, places))]
        for copy in copies:
            copy.start()
        for copy in copies:
            copy.wait()


def match_first(slots, taps):
    tiles = slots.shape[0]
    return pl.pallas_call(
        first_kernel,
        out_shape=jax.ShapeDtypeStruct((KEPT_ROWS, SIDE), f32),
        grid=(tiles // GROUP,),
        in_specs=[
            anywhere,
            pl.BlockSpec((GROUP, SLOT + META, HALF_COLS), lambda s: (s, 0, 0)),
            whole((2, NB, PW + 128)),
        ],
        out_specs=anywhere,
        scratch_shapes=[
            pltpu.VMEM((CANVAS_ROWS, CANVAS_COLS), f32),
            pltpu.SMEM((tiles, META, 128), f32),
            pltpu.SMEM((tiles, 8), i32),
            pltpu.VMEM((tiles, 128), f32),
            pltpu.SemaphoreType.DMA,
            pltpu.SemaphoreType.DMA((2,)),
            pltpu.VMEM((2 * GROUP * PH, NB * PW), bf16),
        ]
        + BANDS,
        compiler_params=pltpu.CompilerParams(vmem_limit_bytes=62 * MIB),
        cost_estimate=pl.CostEstimate(flops=10_000_000_000, bytes_accessed=8_000_000, transcendentals=0),
        name="match_first",
    )(slots, slots, taps)


def second_place_kernel(
    kept, band, slots, rows_next, rows_last, middle, cols_next, cols_last,
    told, numbers, canvas, held, base, sems, base_sem, told_sem,
):
    tiles = slots.shape[0]

    def bring(t):
        return pltpu.make_async_copy(slots.at[t], held.at[t], sems.at[t])

    tell = pltpu.make_async_copy(kept.at[pl.ds(SIDE, tiles), pl.ds(0, 128)], told, told_sem)
    tell.start()
    copy = pltpu.make_async_copy(kept.at[pl.ds(0, SIDE)], base, base_sem)
    copy.start()
    canvas[...] = jnp.zeros_like(canvas)
    tell.wait()

    def fetch(t, carry):
        for place in range(4, 7):
            numbers[t, place] = told[t, place].astype(i32)

        @pl.when(numbers[t, 4] > 0)
        def _():
            bring(t).start()

        return carry

    lax.fori_loop(0, tiles, fetch, 0)

    def add(t, carry):
        @pl.when(numbers[t, 4] > 0)
        def _():
            bring(t).wait()
            add_turned(canvas, held[t], numbers[t, 5] + MARGIN, numbers[t, 6] + MARGIN)

        return carry

    lax.fori_loop(0, tiles, add, 0)
    copy.wait()
    low, high = slice(0, MARGIN), slice(MARGIN + TILE, SIDE)
    core, inner = slice(MARGIN, MARGIN + TILE), slice(2 * MARGIN, TILE)
    middle[...] = base[core] + canvas[core, :SIDE]
    for out in (rows_next, rows_last):
        out[MARGIN:] = jnp.zeros((META, SIDE), f32)
        out[MARGIN:, : band.shape[1]] = band[...]
    for axis, outs in (("skyy", (rows_next, rows_last)), ("skyx", (cols_next, cols_last))):
        for parity in range(2):

            @pl.when(lax.axis_index(axis) % 2 == parity)
            def _():
                for out, strip in zip(outs, (high, low) if parity == 0 else (low, high)):
                    rows, cols = (strip, slice(0, SIDE)) if axis == "skyy" else (inner, strip)
                    out[: rows.stop - rows.start] = base[rows, cols] + canvas[rows, cols]


def place_second(kept, band, slots):
    tiles = slots.shape[0]
    strip = jax.ShapeDtypeStruct((MARGIN + META, SIDE), f32)
    side = jax.ShapeDtypeStruct((TILE - 2 * MARGIN, MARGIN), f32)
    return pl.pallas_call(
        second_place_kernel,
        out_shape=(strip, strip, jax.ShapeDtypeStruct((TILE, SIDE), f32), side, side),
        in_specs=[anywhere, vmem, anywhere],
        out_specs=(vmem,) * 5,
        scratch_shapes=[
            pltpu.SMEM((tiles, 128), f32),
            pltpu.SMEM((tiles, 8), i32),
            pltpu.VMEM((CANVAS_ROWS, CANVAS_COLS), f32),
            pltpu.VMEM(slots.shape, f32),
            pltpu.VMEM((SIDE, SIDE), f32),
            pltpu.SemaphoreType.DMA(slots.shape[:1]),
            pltpu.SemaphoreType.DMA,
            pltpu.SemaphoreType.DMA,
        ],
        compiler_params=pltpu.CompilerParams(vmem_limit_bytes=20 * MIB),
        name="place_second",
    )(kept, band, slots)


def depth_kernel(own, rows_next, rows_last, depth, divisor):
    total = jnp.zeros((TILE, TILE), f32)
    count = own.shape[1]
    toward = jnp.where(lax.axis_index("skyy") % 2 == 0, TILE, -TILE).astype(f32)
    for about, step in ((own, 0.0), (rows_next, toward), (rows_last, -toward)):
        about = about[-META:, :count]
        place_at = lax.broadcasted_iota(i32, (TILE, count), 0).astype(f32)
        from_top = place_at - (about[0:1, :] + step)
        rows = jnp.where((from_top >= 0) & (from_top < about[2:3, :]), about[3:4, :], 0.0)
        from_left = place_at - about[1:2, :]
        cols = jnp.where((from_left >= 0) & (from_left < PW), 1.0, 0.0).astype(bf16)
        for part in split(rows):
            total += lax.dot_general(part, cols, (((1,), (1,)), ((), ())), preferred_element_type=f32)
    depth[...] = total
    divisor[...] = total + prior_weight


def make_depth(own, rows_next, rows_last):
    return pl.pallas_call(
        depth_kernel,
        out_shape=(jax.ShapeDtypeStruct((TILE, TILE), f32),) * 2,
        in_specs=[vmem] * 3,
        out_specs=(vmem, vmem),
        compiler_params=pltpu.CompilerParams(vmem_limit_bytes=16 * MIB),
        cost_estimate=pl.CostEstimate(flops=1_000_000_000, bytes_accessed=1_000_000, transcendentals=0),
        name="make_depth",
    )(own, rows_next, rows_last)


def exchange(block, axis, first):
    pairs = [(i, i + 1) for i in range(first, lax.axis_size(axis) - 1, 2)]
    return lax.ppermute(block, axis, pairs + [(j, i) for i, j in pairs])


def by_side(axis, following, preceding):
    even = lax.axis_index(axis) % 2 == 0
    return jnp.where(even, preceding, following), jnp.where(even, following, preceding)


def edges_kernel(middle, rows_next, rows_last, cols_next, cols_last):
    low = TILE - MARGIN
    strips = slice(0, MARGIN), slice(MARGIN + TILE, SIDE)
    for parity in range(2):

        @pl.when(lax.axis_index("skyx") % 2 == parity)
        def _():
            for out, cols in zip((cols_next, cols_last), strips[::-1] if parity == 0 else strips):
                above, below = by_side("skyy", rows_next[:MARGIN, cols], rows_last[:MARGIN, cols])
                out[:MARGIN] = middle[:MARGIN, cols] + above
                out[MARGIN:] = middle[low:, cols] + below


def make_edges(middle, rows_next, rows_last):
    edge = jax.ShapeDtypeStruct((2 * MARGIN, MARGIN), f32)
    return pl.pallas_call(
        edges_kernel,
        out_shape=(edge, edge),
        in_specs=[vmem] * 3,
        out_specs=(vmem, vmem),
        compiler_params=pltpu.CompilerParams(vmem_limit_bytes=12 * MIB),
        name="make_edges",
    )(middle, rows_next, rows_last)


def final_kernel(middle, rows_next, rows_last, inner_next, inner_last, outer_next, outer_last, divisor, coadd):
    core = slice(MARGIN, MARGIN + TILE)
    low = TILE - MARGIN
    above, below = by_side("skyy", rows_next[:MARGIN, core], rows_last[:MARGIN, core])
    coadd[...] = middle[:, core]
    coadd[:MARGIN] += above
    coadd[low:] += below
    inner = by_side("skyx", inner_next[...], inner_last[...])
    outer = by_side("skyx", outer_next[...], outer_last[...])
    for cols, close, far in zip((slice(0, MARGIN), slice(low, TILE)), inner, outer):
        coadd[:MARGIN, cols] += far[:MARGIN]
        coadd[MARGIN:low, cols] += close
        coadd[low:, cols] += far[MARGIN:]
    coadd[...] = coadd[...] / divisor[...]


def make_coadd(*parts):
    return pl.pallas_call(
        final_kernel,
        out_shape=jax.ShapeDtypeStruct((TILE, TILE), f32),
        in_specs=[vmem] * 8,
        out_specs=vmem,
        compiler_params=pltpu.CompilerParams(vmem_limit_bytes=16 * MIB),
        name="make_coadd",
    )(*parts)


def per_device(patches, dest, row_offset, col_offset, live_rows, weight, coefficient, basis):
    tiles = lax.axis_size("skyx")
    images = patches[0]
    outgoing = pack(
        images, dest[:, :, 0], row_offset, col_offset, live_rows, weight, coefficient[0].T, tiles
    )
    arrived = lax.all_to_all(outgoing, "skyx", split_axis=0, concat_axis=0, tiled=True)
    taps = spread_taps(basis)
    second = list_second(dest[:, :, 0], tiles)
    late = match_second(second, coefficient[0].T, live_rows, weight, row_offset, col_offset, images, taps, tiles)
    late = lax.all_to_all(late, "skyx", split_axis=0, concat_axis=0, tiled=True)

    kept = match_first(arrived, taps)

    about = arrived[:, SLOT : SLOT + 5, : images.shape[0]]
    band = jnp.transpose(about, (1, 0, 2)).reshape(5, -1)
    left = band[2] + (band[0] - lax.axis_index("skyx").astype(f32)) * TILE
    own = jnp.pad(jnp.stack([band[1], left, band[3], band[4]]), ((0, META - 4), (0, 0)))

    rows_next, rows_last, middle, cols_next, cols_last = place_second(kept, own, late)
    rows_last = exchange(rows_last, "skyy", 1)
    rows_next = exchange(rows_next, "skyy", 0)
    inner_last = exchange(cols_last, "skyx", 1)
    inner_next = exchange(cols_next, "skyx", 0)
    cols_next, cols_last = make_edges(middle, rows_next, rows_last)
    outer_last = exchange(cols_last, "skyx", 1)
    outer_next = exchange(cols_next, "skyx", 0)
    depth, divisor = make_depth(own, rows_next, rows_last)
    coadd = make_coadd(
        middle, rows_next, rows_last, inner_next, inner_last, outer_next, outer_last, divisor
    )
    return (coadd, depth)


def solution(mesh):
    in_specs = (
        P("skyy", "skyx", None, None),
        P("skyy", "skyx", None),
        P("skyy", "skyx"),
        P("skyy", "skyx"),
        P("skyy", "skyx"),
        P("skyy", "skyx"),
        P("skyy", "skyx", None),
        P(),
    )
    out_specs = (P("skyy", "skyx"), P("skyy", "skyx"))
    return jax.shard_map(
        per_device, mesh=mesh, in_specs=in_specs, out_specs=out_specs, check_vma=False
    )
```

```python
import jax
import jax.numpy as jnp
from jax import lax
from jax.experimental import pallas as pl
from jax.experimental.pallas import tpu as pltpu
from jax.sharding import PartitionSpec as P

TILE = 512
MARGIN = 128
CAP = 2
PH = 128
PW = 256
NB = 8
TAPS = 41
HALF = TAPS // 2
SIDE = TILE + 2 * MARGIN
CANVAS_ROWS = SIDE + 8
CANVAS_COLS = SIDE + 128
META = 8
HALF_COLS = PW // 2
SLOT = 2 * PH
GROUP = 4
KEPT_ROWS = 20 * SIDE
MIB = 1024 * 1024

prior_weight = 0.5
f32 = jnp.float32
bf16 = jnp.bfloat16
i32 = jnp.int32


def whole(shape):
    return pl.BlockSpec(shape, lambda *_: (0,) * len(shape))


smem = pl.BlockSpec(memory_space=pltpu.SMEM)
vmem = pl.BlockSpec(memory_space=pltpu.VMEM)
anywhere = pl.BlockSpec(memory_space=pl.ANY)
hbm = pl.BlockSpec(memory_space=pltpu.HBM)


def split(x):
    high = x.astype(bf16)
    return high, (x - high.astype(f32)).astype(bf16)


def fill_bands(basis, down_high, down_low, across_high, across_low):
    for b in range(NB):
        taps = jnp.broadcast_to(basis[1, b : b + 1, :], (PW, PW + 128))
        table = pltpu.roll(taps, 0, 1, stride=1, stride_axis=0)[:, :PW]
        high, low = split(table)
        across_high[b * PW : (b + 1) * PW, :] = high
        across_low[b * PW : (b + 1) * PW, :] = low
        taps = jnp.broadcast_to(basis[0, b : b + 1, :], (PH, PW + 128))
        table = pltpu.roll(taps, 0, 1, stride=1, stride_axis=0)[:, :PH]
        high, low = split(table)
        down_high[b * PH : (b + 1) * PH, :PH] = high
        down_high[b * PH : (b + 1) * PH, PH:] = high
        down_low[b * PH : (b + 1) * PH, :] = low


BANDS = [
    pltpu.VMEM((NB * PH, 2 * PH), bf16),
    pltpu.VMEM((NB * PH, PH), bf16),
    pltpu.VMEM((NB * PW, PW), bf16),
    pltpu.VMEM((NB * PW, PW), bf16),
]


def spread_taps(basis):
    taps = jnp.stack([basis[0][:, ::-1], basis[1]])
    gap = jnp.zeros((2, NB, PW + 128 - TAPS), f32)
    return jnp.concatenate([taps[:, :, HALF:], gap, taps[:, :, :HALF]], axis=2)


def assign_slots(dest, slots):
    tiles = slots.shape[1]
    for t in range(tiles):
        slots[0, t] = -1
        slots[1, t] = -1
    for k in range(dest.shape[1]):
        t = dest[0, k]
        rank = jnp.where(slots[0, t] >= 0, 1, 0)
        slots[rank, t] = k


def pack_kernel(*refs):
    given, patches, out = refs[:6], refs[6], refs[7]
    scalars, vectors = refs[8:14], refs[14:19]
    slots, held, meta, small_sems, in_sem, out_sems, meta_sem = refs[19:]
    dest, row_offset, col_offset, live, weight, coefs = scalars
    count = patches.shape[0]
    tiles = out.shape[0]

    def give(k, t, half):
        source = held.at[k, :, pl.ds(half * HALF_COLS, HALF_COLS)]
        return pltpu.make_async_copy(source, out.at[t, pl.ds(half * PH, PH)], out_sems.at[k, half])

    small = [
        pltpu.make_async_copy(source, target, small_sems.at[n])
        for n, (source, target) in enumerate(zip(given + given[:5], scalars + vectors))
    ]
    for copy in small:
        copy.start()
    bring = pltpu.make_async_copy(patches, held, in_sem)
    bring.start()
    meta[...] = jnp.zeros_like(meta)
    for copy in small:
        copy.wait()

    assign_slots(dest, slots)
    for row, values in enumerate(vectors):
        line = values[...].astype(f32)
        for t in range(tiles):
            meta[t, row : row + 1, 0:count] = line

    lane = lax.broadcasted_iota(i32, (1, 128), 1)

    def describe(t, carry):
        first = slots[0, t]
        k = jnp.maximum(first, 0)
        late = slots[1, t]
        j = jnp.maximum(late, 0)
        numbers = (
            jnp.where(first >= 0, 1, 0), row_offset[0, k], col_offset[0, k], live[0, k],
            jnp.where(late >= 0, 1, 0), row_offset[0, j], col_offset[0, j], live[0, j],
        )
        line = jnp.zeros((1, 128), i32)
        for place, number in enumerate(numbers):
            line = jnp.where(lane == place, number, line)
        meta[t, 6:7, 0:128] = line.astype(f32)
        line = jnp.zeros((1, 128), f32)
        for b in range(NB):
            line = jnp.where(lane == b, coefs[b, k] * weight[0, k], line)
        meta[t, 5:6, 0:128] = line
        return carry

    lax.fori_loop(0, tiles, describe, 0, unroll=4)
    about = pltpu.make_async_copy(meta, out.at[:, pl.ds(SLOT, META)], meta_sem)
    about.start()

    bring.wait()
    for k in range(count):
        t = dest[0, k]

        @pl.when(slots[0, t] == k)
        def _():
            give(k, t, 0).start()
            give(k, t, 1).start()

    for k in range(count):
        t = dest[0, k]

        @pl.when(slots[0, t] == k)
        def _():
            give(k, t, 0).wait()
            give(k, t, 1).wait()

    about.wait()


def pack(patches, dest, row_offset, col_offset, live_rows, weight, coefficient, tiles):
    given = (dest, row_offset, col_offset, live_rows, weight, coefficient)
    return pl.pallas_call(
        pack_kernel,
        out_shape=jax.ShapeDtypeStruct((tiles, SLOT + META, HALF_COLS), f32),
        in_specs=[anywhere] * 7,
        out_specs=anywhere,
        scratch_shapes=[pltpu.SMEM(x.shape, x.dtype) for x in given]
        + [pltpu.VMEM(x.shape, x.dtype) for x in given[:5]]
        + [
            pltpu.SMEM((CAP, tiles), i32),
            pltpu.VMEM(patches.shape, f32),
            pltpu.VMEM((tiles, META, HALF_COLS), f32),
            pltpu.SemaphoreType.DMA((11,)),
            pltpu.SemaphoreType.DMA,
            pltpu.SemaphoreType.DMA((patches.shape[0], 2)),
            pltpu.SemaphoreType.DMA,
        ],
        compiler_params=pltpu.CompilerParams(vmem_limit_bytes=62 * MIB),
        name="pack",
    )(*given, patches)


def list_kernel(dest, second, slots):
    tiles = slots.shape[1]
    assign_slots(dest, slots)
    for j in range(tiles):
        second[0, j] = 0
        second[1, j] = 0

    def note(t, n):
        k = slots[1, t]

        @pl.when(k >= 0)
        def _():
            second[0, n] = k
            second[1, n] = t

        return n + jnp.where(k >= 0, 1, 0)

    number = lax.fori_loop(0, tiles, note, 0)
    last = jnp.maximum(number - 1, 0)

    def repeat_last(j, carry):
        second[0, j] = second[0, last]
        second[1, j] = second[1, last]
        return carry

    lax.fori_loop(number, tiles, repeat_last, 0)
    for j in range(tiles):
        second[2, j] = number


def list_second(dest, tiles):
    return pl.pallas_call(
        list_kernel,
        out_shape=jax.ShapeDtypeStruct((3, tiles), i32),
        in_specs=[smem],
        out_specs=smem,
        scratch_shapes=[pltpu.SMEM((CAP, tiles), i32)],
        name="list_second",
    )(dest)


def match(images, coefs, terms, down_high, down_low, across_high, across_low):
    middle = PH * len(images)
    for g, (image, scales) in enumerate(zip(images, coefs)):
        high, low = split(image)
        both = jnp.concatenate([high, low], axis=0)
        rows = slice(g * PH, (g + 1) * PH)
        low_rows = slice(middle + g * PH, middle + (g + 1) * PH)
        for b in range(NB):
            taps = slice(b * PH, (b + 1) * PH)
            cols = slice(b * PW, (b + 1) * PW)
            downward = jnp.dot(down_high[taps], both, preferred_element_type=f32)
            downward += jnp.dot(down_low[taps], high, preferred_element_type=f32)
            terms[rows, cols], terms[low_rows, cols] = split(downward * scales[b])
    wide = jnp.dot(terms[...], across_high[...], preferred_element_type=f32)
    fine = jnp.dot(terms[:middle], across_low[...], preferred_element_type=f32)
    total = wide[:middle] + wide[middle:] + fine
    return [total[g * PH : (g + 1) * PH] for g in range(len(images))]


def live_mask(live):
    return lax.broadcasted_iota(i32, (PH, PW), 0) < live


def second_kernel(second, coefs, live, weight, row_offset, col_offset, patch, taps, out, terms, *bands):
    j = pl.program_id(0)

    @pl.when(j == 0)
    def _():
        fill_bands(taps, *bands)

    @pl.when(j < second[2, 0])
    def _():
        k = second[0, j]
        mask = live_mask(live[0, k])
        scaled = [coefs[b, k] * weight[0, k] for b in range(NB)]
        image = jnp.where(mask, patch[0], 0.0)
        (matched,) = match([image], [scaled], terms, *bands)
        out[0] = turn(jnp.where(mask, matched, 0.0), row_offset[0, k] + MARGIN, col_offset[0, k] + MARGIN)


def match_second(second, coefficient, live_rows, weight, row_offset, col_offset, patches, taps, tiles):
    steps = patches.shape[0] // CAP
    return pl.pallas_call(
        second_kernel,
        out_shape=jax.ShapeDtypeStruct((tiles, PH, PW), f32),
        grid_spec=pltpu.PrefetchScalarGridSpec(
            num_scalar_prefetch=1,
            grid=(steps,),
            in_specs=[smem] * 5
            + [pl.BlockSpec((1, PH, PW), lambda j, second: (second[0, j], 0, 0))]
            + [whole((2, NB, PW + 128))],
            out_specs=pl.BlockSpec((1, PH, PW), lambda j, second: (second[1, j], 0, 0)),
            scratch_shapes=[pltpu.VMEM((2 * PH, NB * PW), bf16)] + BANDS,
        ),
        compiler_params=pltpu.CompilerParams(vmem_limit_bytes=24 * MIB),
        cost_estimate=pl.CostEstimate(flops=5_000_000_000, bytes_accessed=6_000_000, transcendentals=0),
        name="match_second",
    )(second, coefficient, live_rows, weight, row_offset, col_offset, patches, taps)


def turn(piece, top, left):
    down = top % 8
    right = left % 128
    tiles = pltpu.roll(piece.reshape(PH // 8, 8, PW), down, 1)
    before = jnp.concatenate([tiles[-1:], tiles[:-1]], axis=0)
    wrapped = lax.broadcasted_iota(i32, tiles.shape, 1) < down
    piece = jnp.where(wrapped, before, tiles).reshape(PH, PW)
    near = pltpu.roll(piece[:, :128], right, 1)
    far = pltpu.roll(piece[:, 128:], right, 1)
    wrapped = lax.broadcasted_iota(i32, near.shape, 1) < right
    return jnp.concatenate([jnp.where(wrapped, far, near), jnp.where(wrapped, near, far)], axis=1)


def add_turned(canvas, piece, top, left):
    down = top % 8
    right = left % 128
    row = pl.multiple_of(top - down, 8)
    col = pl.multiple_of(left - right, 128)
    near = piece[:, :128]
    wrapped = lax.broadcasted_iota(i32, near.shape, 1) < right
    columns = (jnp.where(wrapped, 0.0, near), piece[:, 128:], jnp.where(wrapped, near, 0.0))
    over = lax.broadcasted_iota(i32, (8, 128), 0) < down
    for place, part in enumerate(columns):
        at = pl.ds(pl.multiple_of(col + 128 * place, 128), 128)
        canvas[pl.ds(row, 8), at] += jnp.where(over, 0.0, part[:8])
        canvas[pl.ds(pl.multiple_of(row + 8, 8), PH - 8), at] += part[8:]
        canvas[pl.ds(pl.multiple_of(row + PH, 8), 8), at] += jnp.where(over, part[:8], 0.0)


def first_kernel(slots, group, taps, out, canvas, about, numbers, lines, sem, out_sem, terms, *bands):
    step = pl.program_id(0)
    tiles = slots.shape[0]
    told = pltpu.make_async_copy(slots.at[:, pl.ds(SLOT, META)], about, sem)

    @pl.when(step == 0)
    def _():
        told.start()
        fill_bands(taps, *bands)
        canvas[...] = jnp.zeros_like(canvas)

    images, coefs, masks = [], [], []
    for g in range(GROUP):
        lines[pl.ds(step * GROUP + g, 1), :] = group[g, SLOT + 6 : SLOT + 7, :]
        line = group[g, SLOT + 6 : SLOT + 7, 0:8]
        rows = jnp.broadcast_to(line[:, 3:4] * line[:, 0:1], (PH, PW)).astype(i32)
        mask = live_mask(rows)
        masks.append(mask)
        image = jnp.concatenate([group[g, :PH, :], group[g, PH:SLOT, :]], axis=1)
        images.append(jnp.where(mask, image, 0.0))
        line = group[g, SLOT + 5 : SLOT + 6, 0:NB]
        coefs.append([line[:, b : b + 1] for b in range(NB)])
    matched = match(images, coefs, terms, *bands)

    @pl.when(step == 0)
    def _():
        told.wait()

        def tell(t, carry):
            for place in range(8):
                numbers[t, place] = about[t, 6, place].astype(i32)
            return carry

        lax.fori_loop(0, tiles, tell, 0)

    for g, (mask, image) in enumerate(zip(masks, matched)):
        t = step * GROUP + g
        corner = numbers[t, 1] + MARGIN, numbers[t, 2] + MARGIN
        add_turned(canvas, turn(jnp.where(mask, image, 0.0), *corner), *corner)

    @pl.when(step == pl.num_programs(0) - 1)
    def _():
        parts = (canvas.at[pl.ds(0, SIDE), pl.ds(0, SIDE)], lines)
        places = (out.at[pl.ds(0, SIDE)], out.at[pl.ds(SIDE, tiles), pl.ds(0, 128)])
        copies = [pltpu.make_async_copy(part, at, out_sem.at[n]) for n, (part, at) in enumerate(zip(parts, places))]
        for copy in copies:
            copy.start()
        for copy in copies:
            copy.wait()


def match_first(slots, taps):
    tiles = slots.shape[0]
    return pl.pallas_call(
        first_kernel,
        out_shape=jax.ShapeDtypeStruct((KEPT_ROWS, SIDE), f32),
        grid=(tiles // GROUP,),
        in_specs=[
            anywhere,
            pl.BlockSpec((GROUP, SLOT + META, HALF_COLS), lambda s: (s, 0, 0)),
            whole((2, NB, PW + 128)),
        ],
        out_specs=anywhere,
        scratch_shapes=[
            pltpu.VMEM((CANVAS_ROWS, CANVAS_COLS), f32),
            pltpu.SMEM((tiles, META, 128), f32),
            pltpu.SMEM((tiles, 8), i32),
            pltpu.VMEM((tiles, 128), f32),
            pltpu.SemaphoreType.DMA,
            pltpu.SemaphoreType.DMA((2,)),
            pltpu.VMEM((2 * GROUP * PH, NB * PW), bf16),
        ]
        + BANDS,
        compiler_params=pltpu.CompilerParams(vmem_limit_bytes=61 * MIB),
        cost_estimate=pl.CostEstimate(flops=10_000_000_000, bytes_accessed=8_000_000, transcendentals=0),
        name="match_first",
    )(slots, slots, taps)


LOW, HIGH = slice(0, MARGIN), slice(MARGIN + TILE, SIDE)
CORE, INNER, ALL = slice(MARGIN, MARGIN + TILE), slice(2 * MARGIN, TILE), slice(0, SIDE)
STRIPS = ((LOW, ALL), (HIGH, ALL), (INNER, LOW), (INNER, HIGH))


def place_slots(kept, slots, parts, told, canvas, base, told_sem, base_sems):
    tiles = slots.shape[0]
    tell = pltpu.make_async_copy(kept.at[pl.ds(SIDE, tiles), pl.ds(0, 128)], told, told_sem)
    tell.start()
    copies = []
    for n, (rows, cols) in enumerate(parts):
        at = pl.ds(rows.start, rows.stop - rows.start), pl.ds(cols.start, cols.stop - cols.start)
        copies.append(pltpu.make_async_copy(kept.at[at], base.at[at], base_sems.at[n]))
        copies[-1].start()
    canvas[...] = jnp.zeros_like(canvas)
    tell.wait()

    def add(t, carry):
        @pl.when(told[t, 4] > 0)
        def _():
            corner = told[t, 5].astype(i32) + MARGIN, told[t, 6].astype(i32) + MARGIN
            add_turned(canvas, slots[t], *corner)

        return carry

    lax.fori_loop(0, tiles, add, 0)
    for copy in copies:
        copy.wait()


def strips_kernel(
    kept, band, slots, rows_next, rows_last, cols_next, cols_last, told, canvas, base, told_sem, base_sems
):
    place_slots(kept, slots, STRIPS, told, canvas, base, told_sem, base_sems)
    for out in (rows_next, rows_last):
        out[MARGIN:] = jnp.zeros((META, SIDE), f32)
        out[MARGIN:, : band.shape[1]] = band[...]
    for axis, outs in (("skyy", (rows_next, rows_last)), ("skyx", (cols_next, cols_last))):
        for parity in range(2):

            @pl.when(lax.axis_index(axis) % 2 == parity)
            def _():
                for out, strip in zip(outs, (HIGH, LOW) if parity == 0 else (LOW, HIGH)):
                    rows, cols = (strip, ALL) if axis == "skyy" else (INNER, strip)
                    out[: rows.stop - rows.start] = base[rows, cols] + canvas[rows, cols]


def place_scratch(slots, parts):
    return [
        pltpu.SMEM((slots.shape[0], 128), f32),
        pltpu.VMEM((CANVAS_ROWS, CANVAS_COLS), f32),
        pltpu.VMEM((SIDE, SIDE), f32),
        pltpu.SemaphoreType.DMA,
        pltpu.SemaphoreType.DMA((parts,)),
    ]


def make_strips(kept, band, slots):
    strip = jax.ShapeDtypeStruct((MARGIN + META, SIDE), f32)
    side = jax.ShapeDtypeStruct((TILE - 2 * MARGIN, MARGIN), f32)
    return pl.pallas_call(
        strips_kernel,
        out_shape=(strip, strip, side, side),
        in_specs=[anywhere, vmem, vmem],
        out_specs=(vmem,) * 4,
        scratch_shapes=place_scratch(slots, len(STRIPS)),
        compiler_params=pltpu.CompilerParams(vmem_limit_bytes=20 * MIB),
        name="place_second",
    )(kept, band, slots)


def middle_kernel(kept, slots, middle, told, canvas, base, told_sem, base_sems):
    place_slots(kept, slots, ((CORE, ALL),), told, canvas, base, told_sem, base_sems)
    middle[...] = base[CORE] + canvas[CORE, :SIDE]


def make_middle(kept, slots):
    return pl.pallas_call(
        middle_kernel,
        out_shape=jax.ShapeDtypeStruct((TILE, SIDE), f32),
        in_specs=[anywhere, vmem],
        out_specs=vmem,
        scratch_shapes=place_scratch(slots, 1),
        compiler_params=pltpu.CompilerParams(vmem_limit_bytes=20 * MIB),
        cost_estimate=pl.CostEstimate(flops=400_000, bytes_accessed=4_000_000, transcendentals=0),
        name="make_middle",
    )(kept, slots)


def depth_kernel(own, rows_next, rows_last, depth, divisor):
    total = jnp.zeros((TILE, TILE), f32)
    count = own.shape[1]
    toward = jnp.where(lax.axis_index("skyy") % 2 == 0, TILE, -TILE).astype(f32)
    for about, step in ((own, 0.0), (rows_next, toward), (rows_last, -toward)):
        about = about[-META:, :count]
        place_at = lax.broadcasted_iota(i32, (TILE, count), 0).astype(f32)
        from_top = place_at - (about[0:1, :] + step)
        rows = jnp.where((from_top >= 0) & (from_top < about[2:3, :]), about[3:4, :], 0.0)
        from_left = place_at - about[1:2, :]
        cols = jnp.where((from_left >= 0) & (from_left < PW), 1.0, 0.0).astype(bf16)
        for part in split(rows):
            total += lax.dot_general(part, cols, (((1,), (1,)), ((), ())), preferred_element_type=f32)
    depth[...] = total
    divisor[...] = total + prior_weight


def make_depth(own, rows_next, rows_last):
    return pl.pallas_call(
        depth_kernel,
        out_shape=(jax.ShapeDtypeStruct((TILE, TILE), f32),) * 2,
        in_specs=[vmem] * 3,
        out_specs=(vmem, vmem),
        compiler_params=pltpu.CompilerParams(vmem_limit_bytes=16 * MIB),
        cost_estimate=pl.CostEstimate(flops=1_000_000_000, bytes_accessed=1_000_000, transcendentals=0),
        name="make_depth",
    )(own, rows_next, rows_last)


def exchange(block, axis, first):
    pairs = [(i, i + 1) for i in range(first, lax.axis_size(axis) - 1, 2)]
    return lax.ppermute(block, axis, pairs + [(j, i) for i, j in pairs])


def by_side(axis, following, preceding):
    even = lax.axis_index(axis) % 2 == 0
    return jnp.where(even, preceding, following), jnp.where(even, following, preceding)


def edges_kernel(middle, rows_next, rows_last, cols_next, cols_last):
    low = TILE - MARGIN
    strips = slice(0, MARGIN), slice(MARGIN + TILE, SIDE)
    for parity in range(2):

        @pl.when(lax.axis_index("skyx") % 2 == parity)
        def _():
            for out, cols in zip((cols_next, cols_last), strips[::-1] if parity == 0 else strips):
                above, below = by_side("skyy", rows_next[:MARGIN, cols], rows_last[:MARGIN, cols])
                out[:MARGIN] = middle[:MARGIN, cols] + above
                out[MARGIN:] = middle[low:, cols] + below


def make_edges(middle, rows_next, rows_last):
    edge = jax.ShapeDtypeStruct((2 * MARGIN, MARGIN), f32)
    return pl.pallas_call(
        edges_kernel,
        out_shape=(edge, edge),
        in_specs=[vmem] * 3,
        out_specs=(vmem, vmem),
        compiler_params=pltpu.CompilerParams(vmem_limit_bytes=12 * MIB),
        name="make_edges",
    )(middle, rows_next, rows_last)


def final_kernel(middle, rows_next, rows_last, inner_next, inner_last, outer_next, outer_last, divisor, coadd):
    core = slice(MARGIN, MARGIN + TILE)
    low = TILE - MARGIN
    above, below = by_side("skyy", rows_next[:MARGIN, core], rows_last[:MARGIN, core])
    coadd[...] = middle[:, core]
    coadd[:MARGIN] += above
    coadd[low:] += below
    inner = by_side("skyx", inner_next[...], inner_last[...])
    outer = by_side("skyx", outer_next[...], outer_last[...])
    for cols, close, far in zip((slice(0, MARGIN), slice(low, TILE)), inner, outer):
        coadd[:MARGIN, cols] += far[:MARGIN]
        coadd[MARGIN:low, cols] += close
        coadd[low:, cols] += far[MARGIN:]
    coadd[...] = coadd[...] / divisor[...]


def make_coadd(*parts):
    return pl.pallas_call(
        final_kernel,
        out_shape=jax.ShapeDtypeStruct((TILE, TILE), f32),
        in_specs=[vmem] * 8,
        out_specs=vmem,
        compiler_params=pltpu.CompilerParams(vmem_limit_bytes=16 * MIB),
        name="make_coadd",
    )(*parts)


def per_device(patches, dest, row_offset, col_offset, live_rows, weight, coefficient, basis):
    tiles = lax.axis_size("skyx")
    images = patches[0]
    outgoing = pack(
        images, dest[:, :, 0], row_offset, col_offset, live_rows, weight, coefficient[0].T, tiles
    )
    arrived = lax.all_to_all(outgoing, "skyx", split_axis=0, concat_axis=0, tiled=True)
    taps = spread_taps(basis)
    second = list_second(dest[:, :, 0], tiles)
    late = match_second(second, coefficient[0].T, live_rows, weight, row_offset, col_offset, images, taps, tiles)
    late = lax.all_to_all(late, "skyx", split_axis=0, concat_axis=0, tiled=True)

    kept = match_first(arrived, taps)

    about = arrived[:, SLOT : SLOT + 5, : images.shape[0]]
    band = jnp.transpose(about, (1, 0, 2)).reshape(5, -1)
    left = band[2] + (band[0] - lax.axis_index("skyx").astype(f32)) * TILE
    own = jnp.pad(jnp.stack([band[1], left, band[3], band[4]]), ((0, META - 4), (0, 0)))

    rows_next, rows_last, cols_next, cols_last = make_strips(kept, own, late)
    rows_last = exchange(rows_last, "skyy", 1)
    rows_next = exchange(rows_next, "skyy", 0)
    inner_last = exchange(cols_last, "skyx", 1)
    inner_next = exchange(cols_next, "skyx", 0)
    middle = make_middle(kept, late)
    cols_next, cols_last = make_edges(middle, rows_next, rows_last)
    outer_last = exchange(cols_last, "skyx", 1)
    outer_next = exchange(cols_next, "skyx", 0)
    depth, divisor = make_depth(own, rows_next, rows_last)
    coadd = make_coadd(
        middle, rows_next, rows_last, inner_next, inner_last, outer_next, outer_last, divisor
    )
    return (coadd, depth)


def solution(mesh):
    in_specs = (
        P("skyy", "skyx", None, None),
        P("skyy", "skyx", None),
        P("skyy", "skyx"),
        P("skyy", "skyx"),
        P("skyy", "skyx"),
        P("skyy", "skyx"),
        P("skyy", "skyx", None),
        P(),
    )
    out_specs = (P("skyy", "skyx"), P("skyy", "skyx"))
    return jax.shard_map(
        per_device, mesh=mesh, in_specs=in_specs, out_specs=out_specs, check_vma=False
    )
```

```python
import functools

import jax
import jax.numpy as jnp
from jax import lax
from jax.experimental import pallas as pl
from jax.experimental.pallas import tpu as pltpu
from jax.sharding import PartitionSpec as P

TILE = 512
MARGIN = 128
CAP = 2
PH = 128
PW = 256
NB = 8
TAPS = 41
HALF = TAPS // 2
SIDE = TILE + 2 * MARGIN
CANVAS_ROWS = SIDE + 8
CANVAS_COLS = SIDE + 128
META = 8
HALF_COLS = PW // 2
SLOT = 2 * PH
GROUP = 4
KEPT_ROWS = 20 * SIDE
MIB = 1024 * 1024

prior_weight = 0.5
f32 = jnp.float32
bf16 = jnp.bfloat16
i32 = jnp.int32


def whole(shape):
    return pl.BlockSpec(shape, lambda *_: (0,) * len(shape))


smem = pl.BlockSpec(memory_space=pltpu.SMEM)
vmem = pl.BlockSpec(memory_space=pltpu.VMEM)
anywhere = pl.BlockSpec(memory_space=pl.ANY)
hbm = pl.BlockSpec(memory_space=pltpu.HBM)


def split(x):
    high = x.astype(bf16)
    return high, (x - high.astype(f32)).astype(bf16)


def fill_bands(basis, down_high, down_low, across_high, across_low):
    for b in range(NB):
        taps = jnp.broadcast_to(basis[1, b : b + 1, :], (PW, PW + 128))
        table = pltpu.roll(taps, 0, 1, stride=1, stride_axis=0)[:, :PW]
        high, low = split(table)
        across_high[b * PW : (b + 1) * PW, :] = high
        across_low[b * PW : (b + 1) * PW, :] = low
        taps = jnp.broadcast_to(basis[0, b : b + 1, :], (PH, PW + 128))
        table = pltpu.roll(taps, 0, 1, stride=1, stride_axis=0)[:, :PH]
        high, low = split(table)
        down_high[b * PH : (b + 1) * PH, :PH] = high
        down_high[b * PH : (b + 1) * PH, PH:] = high
        down_low[b * PH : (b + 1) * PH, :] = low


BANDS = [
    pltpu.VMEM((NB * PH, 2 * PH), bf16),
    pltpu.VMEM((NB * PH, PH), bf16),
    pltpu.VMEM((NB * PW, PW), bf16),
    pltpu.VMEM((NB * PW, PW), bf16),
]


def spread_taps(basis):
    taps = jnp.stack([basis[0][:, ::-1], basis[1]])
    gap = jnp.zeros((2, NB, PW + 128 - TAPS), f32)
    return jnp.concatenate([taps[:, :, HALF:], gap, taps[:, :, :HALF]], axis=2)


def assign_slots(dest, slots):
    tiles = slots.shape[1]
    for t in range(tiles):
        slots[0, t] = -1
        slots[1, t] = -1
    for k in range(dest.shape[1]):
        t = dest[0, k]
        rank = jnp.where(slots[0, t] >= 0, 1, 0)
        slots[rank, t] = k


def pack_kernel(*refs):
    given, patches, out = refs[:6], refs[6], refs[7]
    scalars, vectors = refs[8:14], refs[14:19]
    slots, held, meta, small_sems, in_sem, out_sems, meta_sem = refs[19:]
    dest, row_offset, col_offset, live, weight, coefs = scalars
    count = patches.shape[0]
    tiles = out.shape[0]

    def give(k, t, half):
        source = held.at[k, :, pl.ds(half * HALF_COLS, HALF_COLS)]
        return pltpu.make_async_copy(source, out.at[t, pl.ds(half * PH, PH)], out_sems.at[k, half])

    small = [
        pltpu.make_async_copy(source, target, small_sems.at[n])
        for n, (source, target) in enumerate(zip(given + given[:5], scalars + vectors))
    ]
    for copy in small:
        copy.start()
    bring = pltpu.make_async_copy(patches, held, in_sem)
    bring.start()
    meta[...] = jnp.zeros_like(meta)
    for copy in small:
        copy.wait()

    assign_slots(dest, slots)
    for row, values in enumerate(vectors):
        line = values[...].astype(f32)
        for t in range(tiles):
            meta[t, row : row + 1, 0:count] = line

    lane = lax.broadcasted_iota(i32, (1, 128), 1)

    def describe(t, carry):
        first = slots[0, t]
        k = jnp.maximum(first, 0)
        late = slots[1, t]
        j = jnp.maximum(late, 0)
        numbers = (
            jnp.where(first >= 0, 1, 0), row_offset[0, k], col_offset[0, k], live[0, k],
            jnp.where(late >= 0, 1, 0), row_offset[0, j], col_offset[0, j], live[0, j],
        )
        line = jnp.zeros((1, 128), i32)
        for place, number in enumerate(numbers):
            line = jnp.where(lane == place, number, line)
        meta[t, 6:7, 0:128] = line.astype(f32)
        line = jnp.zeros((1, 128), f32)
        for b in range(NB):
            line = jnp.where(lane == b, coefs[b, k] * weight[0, k], line)
        meta[t, 5:6, 0:128] = line
        return carry

    lax.fori_loop(0, tiles, describe, 0, unroll=4)
    about = pltpu.make_async_copy(meta, out.at[:, pl.ds(SLOT, META)], meta_sem)
    about.start()

    bring.wait()
    for k in range(count):
        t = dest[0, k]

        @pl.when(slots[0, t] == k)
        def _():
            give(k, t, 0).start()
            give(k, t, 1).start()

    for k in range(count):
        t = dest[0, k]

        @pl.when(slots[0, t] == k)
        def _():
            give(k, t, 0).wait()
            give(k, t, 1).wait()

    about.wait()


def pack(patches, dest, row_offset, col_offset, live_rows, weight, coefficient, tiles):
    given = (dest, row_offset, col_offset, live_rows, weight, coefficient)
    return pl.pallas_call(
        pack_kernel,
        out_shape=jax.ShapeDtypeStruct((tiles, SLOT + META, HALF_COLS), f32),
        in_specs=[anywhere] * 7,
        out_specs=anywhere,
        scratch_shapes=[pltpu.SMEM(x.shape, x.dtype) for x in given]
        + [pltpu.VMEM(x.shape, x.dtype) for x in given[:5]]
        + [
            pltpu.SMEM((CAP, tiles), i32),
            pltpu.VMEM(patches.shape, f32),
            pltpu.VMEM((tiles, META, HALF_COLS), f32),
            pltpu.SemaphoreType.DMA((11,)),
            pltpu.SemaphoreType.DMA,
            pltpu.SemaphoreType.DMA((patches.shape[0], 2)),
            pltpu.SemaphoreType.DMA,
        ],
        compiler_params=pltpu.CompilerParams(vmem_limit_bytes=62 * MIB),
        name="pack",
    )(*given, patches)


def list_kernel(dest, second, slots):
    tiles = slots.shape[1]
    assign_slots(dest, slots)
    for j in range(tiles):
        second[0, j] = 0
        second[1, j] = 0

    def note(t, n):
        k = slots[1, t]

        @pl.when(k >= 0)
        def _():
            second[0, n] = k
            second[1, n] = t

        return n + jnp.where(k >= 0, 1, 0)

    number = lax.fori_loop(0, tiles, note, 0)
    last = jnp.maximum(number - 1, 0)

    def repeat_last(j, carry):
        second[0, j] = second[0, last]
        second[1, j] = second[1, last]
        return carry

    lax.fori_loop(number, tiles, repeat_last, 0)
    for j in range(tiles):
        second[2, j] = number


def list_second(dest, tiles):
    return pl.pallas_call(
        list_kernel,
        out_shape=jax.ShapeDtypeStruct((3, tiles), i32),
        in_specs=[smem],
        out_specs=smem,
        scratch_shapes=[pltpu.SMEM((CAP, tiles), i32)],
        name="list_second",
    )(dest)


def match(images, coefs, terms, down_high, down_low, across_high, across_low):
    middle = PH * len(images)
    for g, (image, scales) in enumerate(zip(images, coefs)):
        high, low = split(image)
        both = jnp.concatenate([high, low], axis=0)
        rows = slice(g * PH, (g + 1) * PH)
        low_rows = slice(middle + g * PH, middle + (g + 1) * PH)
        for b in range(NB):
            taps = slice(b * PH, (b + 1) * PH)
            cols = slice(b * PW, (b + 1) * PW)
            downward = jnp.dot(down_high[taps], both, preferred_element_type=f32)
            downward += jnp.dot(down_low[taps], high, preferred_element_type=f32)
            terms[rows, cols], terms[low_rows, cols] = split(downward * scales[b])
    wide = jnp.dot(terms[...], across_high[...], preferred_element_type=f32)
    fine = jnp.dot(terms[:middle], across_low[...], preferred_element_type=f32)
    total = wide[:middle] + wide[middle:] + fine
    return [total[g * PH : (g + 1) * PH] for g in range(len(images))]


def live_mask(live):
    return lax.broadcasted_iota(i32, (PH, PW), 0) < live


def second_kernel(second, coefs, live, weight, row_offset, col_offset, patch, taps, out, terms, *bands):
    j = pl.program_id(0)

    @pl.when(j == 0)
    def _():
        fill_bands(taps, *bands)

    @pl.when(j < second[2, 0])
    def _():
        k = second[0, j]
        mask = live_mask(live[0, k])
        scaled = [coefs[b, k] * weight[0, k] for b in range(NB)]
        image = jnp.where(mask, patch[0], 0.0)
        (matched,) = match([image], [scaled], terms, *bands)
        out[0] = turn(jnp.where(mask, matched, 0.0), row_offset[0, k] + MARGIN, col_offset[0, k] + MARGIN)


def match_second(second, coefficient, live_rows, weight, row_offset, col_offset, patches, taps, tiles):
    steps = patches.shape[0] // CAP
    return pl.pallas_call(
        second_kernel,
        out_shape=jax.ShapeDtypeStruct((tiles, PH, PW), f32),
        grid_spec=pltpu.PrefetchScalarGridSpec(
            num_scalar_prefetch=1,
            grid=(steps,),
            in_specs=[smem] * 5
            + [pl.BlockSpec((1, PH, PW), lambda j, second: (second[0, j], 0, 0))]
            + [whole((2, NB, PW + 128))],
            out_specs=pl.BlockSpec((1, PH, PW), lambda j, second: (second[1, j], 0, 0)),
            scratch_shapes=[pltpu.VMEM((2 * PH, NB * PW), bf16)] + BANDS,
        ),
        compiler_params=pltpu.CompilerParams(vmem_limit_bytes=24 * MIB),
        cost_estimate=pl.CostEstimate(flops=5_000_000_000, bytes_accessed=6_000_000, transcendentals=0),
        name="match_second",
    )(second, coefficient, live_rows, weight, row_offset, col_offset, patches, taps)


def turn(piece, top, left):
    down = top % 8
    right = left % 128
    tiles = pltpu.roll(piece.reshape(PH // 8, 8, PW), down, 1)
    before = jnp.concatenate([tiles[-1:], tiles[:-1]], axis=0)
    wrapped = lax.broadcasted_iota(i32, tiles.shape, 1) < down
    piece = jnp.where(wrapped, before, tiles).reshape(PH, PW)
    near = pltpu.roll(piece[:, :128], right, 1)
    far = pltpu.roll(piece[:, 128:], right, 1)
    wrapped = lax.broadcasted_iota(i32, near.shape, 1) < right
    return jnp.concatenate([jnp.where(wrapped, far, near), jnp.where(wrapped, near, far)], axis=1)


def add_turned(canvas, piece, top, left):
    down = top % 8
    right = left % 128
    row = pl.multiple_of(top - down, 8)
    col = pl.multiple_of(left - right, 128)
    near = piece[:, :128]
    wrapped = lax.broadcasted_iota(i32, near.shape, 1) < right
    columns = (jnp.where(wrapped, 0.0, near), piece[:, 128:], jnp.where(wrapped, near, 0.0))
    over = lax.broadcasted_iota(i32, (8, 128), 0) < down
    for place, part in enumerate(columns):
        at = pl.ds(pl.multiple_of(col + 128 * place, 128), 128)
        canvas[pl.ds(row, 8), at] += jnp.where(over, 0.0, part[:8])
        canvas[pl.ds(pl.multiple_of(row + 8, 8), PH - 8), at] += part[8:]
        canvas[pl.ds(pl.multiple_of(row + PH, 8), 8), at] += jnp.where(over, part[:8], 0.0)


def first_kernel(slots, group, taps, out, canvas, about, numbers, lines, sem, out_sem, terms, *bands):
    step = pl.program_id(0)
    tiles = slots.shape[0]
    told = pltpu.make_async_copy(slots.at[:, pl.ds(SLOT, META)], about, sem)

    @pl.when(step == 0)
    def _():
        told.start()
        fill_bands(taps, *bands)
        canvas[...] = jnp.zeros_like(canvas)

    images, coefs, masks = [], [], []
    for g in range(GROUP):
        lines[pl.ds(step * GROUP + g, 1), :] = group[g, SLOT + 6 : SLOT + 7, :]
        line = group[g, SLOT + 6 : SLOT + 7, 0:8]
        rows = jnp.broadcast_to(line[:, 3:4] * line[:, 0:1], (PH, PW)).astype(i32)
        mask = live_mask(rows)
        masks.append(mask)
        image = jnp.concatenate([group[g, :PH, :], group[g, PH:SLOT, :]], axis=1)
        images.append(jnp.where(mask, image, 0.0))
        line = group[g, SLOT + 5 : SLOT + 6, 0:NB]
        coefs.append([line[:, b : b + 1] for b in range(NB)])
    matched = match(images, coefs, terms, *bands)

    @pl.when(step == 0)
    def _():
        told.wait()

        def tell(t, carry):
            for place in range(8):
                numbers[t, place] = about[t, 6, place].astype(i32)
            return carry

        lax.fori_loop(0, tiles, tell, 0)

    for g, (mask, image) in enumerate(zip(masks, matched)):
        t = step * GROUP + g
        corner = numbers[t, 1] + MARGIN, numbers[t, 2] + MARGIN
        add_turned(canvas, turn(jnp.where(mask, image, 0.0), *corner), *corner)

    @pl.when(step == pl.num_programs(0) - 1)
    def _():
        parts = (canvas.at[pl.ds(0, SIDE), pl.ds(0, SIDE)], lines)
        places = (out.at[pl.ds(0, SIDE)], out.at[pl.ds(SIDE, tiles), pl.ds(0, 128)])
        copies = [pltpu.make_async_copy(part, at, out_sem.at[n]) for n, (part, at) in enumerate(zip(parts, places))]
        for copy in copies:
            copy.start()
        for copy in copies:
            copy.wait()


def match_first(slots, taps):
    tiles = slots.shape[0]
    return pl.pallas_call(
        first_kernel,
        out_shape=jax.ShapeDtypeStruct((KEPT_ROWS, SIDE), f32),
        grid=(tiles // GROUP,),
        in_specs=[
            anywhere,
            pl.BlockSpec((GROUP, SLOT + META, HALF_COLS), lambda s: (s, 0, 0)),
            whole((2, NB, PW + 128)),
        ],
        out_specs=anywhere,
        scratch_shapes=[
            pltpu.VMEM((CANVAS_ROWS, CANVAS_COLS), f32),
            pltpu.SMEM((tiles, META, 128), f32),
            pltpu.SMEM((tiles, 8), i32),
            pltpu.VMEM((tiles, 128), f32),
            pltpu.SemaphoreType.DMA,
            pltpu.SemaphoreType.DMA((2,)),
            pltpu.VMEM((2 * GROUP * PH, NB * PW), bf16),
        ]
        + BANDS,
        compiler_params=pltpu.CompilerParams(vmem_limit_bytes=61 * MIB),
        cost_estimate=pl.CostEstimate(flops=10_000_000_000, bytes_accessed=8_000_000, transcendentals=0),
        name="match_first",
    )(slots, slots, taps)


LOW, HIGH = slice(0, MARGIN), slice(MARGIN + TILE, SIDE)
CORE, ALL = slice(MARGIN, MARGIN + TILE), slice(0, SIDE)
STRIPS = ((LOW, ALL), (HIGH, ALL), (CORE, LOW), (CORE, HIGH))


def place_slots(kept, slots, parts, told, canvas, base, told_sem, base_sems):
    tiles = slots.shape[0]
    tell = pltpu.make_async_copy(kept.at[pl.ds(SIDE, tiles), pl.ds(0, 128)], told, told_sem)
    tell.start()
    copies = []
    for n, (rows, cols) in enumerate(parts):
        at = pl.ds(rows.start, rows.stop - rows.start), pl.ds(cols.start, cols.stop - cols.start)
        copies.append(pltpu.make_async_copy(kept.at[at], base.at[at], base_sems.at[n]))
        copies[-1].start()
    canvas[...] = jnp.zeros_like(canvas)
    tell.wait()

    def add(t, carry):
        @pl.when(told[t, 4] > 0)
        def _():
            corner = told[t, 5].astype(i32) + MARGIN, told[t, 6].astype(i32) + MARGIN
            add_turned(canvas, slots[t], *corner)

        return carry

    lax.fori_loop(0, tiles, add, 0)
    for copy in copies:
        copy.wait()


def strips_kernel(
    kept, band, slots, rows_next, rows_last, cols_next, cols_last, told, canvas, base, told_sem, base_sems
):
    place_slots(kept, slots, STRIPS, told, canvas, base, told_sem, base_sems)
    for out in (rows_next, rows_last):
        out[MARGIN:] = jnp.zeros((META, SIDE), f32)
        out[MARGIN:, : band.shape[1]] = band[...]
    for axis, outs in (("skyy", (rows_next, rows_last)), ("skyx", (cols_next, cols_last))):
        for parity in range(2):

            @pl.when(lax.axis_index(axis) % 2 == parity)
            def _():
                for out, strip in zip(outs, (HIGH, LOW) if parity == 0 else (LOW, HIGH)):
                    rows, cols = (strip, ALL) if axis == "skyy" else (CORE, strip)
                    out[: rows.stop - rows.start] = base[rows, cols] + canvas[rows, cols]


def place_scratch(slots, parts):
    return [
        pltpu.SMEM((slots.shape[0], 128), f32),
        pltpu.VMEM((CANVAS_ROWS, CANVAS_COLS), f32),
        pltpu.VMEM((SIDE, SIDE), f32),
        pltpu.SemaphoreType.DMA,
        pltpu.SemaphoreType.DMA((parts,)),
    ]


def make_strips(kept, band, slots):
    strip = jax.ShapeDtypeStruct((MARGIN + META, SIDE), f32)
    side = jax.ShapeDtypeStruct((TILE, MARGIN), f32)
    return pl.pallas_call(
        strips_kernel,
        out_shape=(strip, strip, side, side),
        in_specs=[anywhere, vmem, vmem],
        out_specs=(vmem,) * 4,
        scratch_shapes=place_scratch(slots, len(STRIPS)),
        compiler_params=pltpu.CompilerParams(vmem_limit_bytes=20 * MIB),
        name="place_second",
    )(kept, band, slots)


def middle_kernel(kept, slots, middle, told, canvas, base, told_sem, base_sems):
    place_slots(kept, slots, ((CORE, ALL),), told, canvas, base, told_sem, base_sems)
    middle[...] = base[CORE] + canvas[CORE, :SIDE]


def make_middle(kept, slots):
    return pl.pallas_call(
        middle_kernel,
        out_shape=jax.ShapeDtypeStruct((TILE, SIDE), f32),
        in_specs=[anywhere, vmem],
        out_specs=vmem,
        scratch_shapes=place_scratch(slots, 1),
        compiler_params=pltpu.CompilerParams(vmem_limit_bytes=20 * MIB),
        cost_estimate=pl.CostEstimate(flops=400_000, bytes_accessed=4_000_000, transcendentals=0),
        name="make_middle",
    )(kept, slots)


def depth_kernel(own, rows_next, rows_last, depth, divisor):
    total = jnp.zeros((TILE, TILE), f32)
    count = own.shape[1]
    toward = jnp.where(lax.axis_index("skyy") % 2 == 0, TILE, -TILE).astype(f32)
    for about, step in ((own, 0.0), (rows_next, toward), (rows_last, -toward)):
        about = about[-META:, :count]
        place_at = lax.broadcasted_iota(i32, (TILE, count), 0).astype(f32)
        from_top = place_at - (about[0:1, :] + step)
        rows = jnp.where((from_top >= 0) & (from_top < about[2:3, :]), about[3:4, :], 0.0)
        from_left = place_at - about[1:2, :]
        cols = jnp.where((from_left >= 0) & (from_left < PW), 1.0, 0.0).astype(bf16)
        for part in split(rows):
            total += lax.dot_general(part, cols, (((1,), (1,)), ((), ())), preferred_element_type=f32)
    depth[...] = total
    divisor[...] = total + prior_weight


def make_depth(own, rows_next, rows_last):
    return pl.pallas_call(
        depth_kernel,
        out_shape=(jax.ShapeDtypeStruct((TILE, TILE), f32),) * 2,
        in_specs=[vmem] * 3,
        out_specs=(vmem, vmem),
        compiler_params=pltpu.CompilerParams(vmem_limit_bytes=16 * MIB),
        cost_estimate=pl.CostEstimate(flops=1_000_000_000, bytes_accessed=1_000_000, transcendentals=0),
        name="make_depth",
    )(own, rows_next, rows_last)


def exchange(block, axis, first):
    pairs = [(i, i + 1) for i in range(first, lax.axis_size(axis) - 1, 2)]
    return lax.ppermute(block, axis, pairs + [(j, i) for i, j in pairs])


def by_side(axis, following, preceding):
    even = lax.axis_index(axis) % 2 == 0
    return jnp.where(even, preceding, following), jnp.where(even, following, preceding)


NEAR = TILE - MARGIN


def edges_kernel(near, cols_next, cols_last, rows, out_next, out_last):
    strips = slice(0, MARGIN), slice(MARGIN + TILE, SIDE)
    for row_parity in range(2):
        for col_parity in range(2):
            here = (lax.axis_index("skyy") % 2 == row_parity) & (lax.axis_index("skyx") % 2 == col_parity)

            @pl.when(here)
            def _():
                for out, side, cols in zip(
                    (out_next, out_last), (cols_next, cols_last), strips[::-1] if col_parity == 0 else strips
                ):
                    came = rows[:MARGIN, cols]
                    if not near:
                        out[...] = (side[:MARGIN] if row_parity == 0 else side[NEAR:]) + came
                    elif row_parity == 0:
                        out[: NEAR - MARGIN] = side[MARGIN:NEAR]
                        out[NEAR - MARGIN :] = side[NEAR:] + came
                    else:
                        out[:MARGIN] = side[:MARGIN] + came
                        out[MARGIN:] = side[MARGIN:NEAR]


def make_edges(near, cols_next, cols_last, rows):
    edge = jax.ShapeDtypeStruct((NEAR if near else MARGIN, MARGIN), f32)
    return pl.pallas_call(
        functools.partial(edges_kernel, near),
        out_shape=(edge, edge),
        in_specs=[vmem] * 3,
        out_specs=(vmem, vmem),
        compiler_params=pltpu.CompilerParams(vmem_limit_bytes=12 * MIB),
        name="make_edges",
    )(cols_next, cols_last, rows)


def final_kernel(middle, rows_next, rows_last, near_next, near_last, far_next, far_last, divisor, coadd):
    core = slice(MARGIN, MARGIN + TILE)
    above, below = by_side("skyy", rows_next[:MARGIN, core], rows_last[:MARGIN, core])
    coadd[...] = middle[:, core]
    coadd[:MARGIN] += above
    coadd[NEAR:] += below
    near = by_side("skyx", near_next[...], near_last[...])
    far = by_side("skyx", far_next[...], far_last[...])
    for parity in range(2):

        @pl.when(lax.axis_index("skyy") % 2 == parity)
        def _():
            near_rows = slice(MARGIN, TILE) if parity == 0 else slice(0, NEAR)
            far_rows = slice(0, MARGIN) if parity == 0 else slice(NEAR, TILE)
            for n, cols in enumerate((slice(0, MARGIN), slice(NEAR, TILE))):
                coadd[near_rows, cols] += near[n]
                coadd[far_rows, cols] += far[n]

    coadd[...] = coadd[...] / divisor[...]


def make_coadd(*parts):
    return pl.pallas_call(
        final_kernel,
        out_shape=jax.ShapeDtypeStruct((TILE, TILE), f32),
        in_specs=[vmem] * 8,
        out_specs=vmem,
        compiler_params=pltpu.CompilerParams(vmem_limit_bytes=16 * MIB),
        name="make_coadd",
    )(*parts)


def per_device(patches, dest, row_offset, col_offset, live_rows, weight, coefficient, basis):
    tiles = lax.axis_size("skyx")
    images = patches[0]
    outgoing = pack(
        images, dest[:, :, 0], row_offset, col_offset, live_rows, weight, coefficient[0].T, tiles
    )
    arrived = lax.all_to_all(outgoing, "skyx", split_axis=0, concat_axis=0, tiled=True)
    taps = spread_taps(basis)
    second = list_second(dest[:, :, 0], tiles)
    late = match_second(second, coefficient[0].T, live_rows, weight, row_offset, col_offset, images, taps, tiles)
    late = lax.all_to_all(late, "skyx", split_axis=0, concat_axis=0, tiled=True)

    kept = match_first(arrived, taps)

    about = arrived[:, SLOT : SLOT + 5, : images.shape[0]]
    band = jnp.transpose(about, (1, 0, 2)).reshape(5, -1)
    left = band[2] + (band[0] - lax.axis_index("skyx").astype(f32)) * TILE
    own = jnp.pad(jnp.stack([band[1], left, band[3], band[4]]), ((0, META - 4), (0, 0)))

    rows_next, rows_last, cols_next, cols_last = make_strips(kept, own, late)
    rows_last = exchange(rows_last, "skyy", 1)
    rows_next = exchange(rows_next, "skyy", 0)
    edges = make_edges(True, cols_next, cols_last, rows_next)
    near_next, near_last = exchange(edges[0], "skyx", 0), exchange(edges[1], "skyx", 1)
    middle = make_middle(kept, late)
    edges = make_edges(False, cols_next, cols_last, rows_last)
    far_next, far_last = exchange(edges[0], "skyx", 0), exchange(edges[1], "skyx", 1)
    depth, divisor = make_depth(own, rows_next, rows_last)
    coadd = make_coadd(middle, rows_next, rows_last, near_next, near_last, far_next, far_last, divisor)
    return (coadd, depth)


def solution(mesh):
    in_specs = (
        P("skyy", "skyx", None, None),
        P("skyy", "skyx", None),
        P("skyy", "skyx"),
        P("skyy", "skyx"),
        P("skyy", "skyx"),
        P("skyy", "skyx"),
        P("skyy", "skyx", None),
        P(),
    )
    out_specs = (P("skyy", "skyx"), P("skyy", "skyx"))
    return jax.shard_map(
        per_device, mesh=mesh, in_specs=in_specs, out_specs=out_specs, check_vma=False
    )
```

```python
import functools

import jax
import jax.numpy as jnp
from jax import lax
from jax.experimental import pallas as pl
from jax.experimental.pallas import tpu as pltpu
from jax.sharding import PartitionSpec as P

TILE = 512
MARGIN = 128
CAP = 2
PH = 128
PW = 256
NB = 8
TAPS = 41
HALF = TAPS // 2
SIDE = TILE + 2 * MARGIN
CANVAS_ROWS = SIDE + 8
CANVAS_COLS = SIDE + 128
META = 8
HALF_COLS = PW // 2
SLOT = 2 * PH
GROUP = 4
CHUNK = 4
KEPT_ROWS = 20 * SIDE
MIB = 1024 * 1024

prior_weight = 0.5
f32 = jnp.float32
bf16 = jnp.bfloat16
i32 = jnp.int32


def whole(shape):
    return pl.BlockSpec(shape, lambda *_: (0,) * len(shape))


smem = pl.BlockSpec(memory_space=pltpu.SMEM)
vmem = pl.BlockSpec(memory_space=pltpu.VMEM)
anywhere = pl.BlockSpec(memory_space=pl.ANY)
hbm = pl.BlockSpec(memory_space=pltpu.HBM)


def split(x):
    high = x.astype(bf16)
    return high, (x - high.astype(f32)).astype(bf16)


def fill_bands(basis, down_high, down_low, across_high, across_low):
    for b in range(NB):
        taps = jnp.broadcast_to(basis[1, b : b + 1, :], (PW, PW + 128))
        table = pltpu.roll(taps, 0, 1, stride=1, stride_axis=0)[:, :PW]
        high, low = split(table)
        across_high[b * PW : (b + 1) * PW, :] = high
        across_low[b * PW : (b + 1) * PW, :] = low
        taps = jnp.broadcast_to(basis[0, b : b + 1, :], (PH, PW + 128))
        table = pltpu.roll(taps, 0, 1, stride=1, stride_axis=0)[:, :PH]
        high, low = split(table)
        down_high[b * PH : (b + 1) * PH, :PH] = high
        down_high[b * PH : (b + 1) * PH, PH:] = high
        down_low[b * PH : (b + 1) * PH, :] = low


BANDS = [
    pltpu.VMEM((NB * PH, 2 * PH), bf16),
    pltpu.VMEM((NB * PH, PH), bf16),
    pltpu.VMEM((NB * PW, PW), bf16),
    pltpu.VMEM((NB * PW, PW), bf16),
]


def spread_taps(basis):
    taps = jnp.stack([basis[0][:, ::-1], basis[1]])
    gap = jnp.zeros((2, NB, PW + 128 - TAPS), f32)
    return jnp.concatenate([taps[:, :, HALF:], gap, taps[:, :, :HALF]], axis=2)


def assign_slots(dest, slots):
    tiles = slots.shape[1]
    for t in range(tiles):
        slots[0, t] = -1
        slots[1, t] = -1
    for k in range(dest.shape[1]):
        t = dest[0, k]
        rank = jnp.where(slots[0, t] >= 0, 1, 0)
        slots[rank, t] = k


def pack_kernel(*refs):
    given, patches, out = refs[:6], refs[6], refs[7]
    scalars, vectors = refs[8:14], refs[14:19]
    slots, held, meta, small_sems, in_sems, out_sems, meta_sem = refs[19:]
    dest, row_offset, col_offset, live, weight, coefs = scalars
    count = patches.shape[0]
    tiles = out.shape[0]

    def give(k, t, half):
        source = held.at[k, :, pl.ds(half * HALF_COLS, HALF_COLS)]
        return pltpu.make_async_copy(source, out.at[t, pl.ds(half * PH, PH)], out_sems.at[k, half])

    small = [
        pltpu.make_async_copy(source, target, small_sems.at[n])
        for n, (source, target) in enumerate(zip(given + given[:5], scalars + vectors))
    ]
    for copy in small:
        copy.start()
    brings = []
    for n in range(count // CHUNK):
        part = pl.ds(n * CHUNK, CHUNK)
        brings.append(pltpu.make_async_copy(patches.at[part], held.at[part], in_sems.at[n]))
        brings[-1].start()
    meta[...] = jnp.zeros_like(meta)
    for copy in small:
        copy.wait()

    assign_slots(dest, slots)
    for k in range(count):
        if k % CHUNK == 0:
            brings[k // CHUNK].wait()
        t = dest[0, k]

        @pl.when(slots[0, t] == k)
        def _():
            give(k, t, 0).start()
            give(k, t, 1).start()

    for row, values in enumerate(vectors):
        line = values[...].astype(f32)
        for t in range(tiles):
            meta[t, row : row + 1, 0:count] = line

    lane = lax.broadcasted_iota(i32, (1, 128), 1)

    def describe(t, carry):
        first = slots[0, t]
        k = jnp.maximum(first, 0)
        late = slots[1, t]
        j = jnp.maximum(late, 0)
        numbers = (
            jnp.where(first >= 0, 1, 0), row_offset[0, k], col_offset[0, k], live[0, k],
            jnp.where(late >= 0, 1, 0), row_offset[0, j], col_offset[0, j], live[0, j],
        )
        line = jnp.zeros((1, 128), i32)
        for place, number in enumerate(numbers):
            line = jnp.where(lane == place, number, line)
        meta[t, 6:7, 0:128] = line.astype(f32)
        line = jnp.zeros((1, 128), f32)
        for b in range(NB):
            line = jnp.where(lane == b, coefs[b, k] * weight[0, k], line)
        meta[t, 5:6, 0:128] = line
        return carry

    lax.fori_loop(0, tiles, describe, 0, unroll=4)
    about = pltpu.make_async_copy(meta, out.at[:, pl.ds(SLOT, META)], meta_sem)
    about.start()

    for k in range(count):
        t = dest[0, k]

        @pl.when(slots[0, t] == k)
        def _():
            give(k, t, 0).wait()
            give(k, t, 1).wait()

    about.wait()


def pack(patches, dest, row_offset, col_offset, live_rows, weight, coefficient, tiles):
    given = (dest, row_offset, col_offset, live_rows, weight, coefficient)
    return pl.pallas_call(
        pack_kernel,
        out_shape=jax.ShapeDtypeStruct((tiles, SLOT + META, HALF_COLS), f32),
        in_specs=[anywhere] * 7,
        out_specs=anywhere,
        scratch_shapes=[pltpu.SMEM(x.shape, x.dtype) for x in given]
        + [pltpu.VMEM(x.shape, x.dtype) for x in given[:5]]
        + [
            pltpu.SMEM((CAP, tiles), i32),
            pltpu.VMEM(patches.shape, f32),
            pltpu.VMEM((tiles, META, HALF_COLS), f32),
            pltpu.SemaphoreType.DMA((11,)),
            pltpu.SemaphoreType.DMA((patches.shape[0] // CHUNK,)),
            pltpu.SemaphoreType.DMA((patches.shape[0], 2)),
            pltpu.SemaphoreType.DMA,
        ],
        compiler_params=pltpu.CompilerParams(vmem_limit_bytes=62 * MIB),
        name="pack",
    )(*given, patches)


def list_kernel(dest, second, slots):
    tiles = slots.shape[1]
    assign_slots(dest, slots)
    for j in range(tiles):
        second[0, j] = 0
        second[1, j] = 0

    def note(t, n):
        k = slots[1, t]

        @pl.when(k >= 0)
        def _():
            second[0, n] = k
            second[1, n] = t

        return n + jnp.where(k >= 0, 1, 0)

    number = lax.fori_loop(0, tiles, note, 0)
    last = jnp.maximum(number - 1, 0)

    def repeat_last(j, carry):
        second[0, j] = second[0, last]
        second[1, j] = second[1, last]
        return carry

    lax.fori_loop(number, tiles, repeat_last, 0)
    for j in range(tiles):
        second[2, j] = number


def list_second(dest, tiles):
    return pl.pallas_call(
        list_kernel,
        out_shape=jax.ShapeDtypeStruct((3, tiles), i32),
        in_specs=[smem],
        out_specs=smem,
        scratch_shapes=[pltpu.SMEM((CAP, tiles), i32)],
        name="list_second",
    )(dest)


def match(images, coefs, terms, down_high, down_low, across_high, across_low):
    middle = PH * len(images)
    for g, (image, scales) in enumerate(zip(images, coefs)):
        high, low = split(image)
        both = jnp.concatenate([high, low], axis=0)
        rows = slice(g * PH, (g + 1) * PH)
        low_rows = slice(middle + g * PH, middle + (g + 1) * PH)
        for b in range(NB):
            taps = slice(b * PH, (b + 1) * PH)
            cols = slice(b * PW, (b + 1) * PW)
            downward = jnp.dot(down_high[taps], both, preferred_element_type=f32)
            downward += jnp.dot(down_low[taps], high, preferred_element_type=f32)
            terms[rows, cols], terms[low_rows, cols] = split(downward * scales[b])
    wide = jnp.dot(terms[...], across_high[...], preferred_element_type=f32)
    fine = jnp.dot(terms[:middle], across_low[...], preferred_element_type=f32)
    total = wide[:middle] + wide[middle:] + fine
    return [total[g * PH : (g + 1) * PH] for g in range(len(images))]


def live_mask(live):
    return lax.broadcasted_iota(i32, (PH, PW), 0) < live


def second_kernel(second, coefs, live, weight, row_offset, col_offset, patch, taps, out, terms, *bands):
    j = pl.program_id(0)

    @pl.when(j == 0)
    def _():
        fill_bands(taps, *bands)

    @pl.when(j < second[2, 0])
    def _():
        k = second[0, j]
        mask = live_mask(live[0, k])
        scaled = [coefs[b, k] * weight[0, k] for b in range(NB)]
        image = jnp.where(mask, patch[0], 0.0)
        (matched,) = match([image], [scaled], terms, *bands)
        out[0] = turn(jnp.where(mask, matched, 0.0), row_offset[0, k] + MARGIN, col_offset[0, k] + MARGIN)


def match_second(second, coefficient, live_rows, weight, row_offset, col_offset, patches, taps, tiles):
    steps = patches.shape[0] // CAP
    return pl.pallas_call(
        second_kernel,
        out_shape=jax.ShapeDtypeStruct((tiles, PH, PW), f32),
        grid_spec=pltpu.PrefetchScalarGridSpec(
            num_scalar_prefetch=1,
            grid=(steps,),
            in_specs=[smem] * 5
            + [pl.BlockSpec((1, PH, PW), lambda j, second: (second[0, j], 0, 0))]
            + [whole((2, NB, PW + 128))],
            out_specs=pl.BlockSpec((1, PH, PW), lambda j, second: (second[1, j], 0, 0)),
            scratch_shapes=[pltpu.VMEM((2 * PH, NB * PW), bf16)] + BANDS,
        ),
        compiler_params=pltpu.CompilerParams(vmem_limit_bytes=24 * MIB),
        cost_estimate=pl.CostEstimate(flops=5_000_000_000, bytes_accessed=6_000_000, transcendentals=0),
        name="match_second",
    )(second, coefficient, live_rows, weight, row_offset, col_offset, patches, taps)


def turn(piece, top, left):
    down = top % 8
    right = left % 128
    tiles = pltpu.roll(piece.reshape(PH // 8, 8, PW), down, 1)
    before = jnp.concatenate([tiles[-1:], tiles[:-1]], axis=0)
    wrapped = lax.broadcasted_iota(i32, tiles.shape, 1) < down
    piece = jnp.where(wrapped, before, tiles).reshape(PH, PW)
    near = pltpu.roll(piece[:, :128], right, 1)
    far = pltpu.roll(piece[:, 128:], right, 1)
    wrapped = lax.broadcasted_iota(i32, near.shape, 1) < right
    return jnp.concatenate([jnp.where(wrapped, far, near), jnp.where(wrapped, near, far)], axis=1)


def add_turned(canvas, piece, top, left):
    down = top % 8
    right = left % 128
    row = pl.multiple_of(top - down, 8)
    col = pl.multiple_of(left - right, 128)
    near = piece[:, :128]
    wrapped = lax.broadcasted_iota(i32, near.shape, 1) < right
    columns = (jnp.where(wrapped, 0.0, near), piece[:, 128:], jnp.where(wrapped, near, 0.0))
    over = lax.broadcasted_iota(i32, (8, 128), 0) < down
    for place, part in enumerate(columns):
        at = pl.ds(pl.multiple_of(col + 128 * place, 128), 128)
        canvas[pl.ds(row, 8), at] += jnp.where(over, 0.0, part[:8])
        canvas[pl.ds(pl.multiple_of(row + 8, 8), PH - 8), at] += part[8:]
        canvas[pl.ds(pl.multiple_of(row + PH, 8), 8), at] += jnp.where(over, part[:8], 0.0)


def first_kernel(slots, group, taps, out, canvas, about, numbers, lines, sem, out_sem, terms, *bands):
    step = pl.program_id(0)
    tiles = slots.shape[0]
    told = pltpu.make_async_copy(slots.at[:, pl.ds(SLOT, META)], about, sem)

    @pl.when(step == 0)
    def _():
        told.start()
        fill_bands(taps, *bands)
        canvas[...] = jnp.zeros_like(canvas)

    images, coefs, masks = [], [], []
    for g in range(GROUP):
        lines[pl.ds(step * GROUP + g, 1), :] = group[g, SLOT + 6 : SLOT + 7, :]
        line = group[g, SLOT + 6 : SLOT + 7, 0:8]
        rows = jnp.broadcast_to(line[:, 3:4] * line[:, 0:1], (PH, PW)).astype(i32)
        mask = live_mask(rows)
        masks.append(mask)
        image = jnp.concatenate([group[g, :PH, :], group[g, PH:SLOT, :]], axis=1)
        images.append(jnp.where(mask, image, 0.0))
        line = group[g, SLOT + 5 : SLOT + 6, 0:NB]
        coefs.append([line[:, b : b + 1] for b in range(NB)])
    matched = match(images, coefs, terms, *bands)

    @pl.when(step == 0)
    def _():
        told.wait()

        def tell(t, carry):
            for place in range(8):
                numbers[t, place] = about[t, 6, place].astype(i32)
            return carry

        lax.fori_loop(0, tiles, tell, 0)

    for g, (mask, image) in enumerate(zip(masks, matched)):
        t = step * GROUP + g
        corner = numbers[t, 1] + MARGIN, numbers[t, 2] + MARGIN
        add_turned(canvas, turn(jnp.where(mask, image, 0.0), *corner), *corner)

    @pl.when(step == pl.num_programs(0) - 1)
    def _():
        parts = (canvas.at[pl.ds(0, SIDE), pl.ds(0, SIDE)], lines)
        places = (out.at[pl.ds(0, SIDE)], out.at[pl.ds(SIDE, tiles), pl.ds(0, 128)])
        copies = [pltpu.make_async_copy(part, at, out_sem.at[n]) for n, (part, at) in enumerate(zip(parts, places))]
        for copy in copies:
            copy.start()
        for copy in copies:
            copy.wait()


def match_first(slots, taps):
    tiles = slots.shape[0]
    return pl.pallas_call(
        first_kernel,
        out_shape=jax.ShapeDtypeStruct((KEPT_ROWS, SIDE), f32),
        grid=(tiles // GROUP,),
        in_specs=[
            anywhere,
            pl.BlockSpec((GROUP, SLOT + META, HALF_COLS), lambda s: (s, 0, 0)),
            whole((2, NB, PW + 128)),
        ],
        out_specs=anywhere,
        scratch_shapes=[
            pltpu.VMEM((CANVAS_ROWS, CANVAS_COLS), f32),
            pltpu.SMEM((tiles, META, 128), f32),
            pltpu.SMEM((tiles, 8), i32),
            pltpu.VMEM((tiles, 128), f32),
            pltpu.SemaphoreType.DMA,
            pltpu.SemaphoreType.DMA((2,)),
            pltpu.VMEM((2 * GROUP * PH, NB * PW), bf16),
        ]
        + BANDS,
        compiler_params=pltpu.CompilerParams(vmem_limit_bytes=61 * MIB),
        cost_estimate=pl.CostEstimate(flops=10_000_000_000, bytes_accessed=8_000_000, transcendentals=0),
        name="match_first",
    )(slots, slots, taps)


LOW, HIGH = slice(0, MARGIN), slice(MARGIN + TILE, SIDE)
CORE, ALL = slice(MARGIN, MARGIN + TILE), slice(0, SIDE)
STRIPS = ((LOW, ALL), (HIGH, ALL), (CORE, LOW), (CORE, HIGH))


def place_slots(kept, slots, parts, told, canvas, base, told_sem, base_sems):
    tiles = slots.shape[0]
    tell = pltpu.make_async_copy(kept.at[pl.ds(SIDE, tiles), pl.ds(0, 128)], told, told_sem)
    tell.start()
    copies = []
    for n, (rows, cols) in enumerate(parts):
        at = pl.ds(rows.start, rows.stop - rows.start), pl.ds(cols.start, cols.stop - cols.start)
        copies.append(pltpu.make_async_copy(kept.at[at], base.at[at], base_sems.at[n]))
        copies[-1].start()
    canvas[...] = jnp.zeros_like(canvas)
    tell.wait()

    def add(t, carry):
        @pl.when(told[t, 4] > 0)
        def _():
            corner = told[t, 5].astype(i32) + MARGIN, told[t, 6].astype(i32) + MARGIN
            add_turned(canvas, slots[t], *corner)

        return carry

    lax.fori_loop(0, tiles, add, 0)
    for copy in copies:
        copy.wait()


def strips_kernel(
    kept, band, slots, rows_next, rows_last, cols_next, cols_last, told, canvas, base, told_sem, base_sems
):
    place_slots(kept, slots, STRIPS, told, canvas, base, told_sem, base_sems)
    for out in (rows_next, rows_last):
        out[MARGIN:] = jnp.zeros((META, SIDE), f32)
        out[MARGIN:, : band.shape[1]] = band[...]
    for axis, outs in (("skyy", (rows_next, rows_last)), ("skyx", (cols_next, cols_last))):
        for parity in range(2):

            @pl.when(lax.axis_index(axis) % 2 == parity)
            def _():
                for out, strip in zip(outs, (HIGH, LOW) if parity == 0 else (LOW, HIGH)):
                    rows, cols = (strip, ALL) if axis == "skyy" else (CORE, strip)
                    out[: rows.stop - rows.start] = base[rows, cols] + canvas[rows, cols]


def place_scratch(slots, parts):
    return [
        pltpu.SMEM((slots.shape[0], 128), f32),
        pltpu.VMEM((CANVAS_ROWS, CANVAS_COLS), f32),
        pltpu.VMEM((SIDE, SIDE), f32),
        pltpu.SemaphoreType.DMA,
        pltpu.SemaphoreType.DMA((parts,)),
    ]


def make_strips(kept, band, slots):
    strip = jax.ShapeDtypeStruct((MARGIN + META, SIDE), f32)
    side = jax.ShapeDtypeStruct((TILE, MARGIN), f32)
    return pl.pallas_call(
        strips_kernel,
        out_shape=(strip, strip, side, side),
        in_specs=[anywhere, vmem, vmem],
        out_specs=(vmem,) * 4,
        scratch_shapes=place_scratch(slots, len(STRIPS)),
        compiler_params=pltpu.CompilerParams(vmem_limit_bytes=20 * MIB),
        name="place_second",
    )(kept, band, slots)


def middle_kernel(kept, slots, middle, told, canvas, base, told_sem, base_sems):
    place_slots(kept, slots, ((CORE, ALL),), told, canvas, base, told_sem, base_sems)
    middle[...] = base[CORE] + canvas[CORE, :SIDE]


def make_middle(kept, slots):
    return pl.pallas_call(
        middle_kernel,
        out_shape=jax.ShapeDtypeStruct((TILE, SIDE), f32),
        in_specs=[anywhere, vmem],
        out_specs=vmem,
        scratch_shapes=place_scratch(slots, 1),
        compiler_params=pltpu.CompilerParams(vmem_limit_bytes=20 * MIB),
        cost_estimate=pl.CostEstimate(flops=400_000, bytes_accessed=4_000_000, transcendentals=0),
        name="make_middle",
    )(kept, slots)


def depth_kernel(own, rows_next, rows_last, depth, divisor):
    total = jnp.zeros((TILE, TILE), f32)
    count = own.shape[1]
    toward = jnp.where(lax.axis_index("skyy") % 2 == 0, TILE, -TILE).astype(f32)
    for about, step in ((own, 0.0), (rows_next, toward), (rows_last, -toward)):
        about = about[-META:, :count]
        place_at = lax.broadcasted_iota(i32, (TILE, count), 0).astype(f32)
        from_top = place_at - (about[0:1, :] + step)
        rows = jnp.where((from_top >= 0) & (from_top < about[2:3, :]), about[3:4, :], 0.0)
        from_left = place_at - about[1:2, :]
        cols = jnp.where((from_left >= 0) & (from_left < PW), 1.0, 0.0).astype(bf16)
        for part in split(rows):
            total += lax.dot_general(part, cols, (((1,), (1,)), ((), ())), preferred_element_type=f32)
    depth[...] = total
    divisor[...] = total + prior_weight


def make_depth(own, rows_next, rows_last):
    return pl.pallas_call(
        depth_kernel,
        out_shape=(jax.ShapeDtypeStruct((TILE, TILE), f32),) * 2,
        in_specs=[vmem] * 3,
        out_specs=(vmem, vmem),
        compiler_params=pltpu.CompilerParams(vmem_limit_bytes=16 * MIB),
        cost_estimate=pl.CostEstimate(flops=1_000_000_000, bytes_accessed=1_000_000, transcendentals=0),
        name="make_depth",
    )(own, rows_next, rows_last)


def exchange(block, axis, first):
    pairs = [(i, i + 1) for i in range(first, lax.axis_size(axis) - 1, 2)]
    return lax.ppermute(block, axis, pairs + [(j, i) for i, j in pairs])


def by_side(axis, following, preceding):
    even = lax.axis_index(axis) % 2 == 0
    return jnp.where(even, preceding, following), jnp.where(even, following, preceding)


NEAR = TILE - MARGIN


def edges_kernel(near, cols_next, cols_last, rows, out_next, out_last):
    strips = slice(0, MARGIN), slice(MARGIN + TILE, SIDE)
    for row_parity in range(2):
        for col_parity in range(2):
            here = (lax.axis_index("skyy") % 2 == row_parity) & (lax.axis_index("skyx") % 2 == col_parity)

            @pl.when(here)
            def _():
                for out, side, cols in zip(
                    (out_next, out_last), (cols_next, cols_last), strips[::-1] if col_parity == 0 else strips
                ):
                    came = rows[:MARGIN, cols]
                    if not near:
                        out[...] = (side[:MARGIN] if row_parity == 0 else side[NEAR:]) + came
                    elif row_parity == 0:
                        out[: NEAR - MARGIN] = side[MARGIN:NEAR]
                        out[NEAR - MARGIN :] = side[NEAR:] + came
                    else:
                        out[:MARGIN] = side[:MARGIN] + came
                        out[MARGIN:] = side[MARGIN:NEAR]


def make_edges(near, cols_next, cols_last, rows):
    edge = jax.ShapeDtypeStruct((NEAR if near else MARGIN, MARGIN), f32)
    return pl.pallas_call(
        functools.partial(edges_kernel, near),
        out_shape=(edge, edge),
        in_specs=[vmem] * 3,
        out_specs=(vmem, vmem),
        compiler_params=pltpu.CompilerParams(vmem_limit_bytes=12 * MIB),
        name="make_edges",
    )(cols_next, cols_last, rows)


SIDES = slice(0, MARGIN), slice(NEAR, TILE)


def with_rows(total, middle, rows_next, rows_last, cols):
    at = slice(MARGIN + cols.start, MARGIN + cols.stop)
    above, below = by_side("skyy", rows_next[:MARGIN, at], rows_last[:MARGIN, at])
    total[:, cols] = middle[:, at]
    total[:MARGIN, cols] += above
    total[NEAR:, cols] += below


def inside_kernel(middle, rows_next, rows_last, divisor, out, total, sem):
    cols = slice(MARGIN, NEAR)
    with_rows(total, middle, rows_next, rows_last, cols)
    total[:, cols] = total[:, cols] / divisor[:, cols]
    at = pl.ds(MARGIN, NEAR - MARGIN)
    copy = pltpu.make_async_copy(total.at[:, at], out.at[:, at], sem)
    copy.start()
    copy.wait()


def make_inside(*parts):
    return pl.pallas_call(
        inside_kernel,
        out_shape=jax.ShapeDtypeStruct((TILE, TILE), f32),
        in_specs=[vmem] * 4,
        out_specs=anywhere,
        scratch_shapes=[pltpu.VMEM((TILE, TILE), f32), pltpu.SemaphoreType.DMA],
        compiler_params=pltpu.CompilerParams(vmem_limit_bytes=16 * MIB),
        name="make_inside",
    )(*parts)


def final_kernel(
    inside, middle, rows_next, rows_last, near_next, near_last, far_next, far_last, divisor, out, total, sems
):
    near = by_side("skyx", near_next[...], near_last[...])
    far = by_side("skyx", far_next[...], far_last[...])
    copies = []
    for n, cols in enumerate(SIDES):
        with_rows(total, middle, rows_next, rows_last, cols)
        for parity in range(2):

            @pl.when(lax.axis_index("skyy") % 2 == parity)
            def _():
                near_rows = slice(MARGIN, TILE) if parity == 0 else slice(0, NEAR)
                far_rows = slice(0, MARGIN) if parity == 0 else slice(NEAR, TILE)
                total[near_rows, cols] += near[n]
                total[far_rows, cols] += far[n]

        total[:, cols] = total[:, cols] / divisor[:, cols]
        at = pl.ds(cols.start, MARGIN)
        copies.append(pltpu.make_async_copy(total.at[:, at], out.at[:, at], sems.at[n]))
        copies[-1].start()
    for copy in copies:
        copy.wait()


def make_coadd(*parts):
    return pl.pallas_call(
        final_kernel,
        out_shape=jax.ShapeDtypeStruct((TILE, TILE), f32),
        in_specs=[anywhere] + [vmem] * 8,
        out_specs=anywhere,
        scratch_shapes=[pltpu.VMEM((TILE, TILE), f32), pltpu.SemaphoreType.DMA((2,))],
        input_output_aliases={0: 0},
        compiler_params=pltpu.CompilerParams(vmem_limit_bytes=16 * MIB),
        name="make_coadd",
    )(*parts)


def per_device(patches, dest, row_offset, col_offset, live_rows, weight, coefficient, basis):
    tiles = lax.axis_size("skyx")
    images = patches[0]
    outgoing = pack(
        images, dest[:, :, 0], row_offset, col_offset, live_rows, weight, coefficient[0].T, tiles
    )
    arrived = lax.all_to_all(outgoing, "skyx", split_axis=0, concat_axis=0, tiled=True)
    taps = spread_taps(basis)
    second = list_second(dest[:, :, 0], tiles)
    late = match_second(second, coefficient[0].T, live_rows, weight, row_offset, col_offset, images, taps, tiles)
    late = lax.all_to_all(late, "skyx", split_axis=0, concat_axis=0, tiled=True)

    kept = match_first(arrived, taps)

    about = arrived[:, SLOT : SLOT + 5, : images.shape[0]]
    band = jnp.transpose(about, (1, 0, 2)).reshape(5, -1)
    left = band[2] + (band[0] - lax.axis_index("skyx").astype(f32)) * TILE
    own = jnp.pad(jnp.stack([band[1], left, band[3], band[4]]), ((0, META - 4), (0, 0)))

    rows_next, rows_last, cols_next, cols_last = make_strips(kept, own, late)
    rows_last = exchange(rows_last, "skyy", 1)
    rows_next = exchange(rows_next, "skyy", 0)
    edges = make_edges(True, cols_next, cols_last, rows_next)
    near_next, near_last = exchange(edges[0], "skyx", 0), exchange(edges[1], "skyx", 1)
    middle = make_middle(kept, late)
    edges = make_edges(False, cols_next, cols_last, rows_last)
    far_next, far_last = exchange(edges[0], "skyx", 0), exchange(edges[1], "skyx", 1)
    depth, divisor = make_depth(own, rows_next, rows_last)
    inside = make_inside(middle, rows_next, rows_last, divisor)
    coadd = make_coadd(inside, middle, rows_next, rows_last, near_next, near_last, far_next, far_last, divisor)
    return (coadd, depth)


def solution(mesh):
    in_specs = (
        P("skyy", "skyx", None, None),
        P("skyy", "skyx", None),
        P("skyy", "skyx"),
        P("skyy", "skyx"),
        P("skyy", "skyx"),
        P("skyy", "skyx"),
        P("skyy", "skyx", None),
        P(),
    )
    out_specs = (P("skyy", "skyx"), P("skyy", "skyx"))
    return jax.shard_map(
        per_device, mesh=mesh, in_specs=in_specs, out_specs=out_specs, check_vma=False
    )
```

```python
import functools

import jax
import jax.numpy as jnp
from jax import lax
from jax.experimental import pallas as pl
from jax.experimental.pallas import tpu as pltpu
from jax.sharding import PartitionSpec as P

TILE = 512
MARGIN = 128
CAP = 2
PH = 128
PW = 256
NB = 8
TAPS = 41
HALF = TAPS // 2
SIDE = TILE + 2 * MARGIN
CANVAS_ROWS = SIDE + 8
CANVAS_COLS = SIDE + 128
META = 8
HALF_COLS = PW // 2
SLOT = 2 * PH
GROUP = 4
CHUNK = 4
KEPT_ROWS = 20 * SIDE
MIB = 1024 * 1024

prior_weight = 0.5
f32 = jnp.float32
bf16 = jnp.bfloat16
i32 = jnp.int32


def whole(shape):
    return pl.BlockSpec(shape, lambda *_: (0,) * len(shape))


smem = pl.BlockSpec(memory_space=pltpu.SMEM)
vmem = pl.BlockSpec(memory_space=pltpu.VMEM)
anywhere = pl.BlockSpec(memory_space=pl.ANY)
hbm = pl.BlockSpec(memory_space=pltpu.HBM)


def split(x):
    high = x.astype(bf16)
    return high, (x - high.astype(f32)).astype(bf16)


def fill_bands(basis, down_high, down_low, across_high, across_low):
    for b in range(NB):
        taps = jnp.broadcast_to(basis[1, b : b + 1, :], (PW, PW + 128))
        table = pltpu.roll(taps, 0, 1, stride=1, stride_axis=0)[:, :PW]
        high, low = split(table)
        across_high[b * PW : (b + 1) * PW, :] = high
        across_low[b * PW : (b + 1) * PW, :] = low
        taps = jnp.broadcast_to(basis[0, b : b + 1, :], (PH, PW + 128))
        table = pltpu.roll(taps, 0, 1, stride=1, stride_axis=0)[:, :PH]
        high, low = split(table)
        down_high[b * PH : (b + 1) * PH, :PH] = high
        down_high[b * PH : (b + 1) * PH, PH:] = high
        down_low[b * PH : (b + 1) * PH, :] = low


BANDS = [
    pltpu.VMEM((NB * PH, 2 * PH), bf16),
    pltpu.VMEM((NB * PH, PH), bf16),
    pltpu.VMEM((NB * PW, PW), bf16),
    pltpu.VMEM((NB * PW, PW), bf16),
]


def spread_taps(basis):
    taps = jnp.stack([basis[0][:, ::-1], basis[1]])
    gap = jnp.zeros((2, NB, PW + 128 - TAPS), f32)
    return jnp.concatenate([taps[:, :, HALF:], gap, taps[:, :, :HALF]], axis=2)


def assign_slots(dest, slots):
    tiles = slots.shape[1]
    for t in range(tiles):
        slots[0, t] = -1
        slots[1, t] = -1
    for k in range(dest.shape[1]):
        t = dest[0, k]
        rank = jnp.where(slots[0, t] >= 0, 1, 0)
        slots[rank, t] = k


def pack_kernel(*refs):
    given, patches, out = refs[:6], refs[6], refs[7]
    scalars, vectors = refs[8:14], refs[14:19]
    slots, held, meta, small_sems, in_sems, out_sems, meta_sem = refs[19:]
    dest, row_offset, col_offset, live, weight, coefs = scalars
    count = patches.shape[0]
    tiles = out.shape[0]

    def give(k, t, half):
        source = held.at[k, :, pl.ds(half * HALF_COLS, HALF_COLS)]
        return pltpu.make_async_copy(source, out.at[t, pl.ds(half * PH, PH)], out_sems.at[k, half])

    small = [
        pltpu.make_async_copy(source, target, small_sems.at[n])
        for n, (source, target) in enumerate(zip(given + given[:5], scalars + vectors))
    ]
    for copy in small:
        copy.start()
    brings = []
    for n in range(count // CHUNK):
        part = pl.ds(n * CHUNK, CHUNK)
        brings.append(pltpu.make_async_copy(patches.at[part], held.at[part], in_sems.at[n]))
        brings[-1].start()
    meta[...] = jnp.zeros_like(meta)
    for copy in small:
        copy.wait()

    assign_slots(dest, slots)
    for k in range(count):
        if k % CHUNK == 0:
            brings[k // CHUNK].wait()
        t = dest[0, k]

        @pl.when(slots[0, t] == k)
        def _():
            give(k, t, 0).start()
            give(k, t, 1).start()

    for row, values in enumerate(vectors):
        line = values[...].astype(f32)
        for t in range(tiles):
            meta[t, row : row + 1, 0:count] = line

    lane = lax.broadcasted_iota(i32, (1, 128), 1)

    def describe(t, carry):
        first = slots[0, t]
        k = jnp.maximum(first, 0)
        late = slots[1, t]
        j = jnp.maximum(late, 0)
        numbers = (
            jnp.where(first >= 0, 1, 0), row_offset[0, k], col_offset[0, k], live[0, k],
            jnp.where(late >= 0, 1, 0), row_offset[0, j], col_offset[0, j], live[0, j],
        )
        line = jnp.zeros((1, 128), i32)
        for place, number in enumerate(numbers):
            line = jnp.where(lane == place, number, line)
        meta[t, 6:7, 0:128] = line.astype(f32)
        line = jnp.zeros((1, 128), f32)
        for b in range(NB):
            line = jnp.where(lane == b, coefs[b, k] * weight[0, k], line)
        meta[t, 5:6, 0:128] = line
        return carry

    lax.fori_loop(0, tiles, describe, 0, unroll=4)
    about = pltpu.make_async_copy(meta, out.at[:, pl.ds(SLOT, META)], meta_sem)
    about.start()

    for k in range(count):
        t = dest[0, k]

        @pl.when(slots[0, t] == k)
        def _():
            give(k, t, 0).wait()
            give(k, t, 1).wait()

    about.wait()


def pack(patches, dest, row_offset, col_offset, live_rows, weight, coefficient, tiles):
    given = (dest, row_offset, col_offset, live_rows, weight, coefficient)
    return pl.pallas_call(
        pack_kernel,
        out_shape=jax.ShapeDtypeStruct((tiles, SLOT + META, HALF_COLS), f32),
        in_specs=[anywhere] * 7,
        out_specs=anywhere,
        scratch_shapes=[pltpu.SMEM(x.shape, x.dtype) for x in given]
        + [pltpu.VMEM(x.shape, x.dtype) for x in given[:5]]
        + [
            pltpu.SMEM((CAP, tiles), i32),
            pltpu.VMEM(patches.shape, f32),
            pltpu.VMEM((tiles, META, HALF_COLS), f32),
            pltpu.SemaphoreType.DMA((11,)),
            pltpu.SemaphoreType.DMA((patches.shape[0] // CHUNK,)),
            pltpu.SemaphoreType.DMA((patches.shape[0], 2)),
            pltpu.SemaphoreType.DMA,
        ],
        compiler_params=pltpu.CompilerParams(vmem_limit_bytes=62 * MIB),
        name="pack",
    )(*given, patches)


def list_kernel(dest, second, slots):
    tiles = slots.shape[1]
    assign_slots(dest, slots)
    for j in range(tiles):
        second[0, j] = 0
        second[1, j] = 0

    def note(t, n):
        k = slots[1, t]

        @pl.when(k >= 0)
        def _():
            second[0, n] = k
            second[1, n] = t

        return n + jnp.where(k >= 0, 1, 0)

    number = lax.fori_loop(0, tiles, note, 0)
    last = jnp.maximum(number - 1, 0)

    def repeat_last(j, carry):
        second[0, j] = second[0, last]
        second[1, j] = second[1, last]
        return carry

    lax.fori_loop(number, tiles, repeat_last, 0)
    for j in range(tiles):
        second[2, j] = number


def list_second(dest, tiles):
    return pl.pallas_call(
        list_kernel,
        out_shape=jax.ShapeDtypeStruct((3, tiles), i32),
        in_specs=[smem],
        out_specs=smem,
        scratch_shapes=[pltpu.SMEM((CAP, tiles), i32)],
        name="list_second",
    )(dest)


def match(images, coefs, terms, down_high, down_low, across_high, across_low):
    middle = PH * len(images)
    for g, (image, scales) in enumerate(zip(images, coefs)):
        high, low = split(image)
        both = jnp.concatenate([high, low], axis=0)
        rows = slice(g * PH, (g + 1) * PH)
        low_rows = slice(middle + g * PH, middle + (g + 1) * PH)
        for b in range(NB):
            taps = slice(b * PH, (b + 1) * PH)
            cols = slice(b * PW, (b + 1) * PW)
            downward = jnp.dot(down_high[taps], both, preferred_element_type=f32)
            downward += jnp.dot(down_low[taps], high, preferred_element_type=f32)
            terms[rows, cols], terms[low_rows, cols] = split(downward * scales[b])
    wide = jnp.dot(terms[...], across_high[...], preferred_element_type=f32)
    fine = jnp.dot(terms[:middle], across_low[...], preferred_element_type=f32)
    total = wide[:middle] + wide[middle:] + fine
    return [total[g * PH : (g + 1) * PH] for g in range(len(images))]


def live_mask(live):
    return lax.broadcasted_iota(i32, (PH, PW), 0) < live


def second_kernel(second, coefs, live, weight, row_offset, col_offset, patch, taps, out, terms, *bands):
    j = pl.program_id(0)

    @pl.when(j == 0)
    def _():
        fill_bands(taps, *bands)

    @pl.when(j < second[2, 0])
    def _():
        k = second[0, j]
        mask = live_mask(live[0, k])
        scaled = [coefs[b, k] * weight[0, k] for b in range(NB)]
        image = jnp.where(mask, patch[0], 0.0)
        (matched,) = match([image], [scaled], terms, *bands)
        out[0] = turn(jnp.where(mask, matched, 0.0), row_offset[0, k] + MARGIN, col_offset[0, k] + MARGIN)


def match_second(second, coefficient, live_rows, weight, row_offset, col_offset, patches, taps, tiles):
    steps = patches.shape[0] // CAP
    return pl.pallas_call(
        second_kernel,
        out_shape=jax.ShapeDtypeStruct((tiles, PH, PW), f32),
        grid_spec=pltpu.PrefetchScalarGridSpec(
            num_scalar_prefetch=1,
            grid=(steps,),
            in_specs=[smem] * 5
            + [pl.BlockSpec((1, PH, PW), lambda j, second: (second[0, j], 0, 0))]
            + [whole((2, NB, PW + 128))],
            out_specs=pl.BlockSpec((1, PH, PW), lambda j, second: (second[1, j], 0, 0)),
            scratch_shapes=[pltpu.VMEM((2 * PH, NB * PW), bf16)] + BANDS,
        ),
        compiler_params=pltpu.CompilerParams(vmem_limit_bytes=24 * MIB),
        cost_estimate=pl.CostEstimate(flops=5_000_000_000, bytes_accessed=6_000_000, transcendentals=0),
        name="match_second",
    )(second, coefficient, live_rows, weight, row_offset, col_offset, patches, taps)


def turn(piece, top, left):
    down = top % 8
    right = left % 128
    tiles = pltpu.roll(piece.reshape(PH // 8, 8, PW), down, 1)
    before = jnp.concatenate([tiles[-1:], tiles[:-1]], axis=0)
    wrapped = lax.broadcasted_iota(i32, tiles.shape, 1) < down
    piece = jnp.where(wrapped, before, tiles).reshape(PH, PW)
    near = pltpu.roll(piece[:, :128], right, 1)
    far = pltpu.roll(piece[:, 128:], right, 1)
    wrapped = lax.broadcasted_iota(i32, near.shape, 1) < right
    return jnp.concatenate([jnp.where(wrapped, far, near), jnp.where(wrapped, near, far)], axis=1)


def add_turned(canvas, piece, top, left):
    down = top % 8
    right = left % 128
    row = pl.multiple_of(top - down, 8)
    col = pl.multiple_of(left - right, 128)
    near = piece[:, :128]
    wrapped = lax.broadcasted_iota(i32, near.shape, 1) < right
    columns = (jnp.where(wrapped, 0.0, near), piece[:, 128:], jnp.where(wrapped, near, 0.0))
    over = lax.broadcasted_iota(i32, (8, 128), 0) < down
    for place, part in enumerate(columns):
        at = pl.ds(pl.multiple_of(col + 128 * place, 128), 128)
        canvas[pl.ds(row, 8), at] += jnp.where(over, 0.0, part[:8])
        canvas[pl.ds(pl.multiple_of(row + 8, 8), PH - 8), at] += part[8:]
        canvas[pl.ds(pl.multiple_of(row + PH, 8), 8), at] += jnp.where(over, part[:8], 0.0)


def first_kernel(slots, group, taps, out, canvas, about, numbers, lines, sem, out_sem, terms, *bands):
    step = pl.program_id(0)
    tiles = slots.shape[0]
    told = pltpu.make_async_copy(slots.at[:, pl.ds(SLOT, META)], about, sem)

    @pl.when(step == 0)
    def _():
        told.start()
        fill_bands(taps, *bands)
        canvas[...] = jnp.zeros_like(canvas)

    images, coefs, masks = [], [], []
    for g in range(GROUP):
        lines[pl.ds(step * GROUP + g, 1), :] = group[g, SLOT + 6 : SLOT + 7, :]
        line = group[g, SLOT + 6 : SLOT + 7, 0:8]
        rows = jnp.broadcast_to(line[:, 3:4] * line[:, 0:1], (PH, PW)).astype(i32)
        mask = live_mask(rows)
        masks.append(mask)
        image = jnp.concatenate([group[g, :PH, :], group[g, PH:SLOT, :]], axis=1)
        images.append(jnp.where(mask, image, 0.0))
        line = group[g, SLOT + 5 : SLOT + 6, 0:NB]
        coefs.append([line[:, b : b + 1] for b in range(NB)])
    matched = match(images, coefs, terms, *bands)

    @pl.when(step == 0)
    def _():
        told.wait()

        def tell(t, carry):
            for place in range(8):
                numbers[t, place] = about[t, 6, place].astype(i32)
            return carry

        lax.fori_loop(0, tiles, tell, 0)

    for g, (mask, image) in enumerate(zip(masks, matched)):
        t = step * GROUP + g
        corner = numbers[t, 1] + MARGIN, numbers[t, 2] + MARGIN
        add_turned(canvas, turn(jnp.where(mask, image, 0.0), *corner), *corner)

    @pl.when(step == pl.num_programs(0) - 1)
    def _():
        parts = (canvas.at[pl.ds(0, SIDE), pl.ds(0, SIDE)], lines)
        places = (out.at[pl.ds(0, SIDE)], out.at[pl.ds(SIDE, tiles), pl.ds(0, 128)])
        copies = [pltpu.make_async_copy(part, at, out_sem.at[n]) for n, (part, at) in enumerate(zip(parts, places))]
        for copy in copies:
            copy.start()
        for copy in copies:
            copy.wait()


def match_first(slots, taps):
    tiles = slots.shape[0]
    return pl.pallas_call(
        first_kernel,
        out_shape=jax.ShapeDtypeStruct((KEPT_ROWS, SIDE), f32),
        grid=(tiles // GROUP,),
        in_specs=[
            anywhere,
            pl.BlockSpec((GROUP, SLOT + META, HALF_COLS), lambda s: (s, 0, 0)),
            whole((2, NB, PW + 128)),
        ],
        out_specs=anywhere,
        scratch_shapes=[
            pltpu.VMEM((CANVAS_ROWS, CANVAS_COLS), f32),
            pltpu.SMEM((tiles, META, 128), f32),
            pltpu.SMEM((tiles, 8), i32),
            pltpu.VMEM((tiles, 128), f32),
            pltpu.SemaphoreType.DMA,
            pltpu.SemaphoreType.DMA((2,)),
            pltpu.VMEM((2 * GROUP * PH, NB * PW), bf16),
        ]
        + BANDS,
        compiler_params=pltpu.CompilerParams(vmem_limit_bytes=61 * MIB),
        cost_estimate=pl.CostEstimate(flops=10_000_000_000, bytes_accessed=8_000_000, transcendentals=0),
        name="match_first",
    )(slots, slots, taps)


LOW, HIGH = slice(0, MARGIN), slice(MARGIN + TILE, SIDE)
CORE, ALL = slice(MARGIN, MARGIN + TILE), slice(0, SIDE)
STRIPS = ((LOW, ALL), (HIGH, ALL), (CORE, LOW), (CORE, HIGH))


def place_slots(kept, slots, parts, told, canvas, base, told_sem, base_sems, core_too):
    tiles = slots.shape[0]
    tell = pltpu.make_async_copy(kept.at[pl.ds(SIDE, tiles), pl.ds(0, 128)], told, told_sem)
    tell.start()
    copies = []
    for n, (rows, cols) in enumerate(parts):
        at = pl.ds(rows.start, rows.stop - rows.start), pl.ds(cols.start, cols.stop - cols.start)
        copies.append(pltpu.make_async_copy(kept.at[at], base.at[at], base_sems.at[n]))
        copies[-1].start()
    canvas[...] = jnp.zeros_like(canvas)
    tell.wait()

    def add(t, carry):
        top, left = told[t, 5].astype(i32) + MARGIN, told[t, 6].astype(i32) + MARGIN
        needed = told[t, 4] > 0
        if not core_too:
            inside = (top >= MARGIN) & (top <= MARGIN + TILE - PH) & (left >= MARGIN) & (left <= MARGIN + TILE - PW)
            needed = needed & jnp.logical_not(inside)

        @pl.when(needed)
        def _():
            add_turned(canvas, slots[t], top, left)

        return carry

    lax.fori_loop(0, tiles, add, 0)
    for copy in copies:
        copy.wait()


def strips_kernel(
    kept, band, slots, rows_next, rows_last, cols_next, cols_last, told, canvas, base, told_sem, base_sems
):
    place_slots(kept, slots, STRIPS, told, canvas, base, told_sem, base_sems, False)
    for out in (rows_next, rows_last):
        out[MARGIN:] = jnp.zeros((META, SIDE), f32)
        out[MARGIN:, : band.shape[1]] = band[...]
    for axis, outs in (("skyy", (rows_next, rows_last)), ("skyx", (cols_next, cols_last))):
        for parity in range(2):

            @pl.when(lax.axis_index(axis) % 2 == parity)
            def _():
                for out, strip in zip(outs, (HIGH, LOW) if parity == 0 else (LOW, HIGH)):
                    rows, cols = (strip, ALL) if axis == "skyy" else (CORE, strip)
                    out[: rows.stop - rows.start] = base[rows, cols] + canvas[rows, cols]


def place_scratch(slots, parts):
    return [
        pltpu.SMEM((slots.shape[0], 128), f32),
        pltpu.VMEM((CANVAS_ROWS, CANVAS_COLS), f32),
        pltpu.VMEM((SIDE, SIDE), f32),
        pltpu.SemaphoreType.DMA,
        pltpu.SemaphoreType.DMA((parts,)),
    ]


def make_strips(kept, band, slots):
    strip = jax.ShapeDtypeStruct((MARGIN + META, SIDE), f32)
    side = jax.ShapeDtypeStruct((TILE, MARGIN), f32)
    return pl.pallas_call(
        strips_kernel,
        out_shape=(strip, strip, side, side),
        in_specs=[anywhere, vmem, vmem],
        out_specs=(vmem,) * 4,
        scratch_shapes=place_scratch(slots, len(STRIPS)),
        compiler_params=pltpu.CompilerParams(vmem_limit_bytes=20 * MIB),
        name="place_second",
    )(kept, band, slots)


def middle_kernel(kept, slots, middle, told, canvas, base, told_sem, base_sems):
    place_slots(kept, slots, ((CORE, ALL),), told, canvas, base, told_sem, base_sems, True)
    middle[...] = base[CORE] + canvas[CORE, :SIDE]


def make_middle(kept, slots):
    return pl.pallas_call(
        middle_kernel,
        out_shape=jax.ShapeDtypeStruct((TILE, SIDE), f32),
        in_specs=[anywhere, vmem],
        out_specs=vmem,
        scratch_shapes=place_scratch(slots, 1),
        compiler_params=pltpu.CompilerParams(vmem_limit_bytes=20 * MIB),
        cost_estimate=pl.CostEstimate(flops=400_000, bytes_accessed=4_000_000, transcendentals=0),
        name="make_middle",
    )(kept, slots)


def depth_kernel(own, rows_next, rows_last, depth, divisor):
    total = jnp.zeros((TILE, TILE), f32)
    count = own.shape[1]
    toward = jnp.where(lax.axis_index("skyy") % 2 == 0, TILE, -TILE).astype(f32)
    for about, step in ((own, 0.0), (rows_next, toward), (rows_last, -toward)):
        about = about[-META:, :count]
        place_at = lax.broadcasted_iota(i32, (TILE, count), 0).astype(f32)
        from_top = place_at - (about[0:1, :] + step)
        rows = jnp.where((from_top >= 0) & (from_top < about[2:3, :]), about[3:4, :], 0.0)
        from_left = place_at - about[1:2, :]
        cols = jnp.where((from_left >= 0) & (from_left < PW), 1.0, 0.0).astype(bf16)
        for part in split(rows):
            total += lax.dot_general(part, cols, (((1,), (1,)), ((), ())), preferred_element_type=f32)
    depth[...] = total
    divisor[...] = total + prior_weight


def make_depth(own, rows_next, rows_last):
    return pl.pallas_call(
        depth_kernel,
        out_shape=(jax.ShapeDtypeStruct((TILE, TILE), f32),) * 2,
        in_specs=[vmem] * 3,
        out_specs=(vmem, vmem),
        compiler_params=pltpu.CompilerParams(vmem_limit_bytes=16 * MIB),
        cost_estimate=pl.CostEstimate(flops=1_000_000_000, bytes_accessed=1_000_000, transcendentals=0),
        name="make_depth",
    )(own, rows_next, rows_last)


def exchange(block, axis, first):
    pairs = [(i, i + 1) for i in range(first, lax.axis_size(axis) - 1, 2)]
    return lax.ppermute(block, axis, pairs + [(j, i) for i, j in pairs])


def by_side(axis, following, preceding):
    even = lax.axis_index(axis) % 2 == 0
    return jnp.where(even, preceding, following), jnp.where(even, following, preceding)


NEAR = TILE - MARGIN


def edges_kernel(near, cols_next, cols_last, rows, out_next, out_last):
    strips = slice(0, MARGIN), slice(MARGIN + TILE, SIDE)
    for row_parity in range(2):
        for col_parity in range(2):
            here = (lax.axis_index("skyy") % 2 == row_parity) & (lax.axis_index("skyx") % 2 == col_parity)

            @pl.when(here)
            def _():
                for out, side, cols in zip(
                    (out_next, out_last), (cols_next, cols_last), strips[::-1] if col_parity == 0 else strips
                ):
                    came = rows[:MARGIN, cols]
                    if not near:
                        out[...] = (side[:MARGIN] if row_parity == 0 else side[NEAR:]) + came
                    elif row_parity == 0:
                        out[: NEAR - MARGIN] = side[MARGIN:NEAR]
                        out[NEAR - MARGIN :] = side[NEAR:] + came
                    else:
                        out[:MARGIN] = side[:MARGIN] + came
                        out[MARGIN:] = side[MARGIN:NEAR]


def make_edges(near, cols_next, cols_last, rows):
    edge = jax.ShapeDtypeStruct((NEAR if near else MARGIN, MARGIN), f32)
    return pl.pallas_call(
        functools.partial(edges_kernel, near),
        out_shape=(edge, edge),
        in_specs=[vmem] * 3,
        out_specs=(vmem, vmem),
        compiler_params=pltpu.CompilerParams(vmem_limit_bytes=12 * MIB),
        name="make_edges",
    )(cols_next, cols_last, rows)


SIDES = slice(0, MARGIN), slice(NEAR, TILE)


def with_rows(total, middle, rows_next, rows_last, cols):
    at = slice(MARGIN + cols.start, MARGIN + cols.stop)
    above, below = by_side("skyy", rows_next[:MARGIN, at], rows_last[:MARGIN, at])
    total[:, cols] = middle[:, at]
    total[:MARGIN, cols] += above
    total[NEAR:, cols] += below


def inside_kernel(middle, rows_next, rows_last, divisor, out, total, sem):
    cols = slice(MARGIN, NEAR)
    with_rows(total, middle, rows_next, rows_last, cols)
    total[:, cols] = total[:, cols] / divisor[:, cols]
    at = pl.ds(MARGIN, NEAR - MARGIN)
    copy = pltpu.make_async_copy(total.at[:, at], out.at[:, at], sem)
    copy.start()
    copy.wait()


def make_inside(*parts):
    return pl.pallas_call(
        inside_kernel,
        out_shape=jax.ShapeDtypeStruct((TILE, TILE), f32),
        in_specs=[vmem] * 4,
        out_specs=anywhere,
        scratch_shapes=[pltpu.VMEM((TILE, TILE), f32), pltpu.SemaphoreType.DMA],
        compiler_params=pltpu.CompilerParams(vmem_limit_bytes=16 * MIB),
        name="make_inside",
    )(*parts)


def final_kernel(
    inside, middle, rows_next, rows_last, near_next, near_last, far_next, far_last, divisor, out, total, sems
):
    near = by_side("skyx", near_next[...], near_last[...])
    far = by_side("skyx", far_next[...], far_last[...])
    copies = []
    for n, cols in enumerate(SIDES):
        with_rows(total, middle, rows_next, rows_last, cols)
        for parity in range(2):

            @pl.when(lax.axis_index("skyy") % 2 == parity)
            def _():
                near_rows = slice(MARGIN, TILE) if parity == 0 else slice(0, NEAR)
                far_rows = slice(0, MARGIN) if parity == 0 else slice(NEAR, TILE)
                total[near_rows, cols] += near[n]
                total[far_rows, cols] += far[n]

        total[:, cols] = total[:, cols] / divisor[:, cols]
        at = pl.ds(cols.start, MARGIN)
        copies.append(pltpu.make_async_copy(total.at[:, at], out.at[:, at], sems.at[n]))
        copies[-1].start()
    for copy in copies:
        copy.wait()


def make_coadd(*parts):
    return pl.pallas_call(
        final_kernel,
        out_shape=jax.ShapeDtypeStruct((TILE, TILE), f32),
        in_specs=[anywhere] + [vmem] * 8,
        out_specs=anywhere,
        scratch_shapes=[pltpu.VMEM((TILE, TILE), f32), pltpu.SemaphoreType.DMA((2,))],
        input_output_aliases={0: 0},
        compiler_params=pltpu.CompilerParams(vmem_limit_bytes=16 * MIB),
        name="make_coadd",
    )(*parts)


def per_device(patches, dest, row_offset, col_offset, live_rows, weight, coefficient, basis):
    tiles = lax.axis_size("skyx")
    images = patches[0]
    outgoing = pack(
        images, dest[:, :, 0], row_offset, col_offset, live_rows, weight, coefficient[0].T, tiles
    )
    arrived = lax.all_to_all(outgoing, "skyx", split_axis=0, concat_axis=0, tiled=True)
    taps = spread_taps(basis)
    second = list_second(dest[:, :, 0], tiles)
    late = match_second(second, coefficient[0].T, live_rows, weight, row_offset, col_offset, images, taps, tiles)
    late = lax.all_to_all(late, "skyx", split_axis=0, concat_axis=0, tiled=True)

    kept = match_first(arrived, taps)

    about = arrived[:, SLOT : SLOT + 5, : images.shape[0]]
    band = jnp.transpose(about, (1, 0, 2)).reshape(5, -1)
    left = band[2] + (band[0] - lax.axis_index("skyx").astype(f32)) * TILE
    own = jnp.pad(jnp.stack([band[1], left, band[3], band[4]]), ((0, META - 4), (0, 0)))

    rows_next, rows_last, cols_next, cols_last = make_strips(kept, own, late)
    rows_last = exchange(rows_last, "skyy", 1)
    rows_next = exchange(rows_next, "skyy", 0)
    edges = make_edges(True, cols_next, cols_last, rows_next)
    near_next, near_last = exchange(edges[0], "skyx", 0), exchange(edges[1], "skyx", 1)
    middle = make_middle(kept, late)
    edges = make_edges(False, cols_next, cols_last, rows_last)
    far_next, far_last = exchange(edges[0], "skyx", 0), exchange(edges[1], "skyx", 1)
    depth, divisor = make_depth(own, rows_next, rows_last)
    inside = make_inside(middle, rows_next, rows_last, divisor)
    coadd = make_coadd(inside, middle, rows_next, rows_last, near_next, near_last, far_next, far_last, divisor)
    return (coadd, depth)


def solution(mesh):
    in_specs = (
        P("skyy", "skyx", None, None),
        P("skyy", "skyx", None),
        P("skyy", "skyx"),
        P("skyy", "skyx"),
        P("skyy", "skyx"),
        P("skyy", "skyx"),
        P("skyy", "skyx", None),
        P(),
    )
    out_specs = (P("skyy", "skyx"), P("skyy", "skyx"))
    return jax.shard_map(
        per_device, mesh=mesh, in_specs=in_specs, out_specs=out_specs, check_vma=False
    )
```

```python
import functools

import jax
import jax.numpy as jnp
from jax import lax
from jax.experimental import pallas as pl
from jax.experimental.pallas import tpu as pltpu
from jax.sharding import PartitionSpec as P

TILE = 512
MARGIN = 128
CAP = 2
PH = 128
PW = 256
NB = 8
TAPS = 41
HALF = TAPS // 2
SIDE = TILE + 2 * MARGIN
CANVAS_ROWS = SIDE + 8
CANVAS_COLS = SIDE + 128
META = 8
HALF_COLS = PW // 2
SLOT = 2 * PH
GROUP = 4
CHUNK = 4
KEPT_ROWS = 20 * SIDE
MIB = 1024 * 1024

prior_weight = 0.5
f32 = jnp.float32
bf16 = jnp.bfloat16
i32 = jnp.int32


def whole(shape):
    return pl.BlockSpec(shape, lambda *_: (0,) * len(shape))


smem = pl.BlockSpec(memory_space=pltpu.SMEM)
vmem = pl.BlockSpec(memory_space=pltpu.VMEM)
anywhere = pl.BlockSpec(memory_space=pl.ANY)
hbm = pl.BlockSpec(memory_space=pltpu.HBM)


def split(x):
    high = x.astype(bf16)
    return high, (x - high.astype(f32)).astype(bf16)


def fill_bands(basis, down_high, down_low, across_high, across_low):
    for b in range(NB):
        taps = jnp.broadcast_to(basis[1, b : b + 1, :], (PW, PW + 128))
        table = pltpu.roll(taps, 0, 1, stride=1, stride_axis=0)[:, :PW]
        high, low = split(table)
        across_high[b * PW : (b + 1) * PW, :] = high
        across_low[b * PW : (b + 1) * PW, :] = low
        taps = jnp.broadcast_to(basis[0, b : b + 1, :], (PH, PW + 128))
        table = pltpu.roll(taps, 0, 1, stride=1, stride_axis=0)[:, :PH]
        high, low = split(table)
        down_high[b * PH : (b + 1) * PH, :PH] = high
        down_high[b * PH : (b + 1) * PH, PH:] = high
        down_low[b * PH : (b + 1) * PH, :] = low


BANDS = [
    pltpu.VMEM((NB * PH, 2 * PH), bf16),
    pltpu.VMEM((NB * PH, PH), bf16),
    pltpu.VMEM((NB * PW, PW), bf16),
    pltpu.VMEM((NB * PW, PW), bf16),
]


def spread_taps(basis):
    taps = jnp.stack([basis[0][:, ::-1], basis[1]])
    gap = jnp.zeros((2, NB, PW + 128 - TAPS), f32)
    return jnp.concatenate([taps[:, :, HALF:], gap, taps[:, :, :HALF]], axis=2)


def assign_slots(dest, slots):
    tiles = slots.shape[1]
    for t in range(tiles):
        slots[0, t] = -1
        slots[1, t] = -1
    for k in range(dest.shape[1]):
        t = dest[0, k]
        rank = jnp.where(slots[0, t] >= 0, 1, 0)
        slots[rank, t] = k


def pack_kernel(*refs):
    given, patches, out = refs[:6], refs[6], refs[7]
    scalars, vectors = refs[8:14], refs[14:19]
    slots, held, meta, small_sems, in_sems, out_sems, meta_sem = refs[19:]
    dest, row_offset, col_offset, live, weight, coefs = scalars
    count = patches.shape[0]
    tiles = out.shape[0]

    def give(k, t, half):
        source = held.at[k, :, pl.ds(half * HALF_COLS, HALF_COLS)]
        return pltpu.make_async_copy(source, out.at[t, pl.ds(half * PH, PH)], out_sems.at[k, half])

    small = [
        pltpu.make_async_copy(source, target, small_sems.at[n])
        for n, (source, target) in enumerate(zip(given + given[:5], scalars + vectors))
    ]
    for copy in small:
        copy.start()
    brings = []
    for n in range(count // CHUNK):
        part = pl.ds(n * CHUNK, CHUNK)
        brings.append(pltpu.make_async_copy(patches.at[part], held.at[part], in_sems.at[n]))
        brings[-1].start()
    meta[...] = jnp.zeros_like(meta)
    small[0].wait()

    assign_slots(dest, slots)
    for k in range(count):
        if k % CHUNK == 0:
            brings[k // CHUNK].wait()
        t = dest[0, k]

        @pl.when(slots[0, t] == k)
        def _():
            give(k, t, 0).start()
            give(k, t, 1).start()

    for copy in small[1:]:
        copy.wait()
    for row, values in enumerate(vectors):
        line = values[...].astype(f32)
        for t in range(tiles):
            meta[t, row : row + 1, 0:count] = line

    lane = lax.broadcasted_iota(i32, (1, 128), 1)

    def describe(t, carry):
        first = slots[0, t]
        k = jnp.maximum(first, 0)
        late = slots[1, t]
        j = jnp.maximum(late, 0)
        numbers = (
            jnp.where(first >= 0, 1, 0), row_offset[0, k], col_offset[0, k], live[0, k],
            jnp.where(late >= 0, 1, 0), row_offset[0, j], col_offset[0, j], live[0, j],
        )
        line = jnp.zeros((1, 128), i32)
        for place, number in enumerate(numbers):
            line = jnp.where(lane == place, number, line)
        meta[t, 6:7, 0:128] = line.astype(f32)
        line = jnp.zeros((1, 128), f32)
        for b in range(NB):
            line = jnp.where(lane == b, coefs[b, k] * weight[0, k], line)
        meta[t, 5:6, 0:128] = line
        return carry

    lax.fori_loop(0, tiles, describe, 0, unroll=4)
    about = pltpu.make_async_copy(meta, out.at[:, pl.ds(SLOT, META)], meta_sem)
    about.start()

    for k in range(count):
        t = dest[0, k]

        @pl.when(slots[0, t] == k)
        def _():
            give(k, t, 0).wait()
            give(k, t, 1).wait()

    about.wait()


def pack(patches, dest, row_offset, col_offset, live_rows, weight, coefficient, tiles):
    given = (dest, row_offset, col_offset, live_rows, weight, coefficient)
    return pl.pallas_call(
        pack_kernel,
        out_shape=jax.ShapeDtypeStruct((tiles, SLOT + META, HALF_COLS), f32),
        in_specs=[anywhere] * 7,
        out_specs=anywhere,
        scratch_shapes=[pltpu.SMEM(x.shape, x.dtype) for x in given]
        + [pltpu.VMEM(x.shape, x.dtype) for x in given[:5]]
        + [
            pltpu.SMEM((CAP, tiles), i32),
            pltpu.VMEM(patches.shape, f32),
            pltpu.VMEM((tiles, META, HALF_COLS), f32),
            pltpu.SemaphoreType.DMA((11,)),
            pltpu.SemaphoreType.DMA((patches.shape[0] // CHUNK,)),
            pltpu.SemaphoreType.DMA((patches.shape[0], 2)),
            pltpu.SemaphoreType.DMA,
        ],
        compiler_params=pltpu.CompilerParams(vmem_limit_bytes=62 * MIB),
        name="pack",
    )(*given, patches)


def list_kernel(dest, second, slots):
    tiles = slots.shape[1]
    assign_slots(dest, slots)
    for j in range(tiles):
        second[0, j] = 0
        second[1, j] = 0

    def note(t, n):
        k = slots[1, t]

        @pl.when(k >= 0)
        def _():
            second[0, n] = k
            second[1, n] = t

        return n + jnp.where(k >= 0, 1, 0)

    number = lax.fori_loop(0, tiles, note, 0)
    last = jnp.maximum(number - 1, 0)

    def repeat_last(j, carry):
        second[0, j] = second[0, last]
        second[1, j] = second[1, last]
        return carry

    lax.fori_loop(number, tiles, repeat_last, 0)
    for j in range(tiles):
        second[2, j] = number


def list_second(dest, tiles):
    return pl.pallas_call(
        list_kernel,
        out_shape=jax.ShapeDtypeStruct((3, tiles), i32),
        in_specs=[smem],
        out_specs=smem,
        scratch_shapes=[pltpu.SMEM((CAP, tiles), i32)],
        name="list_second",
    )(dest)


def match(images, coefs, terms, down_high, down_low, across_high, across_low):
    middle = PH * len(images)
    for g, (image, scales) in enumerate(zip(images, coefs)):
        high, low = split(image)
        both = jnp.concatenate([high, low], axis=0)
        rows = slice(g * PH, (g + 1) * PH)
        low_rows = slice(middle + g * PH, middle + (g + 1) * PH)
        for b in range(NB):
            taps = slice(b * PH, (b + 1) * PH)
            cols = slice(b * PW, (b + 1) * PW)
            downward = jnp.dot(down_high[taps], both, preferred_element_type=f32)
            downward += jnp.dot(down_low[taps], high, preferred_element_type=f32)
            terms[rows, cols], terms[low_rows, cols] = split(downward * scales[b])
    wide = jnp.dot(terms[...], across_high[...], preferred_element_type=f32)
    fine = jnp.dot(terms[:middle], across_low[...], preferred_element_type=f32)
    total = wide[:middle] + wide[middle:] + fine
    return [total[g * PH : (g + 1) * PH] for g in range(len(images))]


def live_mask(live):
    return lax.broadcasted_iota(i32, (PH, PW), 0) < live


def second_kernel(second, coefs, live, weight, row_offset, col_offset, patch, taps, out, terms, *bands):
    j = pl.program_id(0)

    @pl.when(j == 0)
    def _():
        fill_bands(taps, *bands)

    @pl.when(j < second[2, 0])
    def _():
        k = second[0, j]
        mask = live_mask(live[0, k])
        scaled = [coefs[b, k] * weight[0, k] for b in range(NB)]
        image = jnp.where(mask, patch[0], 0.0)
        (matched,) = match([image], [scaled], terms, *bands)
        out[0] = turn(jnp.where(mask, matched, 0.0), row_offset[0, k] + MARGIN, col_offset[0, k] + MARGIN)


def match_second(second, coefficient, live_rows, weight, row_offset, col_offset, patches, taps, tiles):
    steps = patches.shape[0] // CAP
    return pl.pallas_call(
        second_kernel,
        out_shape=jax.ShapeDtypeStruct((tiles, PH, PW), f32),
        grid_spec=pltpu.PrefetchScalarGridSpec(
            num_scalar_prefetch=1,
            grid=(steps,),
            in_specs=[smem] * 5
            + [pl.BlockSpec((1, PH, PW), lambda j, second: (second[0, j], 0, 0))]
            + [whole((2, NB, PW + 128))],
            out_specs=pl.BlockSpec((1, PH, PW), lambda j, second: (second[1, j], 0, 0)),
            scratch_shapes=[pltpu.VMEM((2 * PH, NB * PW), bf16)] + BANDS,
        ),
        compiler_params=pltpu.CompilerParams(vmem_limit_bytes=24 * MIB),
        cost_estimate=pl.CostEstimate(flops=5_000_000_000, bytes_accessed=6_000_000, transcendentals=0),
        name="match_second",
    )(second, coefficient, live_rows, weight, row_offset, col_offset, patches, taps)


def turn(piece, top, left):
    down = top % 8
    right = left % 128
    tiles = pltpu.roll(piece.reshape(PH // 8, 8, PW), down, 1)
    before = jnp.concatenate([tiles[-1:], tiles[:-1]], axis=0)
    wrapped = lax.broadcasted_iota(i32, tiles.shape, 1) < down
    piece = jnp.where(wrapped, before, tiles).reshape(PH, PW)
    near = pltpu.roll(piece[:, :128], right, 1)
    far = pltpu.roll(piece[:, 128:], right, 1)
    wrapped = lax.broadcasted_iota(i32, near.shape, 1) < right
    return jnp.concatenate([jnp.where(wrapped, far, near), jnp.where(wrapped, near, far)], axis=1)


def add_turned(canvas, piece, top, left):
    down = top % 8
    right = left % 128
    row = pl.multiple_of(top - down, 8)
    col = pl.multiple_of(left - right, 128)
    near = piece[:, :128]
    wrapped = lax.broadcasted_iota(i32, near.shape, 1) < right
    columns = (jnp.where(wrapped, 0.0, near), piece[:, 128:], jnp.where(wrapped, near, 0.0))
    over = lax.broadcasted_iota(i32, (8, 128), 0) < down
    for place, part in enumerate(columns):
        at = pl.ds(pl.multiple_of(col + 128 * place, 128), 128)
        canvas[pl.ds(row, 8), at] += jnp.where(over, 0.0, part[:8])
        canvas[pl.ds(pl.multiple_of(row + 8, 8), PH - 8), at] += part[8:]
        canvas[pl.ds(pl.multiple_of(row + PH, 8), 8), at] += jnp.where(over, part[:8], 0.0)


def first_kernel(slots, group, taps, out, canvas, about, numbers, lines, sem, out_sem, terms, *bands):
    step = pl.program_id(0)
    tiles = slots.shape[0]
    told = pltpu.make_async_copy(slots.at[:, pl.ds(SLOT, META)], about, sem)

    @pl.when(step == 0)
    def _():
        told.start()
        fill_bands(taps, *bands)
        canvas[...] = jnp.zeros_like(canvas)

    images, coefs, masks = [], [], []
    for g in range(GROUP):
        lines[pl.ds(step * GROUP + g, 1), :] = group[g, SLOT + 6 : SLOT + 7, :]
        line = group[g, SLOT + 6 : SLOT + 7, 0:8]
        rows = jnp.broadcast_to(line[:, 3:4] * line[:, 0:1], (PH, PW)).astype(i32)
        mask = live_mask(rows)
        masks.append(mask)
        image = jnp.concatenate([group[g, :PH, :], group[g, PH:SLOT, :]], axis=1)
        images.append(jnp.where(mask, image, 0.0))
        line = group[g, SLOT + 5 : SLOT + 6, 0:NB]
        coefs.append([line[:, b : b + 1] for b in range(NB)])
    matched = match(images, coefs, terms, *bands)

    @pl.when(step == 0)
    def _():
        told.wait()

        def tell(t, carry):
            for place in range(8):
                numbers[t, place] = about[t, 6, place].astype(i32)
            return carry

        lax.fori_loop(0, tiles, tell, 0)

    for g, (mask, image) in enumerate(zip(masks, matched)):
        t = step * GROUP + g
        corner = numbers[t, 1] + MARGIN, numbers[t, 2] + MARGIN
        add_turned(canvas, turn(jnp.where(mask, image, 0.0), *corner), *corner)

    @pl.when(step == pl.num_programs(0) - 1)
    def _():
        parts = (canvas.at[pl.ds(0, SIDE), pl.ds(0, SIDE)], lines)
        places = (out.at[pl.ds(0, SIDE)], out.at[pl.ds(SIDE, tiles), pl.ds(0, 128)])
        copies = [pltpu.make_async_copy(part, at, out_sem.at[n]) for n, (part, at) in enumerate(zip(parts, places))]
        for copy in copies:
            copy.start()
        for copy in copies:
            copy.wait()


def match_first(slots, taps):
    tiles = slots.shape[0]
    return pl.pallas_call(
        first_kernel,
        out_shape=jax.ShapeDtypeStruct((KEPT_ROWS, SIDE), f32),
        grid=(tiles // GROUP,),
        in_specs=[
            anywhere,
            pl.BlockSpec((GROUP, SLOT + META, HALF_COLS), lambda s: (s, 0, 0)),
            whole((2, NB, PW + 128)),
        ],
        out_specs=anywhere,
        scratch_shapes=[
            pltpu.VMEM((CANVAS_ROWS, CANVAS_COLS), f32),
            pltpu.SMEM((tiles, META, 128), f32),
            pltpu.SMEM((tiles, 8), i32),
            pltpu.VMEM((tiles, 128), f32),
            pltpu.SemaphoreType.DMA,
            pltpu.SemaphoreType.DMA((2,)),
            pltpu.VMEM((2 * GROUP * PH, NB * PW), bf16),
        ]
        + BANDS,
        compiler_params=pltpu.CompilerParams(vmem_limit_bytes=61 * MIB),
        cost_estimate=pl.CostEstimate(flops=10_000_000_000, bytes_accessed=8_000_000, transcendentals=0),
        name="match_first",
    )(slots, slots, taps)


LOW, HIGH = slice(0, MARGIN), slice(MARGIN + TILE, SIDE)
CORE, ALL = slice(MARGIN, MARGIN + TILE), slice(0, SIDE)
STRIPS = ((LOW, ALL), (HIGH, ALL), (CORE, LOW), (CORE, HIGH))


def place_slots(kept, slots, parts, told, canvas, base, told_sem, base_sems):
    tiles = slots.shape[0]
    tell = pltpu.make_async_copy(kept.at[pl.ds(SIDE, tiles), pl.ds(0, 128)], told, told_sem)
    tell.start()
    copies = []
    for n, (rows, cols) in enumerate(parts):
        at = pl.ds(rows.start, rows.stop - rows.start), pl.ds(cols.start, cols.stop - cols.start)
        copies.append(pltpu.make_async_copy(kept.at[at], base.at[at], base_sems.at[n]))
        copies[-1].start()
    canvas[...] = jnp.zeros_like(canvas)
    tell.wait()

    def add(t, carry):
        @pl.when(told[t, 4] > 0)
        def _():
            corner = told[t, 5].astype(i32) + MARGIN, told[t, 6].astype(i32) + MARGIN
            add_turned(canvas, slots[t], *corner)

        return carry

    lax.fori_loop(0, tiles, add, 0)
    for copy in copies:
        copy.wait()


def strips_kernel(
    kept, band, slots, rows_next, rows_last, cols_next, cols_last, told, canvas, base, told_sem, base_sems
):
    place_slots(kept, slots, STRIPS, told, canvas, base, told_sem, base_sems)
    for out in (rows_next, rows_last):
        out[MARGIN:] = jnp.zeros((META, SIDE), f32)
        out[MARGIN:, : band.shape[1]] = band[...]
    for axis, outs in (("skyy", (rows_next, rows_last)), ("skyx", (cols_next, cols_last))):
        for parity in range(2):

            @pl.when(lax.axis_index(axis) % 2 == parity)
            def _():
                for out, strip in zip(outs, (HIGH, LOW) if parity == 0 else (LOW, HIGH)):
                    rows, cols = (strip, ALL) if axis == "skyy" else (CORE, strip)
                    out[: rows.stop - rows.start] = base[rows, cols] + canvas[rows, cols]


def place_scratch(slots, parts):
    return [
        pltpu.SMEM((slots.shape[0], 128), f32),
        pltpu.VMEM((CANVAS_ROWS, CANVAS_COLS), f32),
        pltpu.VMEM((SIDE, SIDE), f32),
        pltpu.SemaphoreType.DMA,
        pltpu.SemaphoreType.DMA((parts,)),
    ]


def make_strips(kept, band, slots):
    strip = jax.ShapeDtypeStruct((MARGIN + META, SIDE), f32)
    side = jax.ShapeDtypeStruct((TILE, MARGIN), f32)
    return pl.pallas_call(
        strips_kernel,
        out_shape=(strip, strip, side, side),
        in_specs=[anywhere, vmem, vmem],
        out_specs=(vmem,) * 4,
        scratch_shapes=place_scratch(slots, len(STRIPS)),
        compiler_params=pltpu.CompilerParams(vmem_limit_bytes=20 * MIB),
        name="place_second",
    )(kept, band, slots)


def middle_kernel(kept, slots, middle, told, canvas, base, told_sem, base_sems):
    place_slots(kept, slots, ((CORE, ALL),), told, canvas, base, told_sem, base_sems)
    middle[...] = base[CORE] + canvas[CORE, :SIDE]


def make_middle(kept, slots):
    return pl.pallas_call(
        middle_kernel,
        out_shape=jax.ShapeDtypeStruct((TILE, SIDE), f32),
        in_specs=[anywhere, vmem],
        out_specs=vmem,
        scratch_shapes=place_scratch(slots, 1),
        compiler_params=pltpu.CompilerParams(vmem_limit_bytes=20 * MIB),
        cost_estimate=pl.CostEstimate(flops=400_000, bytes_accessed=4_000_000, transcendentals=0),
        name="make_middle",
    )(kept, slots)


def depth_kernel(own, rows_next, rows_last, depth, divisor):
    total = jnp.zeros((TILE, TILE), f32)
    count = own.shape[1]
    toward = jnp.where(lax.axis_index("skyy") % 2 == 0, TILE, -TILE).astype(f32)
    for about, step in ((own, 0.0), (rows_next, toward), (rows_last, -toward)):
        about = about[-META:, :count]
        place_at = lax.broadcasted_iota(i32, (TILE, count), 0).astype(f32)
        from_top = place_at - (about[0:1, :] + step)
        rows = jnp.where((from_top >= 0) & (from_top < about[2:3, :]), about[3:4, :], 0.0)
        from_left = place_at - about[1:2, :]
        cols = jnp.where((from_left >= 0) & (from_left < PW), 1.0, 0.0).astype(bf16)
        for part in split(rows):
            total += lax.dot_general(part, cols, (((1,), (1,)), ((), ())), preferred_element_type=f32)
    depth[...] = total
    divisor[...] = total + prior_weight


def make_depth(own, rows_next, rows_last):
    return pl.pallas_call(
        depth_kernel,
        out_shape=(jax.ShapeDtypeStruct((TILE, TILE), f32),) * 2,
        in_specs=[vmem] * 3,
        out_specs=(vmem, vmem),
        compiler_params=pltpu.CompilerParams(vmem_limit_bytes=16 * MIB),
        cost_estimate=pl.CostEstimate(flops=1_000_000_000, bytes_accessed=1_000_000, transcendentals=0),
        name="make_depth",
    )(own, rows_next, rows_last)


def exchange(block, axis, first):
    pairs = [(i, i + 1) for i in range(first, lax.axis_size(axis) - 1, 2)]
    return lax.ppermute(block, axis, pairs + [(j, i) for i, j in pairs])


def by_side(axis, following, preceding):
    even = lax.axis_index(axis) % 2 == 0
    return jnp.where(even, preceding, following), jnp.where(even, following, preceding)


NEAR = TILE - MARGIN


def edges_kernel(near, cols_next, cols_last, rows, out_next, out_last):
    strips = slice(0, MARGIN), slice(MARGIN + TILE, SIDE)
    for row_parity in range(2):
        for col_parity in range(2):
            here = (lax.axis_index("skyy") % 2 == row_parity) & (lax.axis_index("skyx") % 2 == col_parity)

            @pl.when(here)
            def _():
                for out, side, cols in zip(
                    (out_next, out_last), (cols_next, cols_last), strips[::-1] if col_parity == 0 else strips
                ):
                    came = rows[:MARGIN, cols]
                    if not near:
                        out[...] = (side[:MARGIN] if row_parity == 0 else side[NEAR:]) + came
                    elif row_parity == 0:
                        out[: NEAR - MARGIN] = side[MARGIN:NEAR]
                        out[NEAR - MARGIN :] = side[NEAR:] + came
                    else:
                        out[:MARGIN] = side[:MARGIN] + came
                        out[MARGIN:] = side[MARGIN:NEAR]


def make_edges(near, cols_next, cols_last, rows):
    edge = jax.ShapeDtypeStruct((NEAR if near else MARGIN, MARGIN), f32)
    return pl.pallas_call(
        functools.partial(edges_kernel, near),
        out_shape=(edge, edge),
        in_specs=[vmem] * 3,
        out_specs=(vmem, vmem),
        compiler_params=pltpu.CompilerParams(vmem_limit_bytes=12 * MIB),
        name="make_edges",
    )(cols_next, cols_last, rows)


SIDES = slice(0, MARGIN), slice(NEAR, TILE)


def with_rows(total, middle, rows_next, rows_last, cols):
    at = slice(MARGIN + cols.start, MARGIN + cols.stop)
    above, below = by_side("skyy", rows_next[:MARGIN, at], rows_last[:MARGIN, at])
    total[:, cols] = middle[:, at]
    total[:MARGIN, cols] += above
    total[NEAR:, cols] += below


def inside_kernel(middle, rows_next, rows_last, divisor, out, total, sem):
    cols = slice(MARGIN, NEAR)
    with_rows(total, middle, rows_next, rows_last, cols)
    total[:, cols] = total[:, cols] / divisor[:, cols]
    at = pl.ds(MARGIN, NEAR - MARGIN)
    copy = pltpu.make_async_copy(total.at[:, at], out.at[:, at], sem)
    copy.start()
    copy.wait()


def make_inside(*parts):
    return pl.pallas_call(
        inside_kernel,
        out_shape=jax.ShapeDtypeStruct((TILE, TILE), f32),
        in_specs=[vmem] * 4,
        out_specs=anywhere,
        scratch_shapes=[pltpu.VMEM((TILE, TILE), f32), pltpu.SemaphoreType.DMA],
        compiler_params=pltpu.CompilerParams(vmem_limit_bytes=16 * MIB),
        name="make_inside",
    )(*parts)


def final_kernel(
    inside, middle, rows_next, rows_last, near_next, near_last, far_next, far_last, divisor, out, total, sems
):
    near = by_side("skyx", near_next[...], near_last[...])
    far = by_side("skyx", far_next[...], far_last[...])
    copies = []
    for n, cols in enumerate(SIDES):
        with_rows(total, middle, rows_next, rows_last, cols)
        for parity in range(2):

            @pl.when(lax.axis_index("skyy") % 2 == parity)
            def _():
                near_rows = slice(MARGIN, TILE) if parity == 0 else slice(0, NEAR)
                far_rows = slice(0, MARGIN) if parity == 0 else slice(NEAR, TILE)
                total[near_rows, cols] += near[n]
                total[far_rows, cols] += far[n]

        total[:, cols] = total[:, cols] / divisor[:, cols]
        at = pl.ds(cols.start, MARGIN)
        copies.append(pltpu.make_async_copy(total.at[:, at], out.at[:, at], sems.at[n]))
        copies[-1].start()
    for copy in copies:
        copy.wait()


def make_coadd(*parts):
    return pl.pallas_call(
        final_kernel,
        out_shape=jax.ShapeDtypeStruct((TILE, TILE), f32),
        in_specs=[anywhere] + [vmem] * 8,
        out_specs=anywhere,
        scratch_shapes=[pltpu.VMEM((TILE, TILE), f32), pltpu.SemaphoreType.DMA((2,))],
        input_output_aliases={0: 0},
        compiler_params=pltpu.CompilerParams(vmem_limit_bytes=16 * MIB),
        name="make_coadd",
    )(*parts)


def per_device(patches, dest, row_offset, col_offset, live_rows, weight, coefficient, basis):
    tiles = lax.axis_size("skyx")
    images = patches[0]
    outgoing = pack(
        images, dest[:, :, 0], row_offset, col_offset, live_rows, weight, coefficient[0].T, tiles
    )
    arrived = lax.all_to_all(outgoing, "skyx", split_axis=0, concat_axis=0, tiled=True)
    taps = spread_taps(basis)
    second = list_second(dest[:, :, 0], tiles)
    late = match_second(second, coefficient[0].T, live_rows, weight, row_offset, col_offset, images, taps, tiles)
    late = lax.all_to_all(late, "skyx", split_axis=0, concat_axis=0, tiled=True)

    kept = match_first(arrived, taps)

    about = arrived[:, SLOT : SLOT + 5, : images.shape[0]]
    band = jnp.transpose(about, (1, 0, 2)).reshape(5, -1)
    left = band[2] + (band[0] - lax.axis_index("skyx").astype(f32)) * TILE
    own = jnp.pad(jnp.stack([band[1], left, band[3], band[4]]), ((0, META - 4), (0, 0)))

    rows_next, rows_last, cols_next, cols_last = make_strips(kept, own, late)
    rows_last = exchange(rows_last, "skyy", 1)
    rows_next = exchange(rows_next, "skyy", 0)
    edges = make_edges(True, cols_next, cols_last, rows_next)
    near_next, near_last = exchange(edges[0], "skyx", 0), exchange(edges[1], "skyx", 1)
    middle = make_middle(kept, late)
    edges = make_edges(False, cols_next, cols_last, rows_last)
    far_next, far_last = exchange(edges[0], "skyx", 0), exchange(edges[1], "skyx", 1)
    depth, divisor = make_depth(own, rows_next, rows_last)
    inside = make_inside(middle, rows_next, rows_last, divisor)
    coadd = make_coadd(inside, middle, rows_next, rows_last, near_next, near_last, far_next, far_last, divisor)
    return (coadd, depth)


def solution(mesh):
    in_specs = (
        P("skyy", "skyx", None, None),
        P("skyy", "skyx", None),
        P("skyy", "skyx"),
        P("skyy", "skyx"),
        P("skyy", "skyx"),
        P("skyy", "skyx"),
        P("skyy", "skyx", None),
        P(),
    )
    out_specs = (P("skyy", "skyx"), P("skyy", "skyx"))
    return jax.shard_map(
        per_device, mesh=mesh, in_specs=in_specs, out_specs=out_specs, check_vma=False
    )
```
